32 devices in a mesh: pipe: 2 (over core), dp: 16 (over z, y, x).
Axes of the slice: x: 2, y: 2, z: 4, core: 2. Of those that a mesh axis runs over, the one named last changes fastest.
Arguments:
- section_inputs: bfloat16 [2, 256, 49, 768], P('pipe', 'dp'), may hold values from -6 to 6
- conv_weight: float32 [2, 2, 9, 768], P('pipe'), may hold values from -2 to 2
- conv_bias: float32 [2, 2, 768], P('pipe'), may hold values from -4 to 4
- norm_gain: float32 [2, 2, 768], P('pipe'), may hold values from 0.1 to 1.9
- norm_bias: float32 [2, 2, 768], P('pipe'), may hold values from -4 to 4
- w_qkv: bfloat16 [2, 768, 2304], P('pipe'), may hold values from -0.21875 to 0.21875
- w_proj: bfloat16 [2, 768, 768], P('pipe'), may hold values from -0.625 to 0.625
- b_proj: float32 [2, 768], P('pipe'), may hold values from -4 to 4
- w_fc1: bfloat16 [2, 768, 3072], P('pipe'), may hold values from -0.21875 to 0.21875
- b_fc1: float32 [2, 3072], P('pipe'), may hold values from -6 to 6
- w_fc2: bfloat16 [2, 3072, 768], P('pipe'), may hold values from -0.109375 to 0.109375
- b_fc2: float32 [2, 768], P('pipe'), may hold values from -4 to 4
Outputs:
- section_ends: float32 [2, 256, 49, 768], P('pipe', 'dp')
- grad_conv_weight: float32 [2, 2, 9, 768], P('pipe')
- grad_conv_bias: float32 [2, 2, 768], P('pipe')
- grad_norm_gain: float32 [2, 2, 768], P('pipe')
- grad_norm_bias: float32 [2, 2, 768], P('pipe')
- grad_w_qkv: float32 [2, 768, 2304], P('pipe')
- grad_w_proj: float32 [2, 768, 768], P('pipe')
- grad_b_proj: float32 [2, 768], P('pipe')
- grad_w_fc1: float32 [2, 768, 3072], P('pipe')
- grad_b_fc1: float32 [2, 3072], P('pipe')
- grad_w_fc2: float32 [2, 3072, 768], P('pipe')
- grad_b_fc2: float32 [2, 768], P('pipe')
The draws below stay inside these ranges and needn't reach their ends.
All inputs are finite; a program needn't handle non-finite values.
Results may differ from the reference program's by a relative error of at most 0.023.
Values may be sent and summed in bfloat16 or wider, within the bound.
A program may use at most 320 MiB of HBM per device.

```python
import jax
import jax.numpy as jnp
from jax import lax

C = 768
FF = 3072
IMG_DEV = 16
IMAGES = 256
N_DP = 16


def level_of(key, dims, cuts, smallest, largest):
    level, own = 1.0, jax.random.fold_in(key, 6)
    for axis_at, blocks in cuts:
        heights = jnp.exp(jax.random.uniform(jax.random.fold_in(own, axis_at), (blocks,), jnp.float32, smallest / len(cuts), largest / len(cuts)))
        level = level * jnp.repeat(heights, dims[axis_at] // blocks).reshape([-1 if axis == axis_at else 1 for axis in range(len(dims))])
    return level


def gaussian(key, dims, scale, limit, split=(), dtype=jnp.bfloat16):
    values = scale * jax.random.normal(key, dims, jnp.float32)
    if split:
        values = values * level_of(key, dims, split, -0.22, 0.18)
    return jnp.clip(values, -limit, limit).astype(dtype)


def setup_inputs(seed: int = 0) -> dict:
    streams_of = jax.random.split(jax.random.key(seed), 13)
    return {
        "section_inputs": gaussian(streams_of[0], (2, IMAGES, 49, C), 1.0, 6.0, ((0, 2), (1, 16))),
        "conv_weight": gaussian(streams_of[1], (2, 2, 9, C), 9 ** -0.5, 2.0, ((0, 2),), jnp.float32),
        "conv_bias": gaussian(streams_of[2], (2, 2, C), 0.3, 4.0, ((0, 2),), jnp.float32),
        "norm_gain": jnp.clip(1.0 + 0.18 * jax.random.normal(streams_of[3], (2, 2, C), jnp.float32), 0.1, 1.9),
        "norm_bias": gaussian(streams_of[4], (2, 2, C), 0.3, 4.0, ((0, 2),), jnp.float32),
        "w_qkv": gaussian(streams_of[5], (2, C, 3 * C), C ** -0.5, 0.21875, ((0, 2),)),
        "w_proj": gaussian(streams_of[6], (2, C, C), (C // 8) ** -0.5, 0.625, ((0, 2),)),
        "b_proj": gaussian(streams_of[7], (2, C), 0.3, 4.0, ((0, 2),), jnp.float32),
        "w_fc1": gaussian(streams_of[8], (2, C, FF), C ** -0.5, 0.21875, ((0, 2),)),
        "b_fc1": gaussian(streams_of[9], (2, FF), 0.5, 6.0, ((0, 2),), jnp.float32),
        "w_fc2": gaussian(streams_of[10], (2, FF, C), FF ** -0.5, 0.109375, ((0, 2),)),
        "b_fc2": gaussian(streams_of[11], (2, C), 0.3, 4.0, ((0, 2),), jnp.float32),
    }


@jax.custom_vjp
def low(v):
    return lax.optimization_barrier(v.astype(jnp.bfloat16)).astype(jnp.float32)

@jax.custom_vjp
def low_back(v):
    return v

def low_keep(v):
    return (low(v), None)

def low_pass(kept, grad):
    return (grad,)

def back_keep(v):
    return (v, None)

def back_low(kept, grad):
    return (low(grad),)
low.defvjp(low_keep, low_pass)
low_back.defvjp(back_keep, back_low)

def product(left, right):
    return low_back(jnp.einsum('...ij,...jk->...ik', low(left), low(right), precision=lax.Precision.HIGHEST))

def depthwise(tensor_in, kernel, shift_row):
    image_count = tensor_in.shape[0]
    channels = tensor_in.shape[2]
    square = tensor_in.reshape(image_count, 7, 7, channels)
    padded = jnp.pad(square, ((0, 0), (1, 1), (1, 1), (0, 0)))
    running = jnp.zeros_like(square) + shift_row
    for offset in range(9):
        row_at = offset // 3
        col_at = offset % 3
        running = running + padded[:, row_at:row_at + 7, col_at:col_at + 7, :] * kernel[offset]
    return running.reshape(image_count, 49, channels)

def layer_norm(tensor_in, gain_row, shift_row):
    centered = tensor_in - lax.optimization_barrier(jnp.mean(tensor_in, axis=-1, keepdims=True))
    spread_sq = lax.optimization_barrier(jnp.mean(centered * centered, axis=-1, keepdims=True))
    return centered * lax.rsqrt(spread_sq + 1e-05) * gain_row + shift_row

def spatial_mix(queries, keys_all, values_all):
    scores = product(queries * 32.0 ** (-0.5), jnp.swapaxes(keys_all, 2, 3))
    weights_soft = jax.nn.softmax(scores, axis=-1)
    return product(weights_soft, values_all)

def channel_mix(queries, keys_all, values_all):
    scores = product(jnp.swapaxes(queries, 2, 3) * 32.0 ** (-0.5), keys_all)
    weights_soft = jax.nn.softmax(scores, axis=-1)
    return jnp.swapaxes(product(weights_soft, jnp.swapaxes(values_all, 2, 3)), 2, 3)

def block(tensor_in, params, mixer):
    conv_weight, conv_bias, norm_gain, norm_bias, w_qkv, w_proj, b_proj, w_fc1, b_fc1, w_fc2, b_fc2 = params
    image_count = tensor_in.shape[0]
    channels = tensor_in.shape[2]
    head_count = channels // 32
    stream = tensor_in + depthwise(tensor_in, conv_weight[0], conv_bias[0])
    normed = layer_norm(stream, norm_gain[0], norm_bias[0]).reshape(image_count * 49, channels)
    packed = product(normed, w_qkv).reshape(image_count, 49, 3, head_count, 32)
    queries = jnp.transpose(packed[:, :, 0], (0, 2, 1, 3))
    keys_all = jnp.transpose(packed[:, :, 1], (0, 2, 1, 3))
    values_all = jnp.transpose(packed[:, :, 2], (0, 2, 1, 3))
    mixed = mixer(queries, keys_all, values_all)
    mixed = jnp.transpose(mixed, (0, 2, 1, 3)).reshape(image_count * 49, channels)
    stream = stream + (product(mixed, w_proj) + b_proj).reshape(stream.shape)
    stream = stream + depthwise(stream, conv_weight[1], conv_bias[1])
    normed = layer_norm(stream, norm_gain[1], norm_bias[1]).reshape(image_count * 49, channels)
    hidden = jax.nn.gelu(product(normed, w_fc1) + b_fc1, approximate=False)
    return stream + (product(hidden, w_fc2) + b_fc2).reshape(stream.shape)

def reference(section_inputs, conv_weight, conv_bias, norm_gain, norm_bias, w_qkv, w_proj, b_proj, w_fc1, b_fc1, w_fc2, b_fc2):
    params = tuple((weight.astype(jnp.float32) for weight in (conv_weight, conv_bias, norm_gain, norm_bias, w_qkv, w_proj, b_proj, w_fc1, b_fc1, w_fc2, b_fc2)))
    width = section_inputs.shape[3]
    inputs_all = section_inputs[0].astype(jnp.float32).reshape(N_DP, IMG_DEV, 49, width)
    cotangents = section_inputs[1].astype(jnp.float32).reshape(N_DP, IMG_DEV, 49, width)

    def forward(images_in, weights):
        first_section = tuple((weight[0] for weight in weights))
        second_section = tuple((weight[1] for weight in weights))
        middle = low_back(low(block(images_in, first_section, spatial_mix)))
        return block(middle, second_section, channel_mix)

    def one_group(totals, pair):
        images_in, cotangent = pair
        result, pullback = jax.vjp(forward, images_in, params)
        input_grad, weight_grads = pullback(cotangent)
        totals = jax.tree.map(jnp.add, totals, weight_grads)
        return (totals, (input_grad, result))
    zeros_start = jax.tree.map(jnp.zeros_like, params)
    totals, (input_grads, results) = lax.scan(one_group, zeros_start, (inputs_all, cotangents))
    section_ends = jnp.stack([input_grads.reshape(IMAGES, 49, width), results.reshape(IMAGES, 49, width)])
    return (section_ends, totals[0], totals[1], totals[2], totals[3], totals[4], totals[5], totals[6], totals[7], totals[8], totals[9], totals[10])
```

```python
import functools
import jax
import jax.numpy as jnp
from jax import lax
from jax.experimental import pallas as pl
from jax.experimental.pallas import tpu as pltpu
from jax.sharding import PartitionSpec as P

MESH = pl.DeviceIdType.MESH


def dp_dims(n):
    sizes = [1, 1, 1]
    at = 0
    left = n
    while left > 1:
        factor = 2 if left % 2 == 0 else left
        sizes[at % 3] *= factor
        left //= factor
        at += 1
    return tuple(sizes), (sizes[1] * sizes[2], sizes[2], 1)


class Place:
    def __init__(self, dp, size, stride):
        self.size = size
        pos = lax.rem(lax.div(dp, stride), size)
        low = pos < (size + 1) // 2
        self.outer = jnp.where(low, pos, size - 1 - pos)
        self.pos = pos
        self.low = low
        step = jnp.where(low, stride, -stride)
        self.inner_peer = dp + step
        self.outer_peer = dp - step


def pick(flag, a, b):
    out = object.__new__(Place)
    out.size = a.size
    for name in ("pos", "low", "outer", "inner_peer", "outer_peer"):
        setattr(out, name, jnp.where(flag, getattr(a, name), getattr(b, name)))
    return out


class Ring:
    def __init__(self, dp, dims, rows, grad, land, out, send, recv, local):
        (s0, s1, s2), (t0, t1, t2) = dims
        self.mids = Place(dp, s0, t0)
        self.fast, self.slow = Place(dp, s2, t2), Place(dp, s1, t1)
        self.dp, self.rows = dp, rows
        self.grad, self.land, self.out = grad, land, out
        self.send, self.recv, self.local = send, recv, local
        self.sizes = (s2, s0, s1)
        self.lens = (rows // s2, rows // s2 // s0, rows // (s0 * s1 * s2))

    @staticmethod
    def land_rows(rows, dims):
        s0, s1, s2 = dims[0]
        lens = (rows // s2, rows // s2 // s0, rows // (s0 * s1 * s2))
        total, starts = 0, []
        for n, length in zip((s2, s0, s1), lens):
            starts.append(total)
            total += length * (1 if n == 2 else 5)
        return total, starts

    def level(self, c, i):
        flag = lax.rem(c, 2) == 0
        if i == 1:
            return self.mids
        return pick(flag, self.fast, self.slow) if i == 0 else pick(flag, self.slow, self.fast)

    def base(self, c, i):
        start = 0
        for j in range(i):
            start = start + self.level(c, j).pos * self.lens[j]
        return start

    def span(self, c, i, a, b):
        place, length = self.level(c, i), self.lens[i]
        n = self.sizes[i]
        start = self.base(c, i) + jnp.where(place.low, a * length, (n - b) * length)
        return pl.ds(pl.multiple_of(start, 8), (b - a) * length)

    def copy(self, c, ev, src, dst, peer):
        return pltpu.make_async_remote_copy(
            src_ref=src, dst_ref=dst, send_sem=self.send.at[c, ev], recv_sem=self.recv.at[c, ev],
            device_id={"dp": peer}, device_id_type=MESH)

    def landing(self, c, i, at, length):
        start = self.land_rows(self.rows, ((self.sizes[1], self.sizes[2], self.sizes[0]), None))[1][i]
        return self.land.at[c, pl.ds(start + at, length)]

    def add(self, c, i, a, b, at, lo=None):
        rows = self.span(c, i, a, b)
        length = (b - a) * self.lens[i]
        got = self.landing(c, i, at, length)
        self.grad[c, rows] = self.grad[c, rows] + got[...]

    def reduce_send(self, c, i, ev, a, b, at, peer):
        rows = self.span(c, i, a, b)
        length = (b - a) * self.lens[i]
        return self.copy(c, ev, self.grad.at[c, rows], self.landing(c, i, at, length), peer)

    def reduce_stages(self, i):
        n, length = self.sizes[i], self.lens[i]
        ein, eout = 2 * i, 2 * i + 1
        if n == 1:
            return []
        if n == 2:
            def first(c):
                self.reduce_send(c, i, eout, 1, 2, 0, self.level(c, i).inner_peer).start()

            def last(c):
                self.reduce_send(c, i, eout, 0, 1, 0, self.level(c, i).inner_peer).wait_recv()
                self.add(c, i, 0, 1, 0)
            return [first, last]

        def zero(c):
            place = self.level(c, i)

            @pl.when(place.outer == 0)
            def _():
                self.reduce_send(c, i, ein, 1, 4, 0, place.inner_peer).start()

        def one(c):
            place = self.level(c, i)

            @pl.when(place.outer == 1)
            def _():
                self.reduce_send(c, i, ein, 1, 4, 0, place.inner_peer).wait_recv()
                self.add(c, i, 1, 4, 0)
                self.reduce_send(c, i, eout, 2, 4, 3 * length, place.inner_peer).start()

        def two(c):
            place = self.level(c, i)

            @pl.when(place.outer == 1)
            def _():
                self.reduce_send(c, i, eout, 0, 2, 3 * length, place.inner_peer).wait_recv()
                self.add(c, i, 0, 2, 3 * length)
                self.reduce_send(c, i, ein, 0, 1, 3 * length, place.outer_peer).start()

        def three(c):
            place = self.level(c, i)

            @pl.when(place.outer == 0)
            def _():
                self.reduce_send(c, i, ein, 0, 1, 3 * length, place.inner_peer).wait_recv()
                self.add(c, i, 0, 1, 3 * length)
        return [zero, one, two, three]

    def reduce_ends(self, i):
        n = self.sizes[i]
        ein, eout = 2 * i, 2 * i + 1

        def ends(c):
            place = self.level(c, i)
            if n == 2:
                self.reduce_send(c, i, eout, 1, 2, 0, place.inner_peer).wait_send()
            elif n == 4:
                @pl.when(place.outer == 0)
                def _():
                    self.reduce_send(c, i, ein, 1, 4, 0, place.inner_peer).wait_send()

                @pl.when(place.outer == 1)
                def _():
                    self.reduce_send(c, i, eout, 2, 4, 0, place.inner_peer).wait_send()
                    self.reduce_send(c, i, ein, 0, 1, 0, place.outer_peer).wait_send()
        return ends

    def gather_send(self, c, i, ev, a, b, peer):
        rows = self.span(c, i, a, b)
        dst = self.out.at[c, rows]
        return self.copy(c, ev, dst, dst, peer)

    def gather_stages(self, i):
        n = self.sizes[i]
        ein, eout = 6 + 2 * i, 7 + 2 * i
        if n == 1:
            return []
        if n == 2:
            def first(c):
                self.gather_send(c, i, eout, 0, 1, self.level(c, i).inner_peer).start()

            def last(c):
                self.gather_send(c, i, eout, 1, 2, self.level(c, i).inner_peer).wait_recv()
            return [first, last]

        def zero(c):
            place = self.level(c, i)

            @pl.when(place.outer == 0)
            def _():
                self.gather_send(c, i, ein, 0, 1, place.inner_peer).start()

        def one(c):
            place = self.level(c, i)

            @pl.when(place.outer == 1)
            def _():
                self.gather_send(c, i, ein, 0, 1, place.outer_peer).wait_recv()
                self.gather_send(c, i, eout, 0, 2, place.inner_peer).start()

        def two(c):
            place = self.level(c, i)

            @pl.when(place.outer == 1)
            def _():
                self.gather_send(c, i, eout, 2, 4, place.inner_peer).wait_recv()
                self.gather_send(c, i, ein, 1, 4, place.outer_peer).start()

        def three(c):
            place = self.level(c, i)

            @pl.when(place.outer == 0)
            def _():
                self.gather_send(c, i, ein, 1, 4, place.inner_peer).wait_recv()
        return [zero, one, two, three]

    def gather_ends(self, i):
        n = self.sizes[i]
        ein, eout = 6 + 2 * i, 7 + 2 * i

        def ends(c):
            place = self.level(c, i)
            if n == 2:
                self.gather_send(c, i, eout, 0, 1, place.inner_peer).wait_send()
            elif n == 4:
                @pl.when(place.outer == 0)
                def _():
                    self.gather_send(c, i, ein, 0, 1, place.inner_peer).wait_send()

                @pl.when(place.outer == 1)
                def _():
                    self.gather_send(c, i, eout, 0, 2, place.inner_peer).wait_send()
                    self.gather_send(c, i, ein, 1, 4, place.outer_peer).wait_send()
        return ends

    def own_copy(self, c):
        start = self.base(c, 3)
        rows = pl.ds(pl.multiple_of(start, 8), self.lens[2])
        return pltpu.make_async_copy(self.grad.at[c, rows], self.out.at[c, rows], self.local.at[c])

    def stages(self):
        groups = [self.reduce_stages(0), self.reduce_stages(1), self.reduce_stages(2)]

        def settle(c):
            self.own_copy(c).start()
            self.own_copy(c).wait()
        groups += [[settle], self.gather_stages(2), self.gather_stages(1), self.gather_stages(0)]
        joined = []
        for group in groups:
            if not group:
                continue
            if joined:
                joined[-1] = joined[-1] + [group[0]]
                joined += [[stage] for stage in group[1:]]
            else:
                joined = [[stage] for stage in group]
        return [functools.partial(run_all, stages) for stages in joined]

    def ends(self, c):
        for i in range(3):
            if self.sizes[i] > 1:
                self.reduce_ends(i)(c)
                self.gather_ends(i)(c)

    def greet(self):
        barrier = pltpu.get_barrier_semaphore()
        count = jnp.int32(0)
        for place in (self.fast, self.mids, self.slow):
            if place.size == 1:
                continue
            pl.semaphore_signal(barrier, inc=1, device_id={"dp": place.inner_peer}, device_id_type=MESH)
            count = count + 1
            if place.size == 4:
                @pl.when(place.outer == 1)
                def _():
                    pl.semaphore_signal(barrier, inc=1, device_id={"dp": place.outer_peer}, device_id_type=MESH)
                count = count + jnp.where(place.outer == 1, 1, 0)
        pl.semaphore_wait(barrier, count)


def run_all(stages, c):
    for stage in stages:
        stage(c)


def ar_kernel(dims, count, rows, small_rows, lead, src, small_src, out, small_out,
              grad, land, small_grad, small_land, load, send, recv, local, ssend, srecv, slocal):
    dp = lax.axis_index("dp")
    main = Ring(dp, dims, rows, grad, land, out, send, recv, local)
    small = Ring(dp, dims, small_rows, small_grad, small_land, small_out, ssend, srecv, slocal)

    @pl.loop(0, count)
    def _(c):
        pltpu.make_async_copy(src.at[c], grad.at[c], load.at[c]).start()
    pltpu.make_async_copy(small_src, small_grad, load.at[count]).start()
    main.greet()
    stages, small_stages = main.stages(), small.stages()
    depth = len(stages)

    @pl.loop(0, count + 1 + lead + depth)
    def _(t):
        for s in reversed(range(depth)):
            c = t - s - (lead if s else 0)

            @pl.when((c >= 0) & (c < count))
            def _():
                if s == 0:
                    pltpu.make_async_copy(src.at[c], grad.at[c], load.at[c]).wait()
                stages[s](c)

            @pl.when(c == count)
            def _():
                if s == 0:
                    pltpu.make_async_copy(small_src, small_grad, load.at[count]).wait()
                small_stages[s](0)

    @pl.loop(0, count)
    def _(c):
        main.ends(c)
    small.ends(0)


def all_reduce(src, small, n, lead=1, collective_id=0):
    dims = dp_dims(n)
    count, rows, width = src.shape
    small_rows = small.shape[1]
    land, _ = Ring.land_rows(rows, dims)
    small_land, _ = Ring.land_rows(small_rows, dims)
    return pl.pallas_call(
        functools.partial(ar_kernel, dims, count, rows, small_rows, lead),
        out_shape=(jax.ShapeDtypeStruct(src.shape, src.dtype), jax.ShapeDtypeStruct(small.shape, small.dtype)),
        in_specs=[pl.BlockSpec(memory_space=pl.ANY)] * 2,
        out_specs=(pl.BlockSpec(memory_space=pl.ANY),) * 2,
        scratch_shapes=[
            pltpu.VMEM((count, rows, width), src.dtype),
            pltpu.VMEM((count, land, width), src.dtype),
            pltpu.VMEM(small.shape, small.dtype),
            pltpu.VMEM((1, small_land, small.shape[2]), small.dtype),
            pltpu.SemaphoreType.DMA((count + 1,)),
            pltpu.SemaphoreType.DMA((count, 12)),
            pltpu.SemaphoreType.DMA((count, 12)),
            pltpu.SemaphoreType.DMA((count,)),
            pltpu.SemaphoreType.DMA((1, 12)),
            pltpu.SemaphoreType.DMA((1, 12)),
            pltpu.SemaphoreType.DMA((1,)),
        ],
        compiler_params=pltpu.CompilerParams(collective_id=collective_id, has_side_effects=True, vmem_limit_bytes=62 * 2**20),
    )(src, small)


MICRO = 4


def shifted(x, axis, by):
    count = lax.axis_size(axis)
    pairs = [(i, i + by) for i in range(count) if 0 <= i + by < count]
    return lax.ppermute(x, axis, pairs)


def matmul_low(left, right):
    return jnp.einsum(
        "...ij,...jk->...ik",
        left.astype(jnp.bfloat16),
        right.astype(jnp.bfloat16),
        preferred_element_type=jnp.float32,
    )


def matmul_back(left, right, grad):
    grad_low = grad.astype(jnp.bfloat16)
    left_grad = jnp.einsum(
        "...ik,...jk->...ij",
        grad_low,
        right.astype(jnp.bfloat16),
        preferred_element_type=jnp.float32,
    )
    right_grad = jnp.einsum(
        "...ij,...ik->...jk",
        left.astype(jnp.bfloat16),
        grad_low,
        preferred_element_type=jnp.float32,
    )
    return (left_grad, right_grad)


def depthwise(tensor_in, kernel, shift_row):
    image_count = tensor_in.shape[0]
    channels = tensor_in.shape[2]
    square = tensor_in.reshape(image_count, 7, 7, channels)
    padded = jnp.pad(square, ((0, 0), (1, 1), (1, 1), (0, 0)))
    running = jnp.zeros_like(square) + shift_row
    for offset in range(9):
        row_at = offset // 3
        col_at = offset % 3
        running = running + padded[:, row_at : row_at + 7, col_at : col_at + 7, :] * kernel[offset]
    return running.reshape(image_count, 49, channels)


def layer_norm(tensor_in, gain_row, shift_row):
    centered = tensor_in - jnp.mean(tensor_in, axis=-1, keepdims=True)
    spread_sq = jnp.mean(centered * centered, axis=-1, keepdims=True)
    return centered * lax.rsqrt(spread_sq + 1e-05) * gain_row + shift_row


def first_piece(tensor_in, conv_weight, conv_bias, norm_gain, norm_bias):
    stream = tensor_in + depthwise(tensor_in, conv_weight[0], conv_bias[0])
    normed = layer_norm(stream, norm_gain[0], norm_bias[0]).reshape(-1, tensor_in.shape[2])
    return (stream, normed)


def second_piece(stream, attended, b_proj, conv_weight, conv_bias, norm_gain, norm_bias):
    stream = stream + (attended + b_proj).reshape(stream.shape)
    stream = stream + depthwise(stream, conv_weight[1], conv_bias[1])
    normed = layer_norm(stream, norm_gain[1], norm_bias[1]).reshape(-1, stream.shape[2])
    return (stream, normed)


def gelu_piece(hidden_pre, b_fc1):
    return jax.nn.gelu(hidden_pre + b_fc1, approximate=False)


def softmax_back(weights_soft, grad):
    return weights_soft * (grad - jnp.sum(grad * weights_soft, axis=-1, keepdims=True))


def spatial_mix(queries, keys_all, values_all):
    scaled = queries * 32.0 ** (-0.5)
    weights_soft = jax.nn.softmax(matmul_low(scaled, jnp.swapaxes(keys_all, 2, 3)), axis=-1)
    return matmul_low(weights_soft, values_all)


def channel_mix(queries, keys_all, values_all):
    scaled = jnp.swapaxes(queries, 2, 3) * 32.0 ** (-0.5)
    weights_soft = jax.nn.softmax(matmul_low(scaled, keys_all), axis=-1)
    return jnp.swapaxes(matmul_low(weights_soft, jnp.swapaxes(values_all, 2, 3)), 2, 3)


def spatial_back(queries, keys_all, values_all, grad_mixed):
    scaled = queries * 32.0 ** (-0.5)
    keys_turned = jnp.swapaxes(keys_all, 2, 3)
    weights_soft = jax.nn.softmax(matmul_low(scaled, keys_turned), axis=-1)
    grad_weights, grad_values = matmul_back(weights_soft, values_all, grad_mixed)
    grad_scores = softmax_back(weights_soft, grad_weights)
    grad_scaled, grad_turned = matmul_back(scaled, keys_turned, grad_scores)
    return (grad_scaled * 32.0 ** (-0.5), jnp.swapaxes(grad_turned, 2, 3), grad_values)


def channel_back(queries, keys_all, values_all, grad_mixed):
    scaled = jnp.swapaxes(queries, 2, 3) * 32.0 ** (-0.5)
    weights_soft = jax.nn.softmax(matmul_low(scaled, keys_all), axis=-1)
    values_turned = jnp.swapaxes(values_all, 2, 3)
    grad_weights, grad_turned = matmul_back(
        weights_soft, values_turned, jnp.swapaxes(grad_mixed, 2, 3)
    )
    grad_scores = softmax_back(weights_soft, grad_weights)
    grad_scaled, grad_keys = matmul_back(scaled, keys_all, grad_scores)
    return (
        jnp.swapaxes(grad_scaled, 2, 3) * 32.0 ** (-0.5),
        grad_keys,
        jnp.swapaxes(grad_turned, 2, 3),
    )


def block_forward(tensor_in, params, is_first):
    (
        conv_weight,
        conv_bias,
        norm_gain,
        norm_bias,
        w_qkv,
        w_proj,
        b_proj,
        w_fc1,
        b_fc1,
        w_fc2,
        b_fc2,
    ) = params
    image_count = tensor_in.shape[0]
    channels = tensor_in.shape[2]
    head_count = channels // 32
    stream_one, normed_one = first_piece(tensor_in, conv_weight, conv_bias, norm_gain, norm_bias)
    packed = matmul_low(normed_one, w_qkv).reshape(image_count, 49, 3, head_count, 32)
    queries = jnp.transpose(packed[:, :, 0], (0, 2, 1, 3))
    keys_all = jnp.transpose(packed[:, :, 1], (0, 2, 1, 3))
    values_all = jnp.transpose(packed[:, :, 2], (0, 2, 1, 3))
    mixed = lax.cond(is_first, spatial_mix, channel_mix, queries, keys_all, values_all)
    mixed = jnp.transpose(mixed, (0, 2, 1, 3)).reshape(image_count * 49, channels)
    attended = matmul_low(mixed, w_proj)
    stream_two, normed_two = second_piece(
        stream_one, attended, b_proj, conv_weight, conv_bias, norm_gain, norm_bias
    )
    hidden_pre = matmul_low(normed_two, w_fc1)
    hidden = gelu_piece(hidden_pre, b_fc1)
    result = stream_two + (matmul_low(hidden, w_fc2) + b_fc2).reshape(stream_two.shape)
    saved = (
        tensor_in,
        normed_one,
        queries,
        keys_all,
        values_all,
        mixed,
        stream_one,
        attended,
        normed_two,
        hidden_pre,
        hidden,
    )
    return (result, saved)


def block_backward(saved, cotangent, params, is_first):
    (
        conv_weight,
        conv_bias,
        norm_gain,
        norm_bias,
        w_qkv,
        w_proj,
        b_proj,
        w_fc1,
        b_fc1,
        w_fc2,
        b_fc2,
    ) = params
    (
        tensor_in,
        normed_one,
        queries,
        keys_all,
        values_all,
        mixed,
        stream_one,
        attended,
        normed_two,
        hidden_pre,
        hidden,
    ) = saved
    image_count = tensor_in.shape[0]
    channels = tensor_in.shape[2]
    head_count = channels // 32
    grad_b_fc2 = jnp.sum(cotangent, axis=(0, 1))
    grad_out = cotangent.reshape(image_count * 49, channels)
    grad_hidden, grad_w_fc2 = matmul_back(hidden, w_fc2, grad_out)
    unused_gelu, gelu_pull = jax.vjp(gelu_piece, hidden_pre, b_fc1)
    grad_pre, grad_b_fc1 = gelu_pull(grad_hidden)
    grad_normed_two, grad_w_fc1 = matmul_back(normed_two, w_fc1, grad_pre)
    unused_second, second_pull = jax.vjp(
        second_piece, stream_one, attended, b_proj, conv_weight, conv_bias, norm_gain, norm_bias
    )
    grad_stream_one, grad_attended, grad_b_proj, conv_w_two, conv_b_two, gain_two, shift_two = (
        second_pull((cotangent, grad_normed_two))
    )
    grad_mixed, grad_w_proj = matmul_back(mixed, w_proj, grad_attended)
    grad_mixed = jnp.transpose(grad_mixed.reshape(image_count, 49, head_count, 32), (0, 2, 1, 3))
    grad_q, grad_k, grad_v = lax.cond(
        is_first, spatial_back, channel_back, queries, keys_all, values_all, grad_mixed
    )
    grad_packed = jnp.transpose(
        jnp.stack([grad_q, grad_k, grad_v], axis=1), (0, 3, 1, 2, 4)
    ).reshape(image_count * 49, 3 * channels)
    grad_normed_one, grad_w_qkv = matmul_back(normed_one, w_qkv, grad_packed)
    unused_first, first_pull = jax.vjp(
        first_piece, tensor_in, conv_weight, conv_bias, norm_gain, norm_bias
    )
    grad_in, conv_w_one, conv_b_one, gain_one, shift_one = first_pull(
        (grad_stream_one, grad_normed_one)
    )
    grads = (
        conv_w_one + conv_w_two,
        conv_b_one + conv_b_two,
        gain_one + gain_two,
        shift_one + shift_two,
        grad_w_qkv,
        grad_w_proj,
        grad_b_proj,
        grad_w_fc1,
        grad_b_fc1,
        grad_w_fc2,
        grad_b_fc2,
    )
    return (grad_in, grads)


def on_device(
    section_inputs,
    conv_weight,
    conv_bias,
    norm_gain,
    norm_bias,
    w_qkv,
    w_proj,
    b_proj,
    w_fc1,
    b_fc1,
    w_fc2,
    b_fc2,
):
    is_first = lax.axis_index("pipe") == 0
    params = tuple(
        (
            weight[0].astype(jnp.float32)
            for weight in (
                conv_weight,
                conv_bias,
                norm_gain,
                norm_bias,
                w_qkv,
                w_proj,
                b_proj,
                w_fc1,
                b_fc1,
                w_fc2,
                b_fc2,
            )
        )
    )
    image_count = section_inputs.shape[1]
    width = section_inputs.shape[3]
    pieces = section_inputs[0].reshape(MICRO, image_count // MICRO, 49, width)
    received = jnp.zeros(pieces.shape[1:], jnp.bfloat16)
    saved_all = []
    outputs = []
    for moment in range(MICRO + 1):
        own_piece = pieces[min(moment, MICRO - 1)].astype(jnp.float32)
        section_in = jnp.where(is_first, own_piece, received.astype(jnp.float32))
        result, saved = block_forward(section_in, params, is_first)
        saved_all.append(saved)
        outputs.append(result)
        if moment < MICRO:
            received = shifted(result.astype(jnp.bfloat16), "pipe", 1)
    grad_received = jnp.zeros(pieces.shape[1:], jnp.bfloat16)
    totals = jax.tree.map(jnp.zeros_like, params)
    input_grads = []
    for moment in range(MICRO + 1):
        own_piece = pieces[max(MICRO - 1 - moment, 0)].astype(jnp.float32)
        cotangent = jnp.where(is_first, grad_received.astype(jnp.float32), own_piece)
        saved = saved_all[MICRO - moment]
        input_grad, weight_grads = block_backward(saved, cotangent, params, is_first)
        valid = jnp.where(
            is_first, 1.0 if moment >= 1 else 0.0, 1.0 if moment < MICRO else 0.0
        ).astype(jnp.float32)
        totals = jax.tree.map(lambda running, fresh: running + fresh * valid, totals, weight_grads)
        input_grads.append(input_grad)
        if moment < MICRO:
            grad_received = shifted(input_grad.astype(jnp.bfloat16), "pipe", -1)
    grads_ordered = jnp.concatenate(
        [input_grads[MICRO - index_mb] for index_mb in range(MICRO)], axis=0
    )
    acts_ordered = jnp.concatenate([outputs[index_mb + 1] for index_mb in range(MICRO)], axis=0)
    section_ends = jnp.where(is_first, grads_ordered, acts_ordered)[None]
    names = len(totals)
    small = jnp.concatenate([totals[i].reshape(-1) for i in (0, 1, 2, 3, 6, 8, 10)])
    lanes = 128
    small_rows = 16 * lax.axis_size("dp")
    small = jnp.pad(small, (0, small_rows * lanes - small.shape[0])).reshape(1, small_rows, lanes)
    big = [to_chunks(totals[i].astype(jnp.bfloat16)) for i in (9, 7, 5, 4)]
    counts = [v.shape[0] for v in big]
    rows = padded_rows(width, lax.axis_size("dp"))
    stacked = jnp.pad(jnp.concatenate(big, axis=0), ((0, 0), (0, rows - width), (0, 0)))
    done, small_done = all_reduce(stacked, small, lax.axis_size("dp"))
    done = done[:, :width]
    small_done = small_done.reshape(-1)
    summed = [None] * names
    at = 0
    for i in (0, 1, 2, 3, 6, 8, 10):
        summed[i] = small_done[at : at + totals[i].size].reshape(totals[i].shape)[None]
        at += totals[i].size
    at = 0
    for i, number in zip((9, 7, 5, 4), counts):
        summed[i] = from_chunks(done[at : at + number], totals[i].shape)[None]
        at += number
    return (section_ends, *summed)


CHUNK = 384


def padded_rows(rows, n):
    return -(-rows // (16 * n)) * 16 * n


def to_chunks(grad):
    rows, columns = grad.shape
    side = 768
    cut = grad.reshape(rows // side, side, columns // CHUNK, CHUNK)
    return jnp.transpose(cut, (0, 2, 1, 3)).reshape(-1, side, CHUNK)


def from_chunks(chunks, shape):
    rows, columns = shape
    side = 768
    cut = chunks.reshape(rows // side, columns // CHUNK, side, CHUNK)
    return jnp.transpose(cut, (0, 2, 1, 3)).reshape(shape).astype(jnp.float32)


def solution(mesh):
    return jax.shard_map(
        on_device,
        mesh=mesh,
        in_specs=(
            P("pipe", "dp", None, None),
            P("pipe", None, None, None),
            P("pipe", None, None),
            P("pipe", None, None),
            P("pipe", None, None),
            P("pipe", None, None),
            P("pipe", None, None),
            P("pipe", None),
            P("pipe", None, None),
            P("pipe", None),
            P("pipe", None, None),
            P("pipe", None),
        ),
        out_specs=(
            P("pipe", "dp", None, None),
            P("pipe", None, None, None),
            P("pipe", None, None),
            P("pipe", None, None),
            P("pipe", None, None),
            P("pipe", None, None),
            P("pipe", None, None),
            P("pipe", None),
            P("pipe", None, None),
            P("pipe", None),
            P("pipe", None, None),
            P("pipe", None),
        ),
        check_vma=False,
    )
```

```python
import functools

import jax
import jax.numpy as jnp
from jax import lax
from jax.experimental import pallas as pl
from jax.experimental.pallas import tpu as pltpu
from jax.sharding import PartitionSpec as P

HEAD = 32
GROUP = 256
SLOT = 64
BF = jnp.bfloat16
F32 = jnp.float32


def cols(j, width=GROUP):
    return pl.ds(pl.multiple_of(j * width, width), width)


def dot(a, b):
    return lax.dot_general(a, b, (((1,), (0,)), ((), ())), preferred_element_type=F32)


def dot_t(a, b):
    return lax.dot_general(a, b, (((1,), (1,)), ((), ())), preferred_element_type=F32)


def t_dot(a, b):
    return lax.dot_general(a, b, (((0,), (0,)), ((), ())), preferred_element_type=F32)


def fill_swap(ref, images):
    rows, columns = ref.shape
    block = 128

    @pl.loop(0, rows // block)
    def _(b):
        r = lax.broadcasted_iota(jnp.int32, (block, columns), 0) + b * block
        c = lax.broadcasted_iota(jnp.int32, (block, columns), 1)
        image, position = lax.div(r, SLOT), lax.rem(r, SLOT)
        hit = (c == position * images + image) & (position < 49)
        ref[pl.ds(pl.multiple_of(b * block, block), block), :] = jnp.where(hit, 1.0, 0.0).astype(BF)


def clear_border(pad, images):
    zero = jnp.zeros((9 * images, pad.shape[1]), pad.dtype)
    pad[0 : 9 * images, :] = zero
    pad[72 * images : 81 * images, :] = zero
    one = jnp.zeros((images, pad.shape[1]), pad.dtype)

    @pl.loop(1, 8)
    def _(r):
        pad[pl.ds(pl.multiple_of(r * 9 * images, 16), images), :] = one
        pad[pl.ds(pl.multiple_of((r * 9 + 8) * images, 16), images), :] = one


def inside(r, images):
    return pl.ds(pl.multiple_of(((r + 1) * 9 + 1) * images, 16), 7 * images)


def grid_row(r, images):
    return pl.ds(pl.multiple_of(r * 7 * images, 16), 7 * images)


def encode(pad, kernel, bias, out, images):
    @pl.loop(0, pad.shape[1] // 128)
    def _(lane):
        ls = cols(lane, 128)
        taps = [jnp.broadcast_to(kernel[pl.ds(t, 1), ls], (images, 128)) for t in range(9)]
        shift = jnp.broadcast_to(bias[:, ls], (images, 128))

        @pl.loop(0, 7)
        def _(r):
            for c in range(7):
                total = shift
                for t in range(9):
                    at = pl.multiple_of(((r + t // 3) * 9 + c + t % 3) * images, 16)
                    piece = pad[pl.ds(at, images), ls]
                    total = total + piece * taps[t]
                    if t == 4:
                        total = total + piece
                out[pl.ds(pl.multiple_of((r * 7 + c) * images, 16), images), ls] = total


def normalise(stream, gain, bias, out, images):
    @pl.loop(0, 49, unroll=7)
    def _(p):
        rows = pl.ds(pl.multiple_of(p * images, 16), images)
        s = stream[rows, :]
        centered = s - jnp.mean(s, axis=-1, keepdims=True)
        spread = jnp.mean(centered * centered, axis=-1, keepdims=True)
        out[rows, :] = (centered * lax.rsqrt(spread + 1e-5) * gain[...] + bias[...]).astype(BF)


def head_mask(rows_per, count, lanes):
    shape = (count * rows_per, lanes)
    r = lax.broadcasted_iota(jnp.int32, shape, 0)
    c = lax.broadcasted_iota(jnp.int32, shape, 1)
    return lax.div(r, rows_per) == lax.div(c, HEAD)


def spread_heads(x, mask):
    count = mask.shape[0] // x.shape[0]
    return jnp.where(mask, jnp.concatenate([x] * count, axis=0), jnp.zeros((), x.dtype))


def fold_heads(x, mask, rows_per):
    kept = jnp.where(mask, x, 0.0)
    total = kept[0:rows_per]
    for h in range(1, x.shape[0] // rows_per):
        total = total + kept[h * rows_per : (h + 1) * rows_per]
    return total


def soft_down(scores, valid):
    if valid < scores.shape[0]:
        r = lax.broadcasted_iota(jnp.int32, scores.shape, 0)
        scores = jnp.where(r < valid, scores, -jnp.inf)
    e = jnp.exp(scores - jnp.max(scores, axis=0, keepdims=True))
    return e / jnp.sum(e, axis=0, keepdims=True)


def spatial_forward(packed, mixed, soft, images):
    width = mixed.shape[1]
    groups = width // GROUP

    @pl.loop(0, images)
    def _(i):
        rows = pl.ds(pl.multiple_of(i * SLOT, SLOT), SLOT)
        mask = head_mask(SLOT, GROUP // HEAD, GROUP)
        for g in range(groups):
            q, k, v = (packed[rows, part * width + g * GROUP : part * width + (g + 1) * GROUP] for part in range(3))
            weights = soft_down(dot_t(k, spread_heads(q, mask)), 49).astype(BF)
            soft[i, g] = weights
            mixed[rows, g * GROUP : (g + 1) * GROUP] = fold_heads(t_dot(weights, v), mask, SLOT).astype(BF)


def channel_forward(packed, mixed, soft, images):
    width = mixed.shape[1]

    @pl.loop(0, images)
    def _(i):
        rows = pl.ds(pl.multiple_of(i * SLOT, SLOT), SLOT)
        mask = head_mask(HEAD, 128 // HEAD, 128)
        for g in range(width // 128):
            q, k, v = (packed[rows, part * width + g * 128 : part * width + (g + 1) * 128] for part in range(3))
            weights = soft_down(fold_heads(t_dot(k, q), mask, HEAD), HEAD).astype(BF)
            soft[i, g // 2, g % 2 * HEAD : (g % 2 + 1) * HEAD, 0:128] = weights
            mixed[rows, g * 128 : (g + 1) * 128] = dot(v, spread_heads(weights, mask)).astype(BF)


def gelu_both(x):
    half = 0.5 + 0.5 * lax.erf(x * 0.7071067811865476)
    return x * half, half + x * (0.3989422804014327 * jnp.exp(-0.5 * x * x))


def forward_kernel(images, role, x, conv_w, conv_b, gain, shift, b_proj, b_fc1, b_fc2,
                   w_qkv, w_proj, w_fc1, w_fc2, *refs):
    earlier = len(refs) - 32
    (result, o_one, o_mid, o_two, o_n1, o_packed, o_soft, o_mixed, o_n2, o_hidden, o_slope,
     v_qkv, v_proj, v_fc1, v_fc2, pad, one, mid, two, n1, swap, n1s, packed, soft, mixed_s, mixed,
     n2, hidden, slope, end, load, store) = refs[earlier:]
    rows = 49 * images
    width = x.shape[1]
    loads = [pltpu.make_async_copy(src, dst, load.at[at]) for at, (src, dst) in enumerate(
        ((w_qkv, v_qkv), (w_proj, v_proj), (w_fc1, v_fc1), (w_fc2, v_fc2)))]
    stores = [pltpu.make_async_copy(src, dst, store.at[at]) for at, (src, dst) in enumerate(
        ((one, o_one), (mid, o_mid), (two, o_two), (n1, o_n1), (packed, o_packed), (soft, o_soft),
         (mixed, o_mixed), (n2, o_n2), (hidden, o_hidden), (slope, o_slope), (end, result)))]

    @pl.when(role[1] == 1)
    def _():
        for copy in loads:
            copy.start()
        fill_swap(swap, images)
        clear_border(pad, images)

        @pl.loop(0, 7)
        def _(r):
            pad[inside(r, images), :] = x[grid_row(r, images), :].astype(F32)
        encode(pad, conv_w.at[0], conv_b.at[pl.ds(0, 1)], one, images)
        stores[0].start()
        normalise(one, gain.at[pl.ds(0, 1)], shift.at[pl.ds(0, 1)], n1, images)
        stores[3].start()

        @pl.loop(0, width // GROUP)
        def _(j):
            n1s[:, cols(j)] = dot(swap[...], n1[:, cols(j)]).astype(BF)
        loads[0].wait()

        @pl.loop(0, 3 * width // GROUP)
        def _(j):
            scale = jnp.where(j < width // GROUP, HEAD ** -0.5, 1.0)
            packed[:, cols(j)] = (dot(n1s[...], v_qkv[:, cols(j)]) * scale).astype(BF)
        stores[4].start()

        @pl.when(role[0] == 1)
        def _():
            spatial_forward(packed, mixed_s, soft, images)

        @pl.when(role[0] == 0)
        def _():
            channel_forward(packed, mixed_s, soft, images)
        stores[5].start()

        @pl.loop(0, width // GROUP)
        def _(j):
            mixed[:, cols(j)] = t_dot(swap[...], mixed_s[:, cols(j)]).astype(BF)
        stores[6].start()
        loads[1].wait()

        @pl.loop(0, width // GROUP)
        def _(j):
            mid[:, cols(j)] = one[:, cols(j)] + dot(mixed[...], v_proj[:, cols(j)]) + b_proj[:, cols(j)]
        stores[1].start()

        @pl.loop(0, 7)
        def _(r):
            pad[inside(r, images), :] = mid[grid_row(r, images), :]
        encode(pad, conv_w.at[1], conv_b.at[pl.ds(1, 1)], two, images)
        stores[2].start()
        normalise(two, gain.at[pl.ds(1, 1)], shift.at[pl.ds(1, 1)], n2, images)
        stores[7].start()
        loads[2].wait()

        @pl.loop(0, v_fc1.shape[1] // GROUP)
        def _(j):
            pre = dot(n2[...], v_fc1[:, cols(j)]) + b_fc1[:, cols(j)]
            value, rate = gelu_both(pre)
            hidden[:, cols(j)] = value.astype(BF)
            slope[:, cols(j)] = rate.astype(BF)
        stores[8].start()
        stores[9].start()
        loads[3].wait()

        @pl.loop(0, width // GROUP)
        def _(j):
            end[:, cols(j)] = two[:, cols(j)] + dot(hidden[...], v_fc2[:, cols(j)]) + b_fc2[:, cols(j)]
        stores[10].start()
        for copy in stores:
            copy.wait()


def forward_block(role, x, params, images, earlier=()):
    conv_w, conv_b, gain, shift, w_qkv, w_proj, b_proj, w_fc1, b_fc1, w_fc2, b_fc2 = params
    rows, width = x.shape
    wide = w_fc1.shape[1]
    slots = images * SLOT
    any_space = pl.BlockSpec(memory_space=pl.ANY)
    vmem = pl.BlockSpec(memory_space=pltpu.VMEM)
    outs = [((rows, width), F32), ((rows, width), F32), ((rows, width), F32), ((rows, width), F32),
            ((rows, width), BF), ((slots, 3 * width), BF), ((images, width // GROUP, SLOT, 2 * GROUP), BF),
            ((rows, width), BF), ((rows, width), BF), ((rows, wide), BF), ((rows, wide), BF)]
    scratch = [w_qkv, w_proj, w_fc1, w_fc2]
    return pl.pallas_call(
        functools.partial(forward_kernel, images),
        out_shape=[jax.ShapeDtypeStruct(*o) for o in outs],
        in_specs=[pl.BlockSpec(memory_space=pltpu.SMEM)] + [vmem] * 8 + [any_space] * (4 + len(earlier)),
        out_specs=[any_space] * len(outs),
        input_output_aliases={13 + at: at for at in range(len(earlier))},
        scratch_shapes=[pltpu.VMEM(w.shape, w.dtype) for w in scratch] + [
            pltpu.VMEM((81 * images, width), F32),
            pltpu.VMEM((rows, width), F32), pltpu.VMEM((rows, width), F32), pltpu.VMEM((rows, width), F32),
            pltpu.VMEM((rows, width), BF), pltpu.VMEM((slots, rows), BF), pltpu.VMEM((slots, width), BF),
            pltpu.VMEM((slots, 3 * width), BF), pltpu.VMEM((images, width // GROUP, SLOT, 2 * GROUP), BF),
            pltpu.VMEM((slots, width), BF), pltpu.VMEM((rows, width), BF), pltpu.VMEM((rows, width), BF),
            pltpu.VMEM((rows, wide), BF), pltpu.VMEM((rows, wide), BF), pltpu.VMEM((rows, width), F32),
            pltpu.SemaphoreType.DMA((4,)), pltpu.SemaphoreType.DMA((11,)),
        ],
        compiler_params=pltpu.CompilerParams(vmem_limit_bytes=62 * 2**20),
    )(role, x, conv_w, conv_b, gain, shift, b_proj, b_fc1, b_fc2, w_qkv, w_proj, w_fc1, w_fc2, *earlier)


def encode_back(gpad, ipad, kernel, out, sums, first_row, bias_row, images):
    @pl.loop(0, gpad.shape[1] // 128)
    def _(lane):
        ls = cols(lane, 128)
        taps = [jnp.broadcast_to(kernel[pl.ds(8 - t, 1), ls], (images, 128)) for t in range(9)]
        zero = jnp.zeros((images, 128), F32)

        def row(r, totals):
            totals = list(totals)
            for c in range(7):
                centre = gpad[pl.ds(pl.multiple_of(((r + 1) * 9 + c + 1) * images, 16), images), ls]
                total = centre
                totals[9] = totals[9] + centre
                for t in range(9):
                    at = pl.ds(pl.multiple_of(((r + t // 3) * 9 + c + t % 3) * images, 16), images)
                    total = total + gpad[at, ls] * taps[t]
                    totals[t] = totals[t] + ipad[at, ls] * centre
                out[pl.ds(pl.multiple_of((r * 7 + c) * images, 16), images), ls] = total
            return tuple(totals)
        totals = lax.fori_loop(0, 7, row, (zero,) * 10)
        for t in range(9):
            sums[pl.ds(first_row + t, 1), ls] = jnp.sum(totals[t], axis=0, keepdims=True)
        sums[pl.ds(bias_row, 1), ls] = jnp.sum(totals[9], axis=0, keepdims=True)


def normalise_back(stream, grad, base, gain, out_rows, sums, gain_row, shift_row, acc, images):
    acc[...] = jnp.zeros_like(acc)

    @pl.loop(0, 49, unroll=7)
    def _(p):
        rows = pl.ds(pl.multiple_of(p * images, 16), images)
        s, dy = stream[rows, :], grad[rows, :]
        centered = s - jnp.mean(s, axis=-1, keepdims=True)
        rate = lax.rsqrt(jnp.mean(centered * centered, axis=-1, keepdims=True) + 1e-5)
        unit = centered * rate
        acc[0] += dy * unit
        acc[1] += dy
        dg = dy * gain[...]
        m1 = jnp.mean(dg, axis=-1, keepdims=True)
        m2 = jnp.mean(dg * unit, axis=-1, keepdims=True)
        ref, at = out_rows(p)
        ref[at, :] = base[rows, :].astype(F32) + rate * (dg - m1 - unit * m2)
    sums[pl.ds(gain_row, 1), :] = jnp.sum(acc[0], axis=0, keepdims=True)
    sums[pl.ds(shift_row, 1), :] = jnp.sum(acc[1], axis=0, keepdims=True)


def spatial_backward(packed, grad_mixed, soft, images):
    width = grad_mixed.shape[1]

    @pl.loop(0, images)
    def _(i):
        rows = pl.ds(pl.multiple_of(i * SLOT, SLOT), SLOT)
        mask = head_mask(SLOT, GROUP // HEAD, GROUP)
        for g in range(width // GROUP):
            at = [slice(part * width + g * GROUP, part * width + (g + 1) * GROUP) for part in range(3)]
            q, k, v = (packed[rows, a] for a in at)
            weights = soft[i, g]
            out_spread = spread_heads(grad_mixed[rows, g * GROUP : (g + 1) * GROUP], mask)
            w = weights.astype(F32)
            dw = dot_t(v, out_spread)
            ds = (w * (dw - jnp.sum(dw * w, axis=0, keepdims=True))).astype(BF)
            packed[rows, at[2]] = dot(weights, out_spread).astype(BF)
            packed[rows, at[1]] = dot(ds, spread_heads(q, mask)).astype(BF)
            packed[rows, at[0]] = (fold_heads(t_dot(ds, k), mask, SLOT) * HEAD ** -0.5).astype(BF)


def channel_backward(packed, grad_mixed, soft, images):
    width = grad_mixed.shape[1]

    @pl.loop(0, images)
    def _(i):
        rows = pl.ds(pl.multiple_of(i * SLOT, SLOT), SLOT)
        mask = head_mask(HEAD, 128 // HEAD, 128)
        for g in range(width // 128):
            at = [slice(part * width + g * 128, part * width + (g + 1) * 128) for part in range(3)]
            q, k, v = (packed[rows, a] for a in at)
            weights = soft[i, g // 2, g % 2 * HEAD : (g % 2 + 1) * HEAD, 0:128]
            do = grad_mixed[rows, g * 128 : (g + 1) * 128]
            w = weights.astype(F32)
            dw = fold_heads(t_dot(v, do), mask, HEAD)
            ds = spread_heads((w * (dw - jnp.sum(dw * w, axis=0, keepdims=True))).astype(BF), mask)
            packed[rows, at[2]] = dot_t(do, spread_heads(weights, mask)).astype(BF)
            packed[rows, at[1]] = dot_t(q, ds).astype(BF)
            packed[rows, at[0]] = (dot(k, ds) * HEAD ** -0.5).astype(BF)


def backward_kernel(images, role, cot, x, conv_w, gain, w_qkv, w_proj, w_fc1, w_fc2,
                    one, mid, two, h_packed, h_soft, h_slope, *refs):
    earlier = len(refs) - 26
    (o_grad, o_packed, o_att, o_pre, o_sums,
     v_qkv, v_proj, v_fc1, v_fc2, gpad, ipad, stream_two, stream_one, packed, soft, slope,
     swap, gm_s, gp, gn, gmid, gatt, acc, sums, load, store) = refs[earlier:]
    rows = 49 * images
    width = x.shape[1]
    loads = [pltpu.make_async_copy(src, dst, load.at[at]) for at, (src, dst) in enumerate(
        ((w_fc2, v_fc2), (h_slope, slope), (w_fc1, v_fc1), (two, stream_two), (mid, gmid), (w_proj, v_proj),
         (h_soft, soft), (h_packed, packed), (w_qkv, v_qkv), (one, stream_one)))]
    stores = [pltpu.make_async_copy(src, dst, store.at[at]) for at, (src, dst) in enumerate(
        ((slope, o_pre), (gatt, o_att), (gp, o_packed), (gmid, o_grad), (sums, o_sums)))]

    @pl.when(role[1] == 1)
    def _():
        for copy in loads:
            copy.start()
        fill_swap(swap, images)
        clear_border(gpad, images)
        clear_border(ipad, images)
        sums[...] = jnp.zeros_like(sums)
        loads[0].wait()
        loads[1].wait()

        @pl.loop(0, v_fc2.shape[0] // GROUP)
        def _(j):
            pre = dot_t(cot[...], v_fc2[cols(j), :]) * slope[:, cols(j)].astype(F32)
            slope[:, cols(j)] = pre.astype(BF)
            sums[pl.ds(25 + lax.div(j, 3), 1), cols(lax.rem(j, 3))] = jnp.sum(pre, axis=0, keepdims=True)
        stores[0].start()

        @pl.loop(0, width // GROUP)
        def _(j):
            sums[pl.ds(29, 1), cols(j)] = jnp.sum(cot[:, cols(j)].astype(F32), axis=0, keepdims=True)
        loads[2].wait()

        @pl.loop(0, width // GROUP)
        def _(j):
            gn[:, cols(j)] = dot_t(slope[...], v_fc1[cols(j), :])
        loads[3].wait()
        loads[4].wait()

        def in_pad(p):
            at = ((lax.div(p, 7) + 1) * 9 + lax.rem(p, 7) + 1) * images
            return gpad, pl.ds(pl.multiple_of(at, 16), images)
        normalise_back(stream_two, gn, cot, gain.at[pl.ds(1, 1)], in_pad, sums, 21, 23, acc, images)

        @pl.loop(0, 7)
        def _(r):
            ipad[inside(r, images), :] = gmid[grid_row(r, images), :]
        encode_back(gpad, ipad, conv_w.at[1], gmid, sums, 9, 19, images)

        @pl.loop(0, width // GROUP)
        def _(j):
            sums[pl.ds(24, 1), cols(j)] = jnp.sum(gmid[:, cols(j)], axis=0, keepdims=True)
            gatt[:, cols(j)] = gmid[:, cols(j)].astype(BF)
        stores[1].start()
        loads[5].wait()

        @pl.loop(0, width // GROUP)
        def _(j):
            gp[:, cols(j)] = dot_t(gatt[...], v_proj[cols(j), :]).astype(BF)

        @pl.loop(0, width // GROUP)
        def _(j):
            gm_s[:, cols(j)] = dot(swap[...], gp[:, cols(j)]).astype(BF)
        loads[6].wait()
        loads[7].wait()

        @pl.when(role[0] == 1)
        def _():
            spatial_backward(packed, gm_s, soft, images)

        @pl.when(role[0] == 0)
        def _():
            channel_backward(packed, gm_s, soft, images)

        @pl.loop(0, 3 * width // GROUP)
        def _(j):
            gp[:, cols(j)] = t_dot(swap[...], packed[:, cols(j)]).astype(BF)
        stores[2].start()
        loads[8].wait()

        @pl.loop(0, width // GROUP)
        def _(j):
            gn[:, cols(j)] = dot_t(gp[...], v_qkv[cols(j), :])
        loads[9].wait()
        normalise_back(stream_one, gn, gmid, gain.at[pl.ds(0, 1)], in_pad, sums, 20, 22, acc, images)

        @pl.loop(0, 7)
        def _(r):
            ipad[inside(r, images), :] = x[grid_row(r, images), :].astype(F32)
        encode_back(gpad, ipad, conv_w.at[0], gmid, sums, 0, 18, images)
        stores[3].start()
        stores[4].start()
        for copy in stores:
            copy.wait()


def backward_block(role, cot, x, saved, params, images, earlier=()):
    conv_w, conv_b, gain, shift, w_qkv, w_proj, b_proj, w_fc1, b_fc1, w_fc2, b_fc2 = params
    one, mid, two, packed, soft, slope = saved
    rows, width = x.shape
    wide = w_fc1.shape[1]
    slots = images * SLOT
    any_space = pl.BlockSpec(memory_space=pl.ANY)
    vmem = pl.BlockSpec(memory_space=pltpu.VMEM)
    outs = [((rows, width), F32), ((rows, 3 * width), BF), ((rows, width), BF), ((rows, wide), BF), ((32, width), F32)]
    return pl.pallas_call(
        functools.partial(backward_kernel, images),
        out_shape=[jax.ShapeDtypeStruct(*o) for o in outs],
        in_specs=[pl.BlockSpec(memory_space=pltpu.SMEM)] + [vmem] * 4 + [any_space] * (10 + len(earlier)),
        out_specs=[any_space] * len(outs),
        input_output_aliases={15 + at: at for at in range(len(earlier))},
        scratch_shapes=[pltpu.VMEM(w.shape, w.dtype) for w in (w_qkv, w_proj, w_fc1, w_fc2)] + [
            pltpu.VMEM((81 * images, width), F32), pltpu.VMEM((81 * images, width), F32),
            pltpu.VMEM((rows, width), F32), pltpu.VMEM((rows, width), F32),
            pltpu.VMEM(packed.shape, BF), pltpu.VMEM(soft.shape, BF), pltpu.VMEM((rows, wide), BF),
            pltpu.VMEM((slots, rows), BF), pltpu.VMEM((slots, width), BF), pltpu.VMEM((rows, 3 * width), BF),
            pltpu.VMEM((rows, width), F32), pltpu.VMEM((rows, width), F32), pltpu.VMEM((rows, width), BF),
            pltpu.VMEM((2, images, width), F32), pltpu.VMEM((32, width), F32),
            pltpu.SemaphoreType.DMA((10,)), pltpu.SemaphoreType.DMA((5,)),
        ],
        compiler_params=pltpu.CompilerParams(vmem_limit_bytes=63 * 2**20),
    )(role, cot, x, conv_w, gain, w_qkv, w_proj, w_fc1, w_fc2, one, mid, two, packed, soft, slope, *earlier)


MESH = pl.DeviceIdType.MESH


def dp_dims(n):
    sizes = [1, 1, 1]
    at = 0
    left = n
    while left > 1:
        factor = 2 if left % 2 == 0 else left
        sizes[at % 3] *= factor
        left //= factor
        at += 1
    return tuple(sizes), (sizes[1] * sizes[2], sizes[2], 1)


class Place:
    def __init__(self, dp, size, stride):
        self.size = size
        pos = lax.rem(lax.div(dp, stride), size)
        low = pos < (size + 1) // 2
        self.outer = jnp.where(low, pos, size - 1 - pos)
        self.pos = pos
        self.low = low
        step = jnp.where(low, stride, -stride)
        self.inner_peer = dp + step
        self.outer_peer = dp - step


def pick(flag, a, b):
    out = object.__new__(Place)
    out.size = a.size
    for name in ("pos", "low", "outer", "inner_peer", "outer_peer"):
        setattr(out, name, jnp.where(flag, getattr(a, name), getattr(b, name)))
    return out


class Ring:
    def __init__(self, dp, dims, rows, grad, land, out, send, recv, local):
        (s0, s1, s2), (t0, t1, t2) = dims
        self.mids = Place(dp, s0, t0)
        self.fast, self.slow = Place(dp, s2, t2), Place(dp, s1, t1)
        self.dp, self.rows = dp, rows
        self.grad, self.land, self.out = grad, land, out
        self.send, self.recv, self.local = send, recv, local
        self.sizes = (s2, s0, s1)
        self.lens = (rows // s2, rows // s2 // s0, rows // (s0 * s1 * s2))

    @staticmethod
    def land_rows(rows, dims):
        s0, s1, s2 = dims[0]
        lens = (rows // s2, rows // s2 // s0, rows // (s0 * s1 * s2))
        total, starts = 0, []
        for n, length in zip((s2, s0, s1), lens):
            starts.append(total)
            total += length * (1 if n == 2 else 5)
        return total, starts

    def level(self, c, i):
        flag = lax.rem(c, 2) == 0
        if i == 1:
            return self.mids
        return pick(flag, self.fast, self.slow) if i == 0 else pick(flag, self.slow, self.fast)

    def base(self, c, i):
        start = 0
        for j in range(i):
            start = start + self.level(c, j).pos * self.lens[j]
        return start

    def span(self, c, i, a, b):
        place, length = self.level(c, i), self.lens[i]
        n = self.sizes[i]
        start = self.base(c, i) + jnp.where(place.low, a * length, (n - b) * length)
        return pl.ds(pl.multiple_of(start, 8), (b - a) * length)

    def copy(self, c, ev, src, dst, peer):
        return pltpu.make_async_remote_copy(
            src_ref=src, dst_ref=dst, send_sem=self.send.at[c, ev], recv_sem=self.recv.at[c, ev],
            device_id={"dp": peer}, device_id_type=MESH)

    def landing(self, c, i, at, length):
        start = self.land_rows(self.rows, ((self.sizes[1], self.sizes[2], self.sizes[0]), None))[1][i]
        return self.land.at[c, pl.ds(start + at, length)]

    def add(self, c, i, a, b, at, lo=None):
        rows = self.span(c, i, a, b)
        length = (b - a) * self.lens[i]
        got = self.landing(c, i, at, length)
        self.grad[c, rows] = self.grad[c, rows] + got[...]

    def reduce_send(self, c, i, ev, a, b, at, peer):
        rows = self.span(c, i, a, b)
        length = (b - a) * self.lens[i]
        return self.copy(c, ev, self.grad.at[c, rows], self.landing(c, i, at, length), peer)

    def reduce_stages(self, i):
        n, length = self.sizes[i], self.lens[i]
        ein, eout = 2 * i, 2 * i + 1
        if n == 1:
            return []
        if n == 2:
            def first(c):
                self.reduce_send(c, i, eout, 1, 2, 0, self.level(c, i).inner_peer).start()

            def last(c):
                self.reduce_send(c, i, eout, 0, 1, 0, self.level(c, i).inner_peer).wait_recv()
                self.add(c, i, 0, 1, 0)
            return [first, last]

        def zero(c):
            place = self.level(c, i)

            @pl.when(place.outer == 0)
            def _():
                self.reduce_send(c, i, ein, 1, 4, 0, place.inner_peer).start()

        def one(c):
            place = self.level(c, i)

            @pl.when(place.outer == 1)
            def _():
                self.reduce_send(c, i, ein, 1, 4, 0, place.inner_peer).wait_recv()
                self.add(c, i, 1, 4, 0)
                self.reduce_send(c, i, eout, 2, 4, 3 * length, place.inner_peer).start()

        def two(c):
            place = self.level(c, i)

            @pl.when(place.outer == 1)
            def _():
                self.reduce_send(c, i, eout, 0, 2, 3 * length, place.inner_peer).wait_recv()
                self.add(c, i, 0, 2, 3 * length)
                self.reduce_send(c, i, ein, 0, 1, 3 * length, place.outer_peer).start()

        def three(c):
            place = self.level(c, i)

            @pl.when(place.outer == 0)
            def _():
                self.reduce_send(c, i, ein, 0, 1, 3 * length, place.inner_peer).wait_recv()
                self.add(c, i, 0, 1, 3 * length)
        return [zero, one, two, three]

    def reduce_ends(self, i):
        n = self.sizes[i]
        ein, eout = 2 * i, 2 * i + 1

        def ends(c):
            place = self.level(c, i)
            if n == 2:
                self.reduce_send(c, i, eout, 1, 2, 0, place.inner_peer).wait_send()
            elif n == 4:
                @pl.when(place.outer == 0)
                def _():
                    self.reduce_send(c, i, ein, 1, 4, 0, place.inner_peer).wait_send()

                @pl.when(place.outer == 1)
                def _():
                    self.reduce_send(c, i, eout, 2, 4, 0, place.inner_peer).wait_send()
                    self.reduce_send(c, i, ein, 0, 1, 0, place.outer_peer).wait_send()
        return ends

    def gather_send(self, c, i, ev, a, b, peer):
        rows = self.span(c, i, a, b)
        dst = self.out.at[c, rows]
        return self.copy(c, ev, dst, dst, peer)

    def gather_stages(self, i):
        n = self.sizes[i]
        ein, eout = 6 + 2 * i, 7 + 2 * i
        if n == 1:
            return []
        if n == 2:
            def first(c):
                self.gather_send(c, i, eout, 0, 1, self.level(c, i).inner_peer).start()

            def last(c):
                self.gather_send(c, i, eout, 1, 2, self.level(c, i).inner_peer).wait_recv()
            return [first, last]

        def zero(c):
            place = self.level(c, i)

            @pl.when(place.outer == 0)
            def _():
                self.gather_send(c, i, ein, 0, 1, place.inner_peer).start()

        def one(c):
            place = self.level(c, i)

            @pl.when(place.outer == 1)
            def _():
                self.gather_send(c, i, ein, 0, 1, place.outer_peer).wait_recv()
                self.gather_send(c, i, eout, 0, 2, place.inner_peer).start()

        def two(c):
            place = self.level(c, i)

            @pl.when(place.outer == 1)
            def _():
                self.gather_send(c, i, eout, 2, 4, place.inner_peer).wait_recv()
                self.gather_send(c, i, ein, 1, 4, place.outer_peer).start()

        def three(c):
            place = self.level(c, i)

            @pl.when(place.outer == 0)
            def _():
                self.gather_send(c, i, ein, 1, 4, place.inner_peer).wait_recv()
        return [zero, one, two, three]

    def gather_ends(self, i):
        n = self.sizes[i]
        ein, eout = 6 + 2 * i, 7 + 2 * i

        def ends(c):
            place = self.level(c, i)
            if n == 2:
                self.gather_send(c, i, eout, 0, 1, place.inner_peer).wait_send()
            elif n == 4:
                @pl.when(place.outer == 0)
                def _():
                    self.gather_send(c, i, ein, 0, 1, place.inner_peer).wait_send()

                @pl.when(place.outer == 1)
                def _():
                    self.gather_send(c, i, eout, 0, 2, place.inner_peer).wait_send()
                    self.gather_send(c, i, ein, 1, 4, place.outer_peer).wait_send()
        return ends

    def own_copy(self, c):
        start = self.base(c, 3)
        rows = pl.ds(pl.multiple_of(start, 8), self.lens[2])
        return pltpu.make_async_copy(self.grad.at[c, rows], self.out.at[c, rows], self.local.at[c])

    def stages(self):
        groups = [self.reduce_stages(0), self.reduce_stages(1), self.reduce_stages(2)]

        def settle(c):
            self.own_copy(c).start()
            self.own_copy(c).wait()
        groups += [[settle], self.gather_stages(2), self.gather_stages(1), self.gather_stages(0)]
        joined = []
        for group in groups:
            if not group:
                continue
            if joined:
                joined[-1] = joined[-1] + [group[0]]
                joined += [[stage] for stage in group[1:]]
            else:
                joined = [[stage] for stage in group]
        return [functools.partial(run_all, stages) for stages in joined]

    def ends(self, c):
        for i in range(3):
            if self.sizes[i] > 1:
                self.reduce_ends(i)(c)
                self.gather_ends(i)(c)

    def greet(self):
        barrier = pltpu.get_barrier_semaphore()
        count = jnp.int32(0)
        for place in (self.fast, self.mids, self.slow):
            if place.size == 1:
                continue
            pl.semaphore_signal(barrier, inc=1, device_id={"dp": place.inner_peer}, device_id_type=MESH)
            count = count + 1
            if place.size == 4:
                @pl.when(place.outer == 1)
                def _():
                    pl.semaphore_signal(barrier, inc=1, device_id={"dp": place.outer_peer}, device_id_type=MESH)
                count = count + jnp.where(place.outer == 1, 1, 0)
        pl.semaphore_wait(barrier, count)


def run_all(stages, c):
    for stage in stages:
        stage(c)


CHUNK = 384
SIDE = 768


class Makers:
    def __init__(self, lefts, rights):
        self.parts = []
        start = 0
        for left, right in zip(lefts, rights):
            across = right.shape[1] // CHUNK
            number = left.shape[1] // SIDE * across
            self.parts.append((start, number, across, left, right))
            start += number
        self.count = start

    def fetch(self, c, left_buf, right_buf, sems):
        slot = lax.rem(c, 2)
        for start, number, across, left, right in self.parts:
            @pl.when((c >= start) & (c < start + number))
            def _():
                at = c - start
                pltpu.make_async_copy(left.at[:, cols(lax.div(at, across), SIDE)], left_buf.at[slot], sems.at[slot, 0]).start()
                pltpu.make_async_copy(right.at[:, cols(lax.rem(at, across), CHUNK)], right_buf.at[slot], sems.at[slot, 1]).start()

    def wait(self, c, left_buf, right_buf, sems):
        slot = lax.rem(c, 2)
        _, _, _, left, right = self.parts[0]
        pltpu.make_async_copy(left.at[:, cols(0, SIDE)], left_buf.at[slot], sems.at[slot, 0]).wait()
        pltpu.make_async_copy(right.at[:, cols(0, CHUNK)], right_buf.at[slot], sems.at[slot, 1]).wait()


def sum_kernel(dims, rows, lead, h_left, h_right, n_left, n_right, m_left, m_right, q_left, q_right, small_src,
               out, small_out, grad, land, small_grad, small_land, left_buf, right_buf, load, send, recv, local, ssend, srecv, slocal):
    dp = lax.axis_index("dp")
    makers = Makers((h_left, n_left, m_left, q_left), (h_right, n_right, m_right, q_right))
    count = makers.count
    main = Ring(dp, dims, rows, grad, land, out, send, recv, local)
    small = Ring(dp, dims, small_grad.shape[1], small_grad, small_land, small_out, ssend, srecv, slocal)
    makers.fetch(0, left_buf, right_buf, load)
    pltpu.make_async_copy(small_src, small_grad, load.at[2, 0]).start()
    main.greet()
    stages, small_stages = main.stages(), small.stages()
    depth = len(stages)

    def make(c):
        makers.wait(c, left_buf, right_buf, load)
        makers.fetch(c + 1, left_buf, right_buf, load)
        slot = lax.rem(c, 2)
        for j in range(SIDE // GROUP):
            grad[c, j * GROUP : (j + 1) * GROUP] = t_dot(left_buf[slot, :, j * GROUP : (j + 1) * GROUP], right_buf[slot]).astype(BF)
        if rows > SIDE:
            grad[c, SIDE:rows] = jnp.zeros((rows - SIDE, CHUNK), BF)

    @pl.loop(0, count + 1 + lead + depth)
    def _(t):
        for s in reversed(range(depth)):
            c = t - s - (lead if s else 0)

            @pl.when((c >= 0) & (c < count))
            def _():
                if s == 0:
                    make(c)
                stages[s](c)

            @pl.when(c == count)
            def _():
                if s == 0:
                    pltpu.make_async_copy(small_src, small_grad, load.at[2, 0]).wait()
                small_stages[s](0)

    @pl.loop(0, count)
    def _(c):
        main.ends(c)
    small.ends(0)


def sum_grads(pairs, small, n, lead=2, collective_id=0):
    dims = dp_dims(n)
    rows = -(-SIDE // (16 * n)) * 16 * n
    count = sum(left.shape[1] // SIDE * right.shape[1] // CHUNK for left, right in pairs)
    tokens = pairs[0][0].shape[0]
    land, _ = Ring.land_rows(rows, dims)
    small_land, _ = Ring.land_rows(small.shape[1], dims)
    any_space = pl.BlockSpec(memory_space=pl.ANY)
    return pl.pallas_call(
        functools.partial(sum_kernel, dims, rows, lead),
        out_shape=(jax.ShapeDtypeStruct((count, rows, CHUNK), BF), jax.ShapeDtypeStruct(small.shape, small.dtype)),
        in_specs=[any_space] * 9,
        out_specs=(any_space,) * 2,
        scratch_shapes=[
            pltpu.VMEM((count, rows, CHUNK), BF),
            pltpu.VMEM((count, land, CHUNK), BF),
            pltpu.VMEM(small.shape, small.dtype),
            pltpu.VMEM((1, small_land, small.shape[2]), small.dtype),
            pltpu.VMEM((2, tokens, SIDE), BF),
            pltpu.VMEM((2, tokens, CHUNK), BF),
            pltpu.SemaphoreType.DMA((3, 2)),
            pltpu.SemaphoreType.DMA((count, 12)),
            pltpu.SemaphoreType.DMA((count, 12)),
            pltpu.SemaphoreType.DMA((count,)),
            pltpu.SemaphoreType.DMA((1, 12)),
            pltpu.SemaphoreType.DMA((1, 12)),
            pltpu.SemaphoreType.DMA((1,)),
        ],
        compiler_params=pltpu.CompilerParams(collective_id=collective_id, has_side_effects=True, vmem_limit_bytes=63 * 2**20),
    )(*[x for pair in pairs for x in pair], small)


def shifted(x, axis, by):
    count = lax.axis_size(axis)
    pairs = [(i, i + by) for i in range(count) if 0 <= i + by < count]
    return lax.ppermute(x, axis, pairs)


def widen(src, dst):
    dst[...] = src[0].astype(F32)


def from_chunks(done, start, shape):
    rows, columns = shape
    across = columns // CHUNK
    return pl.pallas_call(
        widen,
        grid=(rows // SIDE, across),
        in_specs=[pl.BlockSpec((1, SIDE, CHUNK), lambda r, j: (start + r * across + j, 0, 0))],
        out_specs=pl.BlockSpec((SIDE, CHUNK), lambda r, j: (r, j)),
        out_shape=jax.ShapeDtypeStruct(shape, F32),
    )(done)


def on_device(section_inputs, conv_weight, conv_bias, norm_gain, norm_bias, w_qkv, w_proj, b_proj, w_fc1, b_fc1, w_fc2, b_fc2):
    pipe, n = lax.axis_index("pipe"), lax.axis_size("dp")
    is_first = pipe == 0
    weights = (conv_weight, conv_bias, norm_gain, norm_bias, w_qkv, w_proj, b_proj, w_fc1, b_fc1, w_fc2, b_fc2)
    conv_w, conv_b, gain, shift, wq, wp, bp, w1, b1, w2, b2 = (weight[0] for weight in weights)
    params = (conv_w, conv_b, gain, shift, wq, wp, bp[None], w1, b1[None], w2, b2[None])
    images, _, width = section_inputs.shape[1:]

    def role(first):
        return jnp.stack([is_first.astype(jnp.int32), (is_first == first).astype(jnp.int32)])

    own = jnp.swapaxes(section_inputs[0], 0, 1).reshape(-1, width)
    first_out = forward_block(role(True), own, params, images)
    middle = shifted(first_out[0].astype(BF), "pipe", 1)
    second_out = forward_block(role(False), middle, params, images, first_out)
    x = jnp.where(is_first, own, middle)
    result, one, mid, two, n1, packed, soft, mixed, n2, hidden, slope = second_out
    saved = (one, mid, two, packed, soft, slope)
    back_second = backward_block(role(False), own, middle, saved, params, images)
    received = shifted(back_second[0].astype(BF), "pipe", -1)
    back_first = backward_block(role(True), received, own, saved, params, images, back_second)
    grad_in, grad_packed, grad_att, grad_pre, sums = back_first
    cot = jnp.where(is_first, received, own)
    ends = jnp.where(is_first, grad_in, result).reshape(49, images, width)
    section_ends = jnp.swapaxes(ends, 0, 1)[None]

    lanes = 128
    small = sums[:30].reshape(-1, lanes)
    small = jnp.pad(small, ((0, 16 * n - small.shape[0]), (0, 0)))[None]
    pairs = ((hidden, cot), (n2, grad_pre), (mixed, grad_att), (n1, grad_packed))
    done, small_done = sum_grads(pairs, small, n)
    grads, at = [], 0
    for shape in (w2.shape, w1.shape, wp.shape, wq.shape):
        number = shape[0] // SIDE * shape[1] // CHUNK
        grads.append(from_chunks(done, at, shape)[None])
        at += number
    grad_fc2, grad_fc1, grad_proj, grad_qkv = grads
    sums = small_done.reshape(-1)[: 30 * width].reshape(30, width)
    return (section_ends, sums[:18].reshape(conv_weight.shape), sums[18:20][None], sums[20:22][None], sums[22:24][None],
            grad_qkv, grad_proj, sums[24:25], grad_fc1, sums[25:29].reshape(b_fc1.shape), grad_fc2, sums[29:30])


def solution(mesh):
    return jax.shard_map(
        on_device,
        mesh=mesh,
        in_specs=(
            P("pipe", "dp", None, None),
            P("pipe", None, None, None),
            P("pipe", None, None),
            P("pipe", None, None),
            P("pipe", None, None),
            P("pipe", None, None),
            P("pipe", None, None),
            P("pipe", None),
            P("pipe", None, None),
            P("pipe", None),
            P("pipe", None, None),
            P("pipe", None),
        ),
        out_specs=(
            P("pipe", "dp", None, None),
            P("pipe", None, None, None),
            P("pipe", None, None),
            P("pipe", None, None),
            P("pipe", None, None),
            P("pipe", None, None),
            P("pipe", None, None),
            P("pipe", None),
            P("pipe", None, None),
            P("pipe", None),
            P("pipe", None, None),
            P("pipe", None),
        ),
        check_vma=False,
    )
```

```python
import functools

import jax
import jax.numpy as jnp
from jax import lax
from jax.experimental import pallas as pl
from jax.experimental.pallas import tpu as pltpu
from jax.sharding import PartitionSpec as P

MESH = pl.DeviceIdType.MESH
SIDE = 768
HEAD = 32
GROUP = 256
SLOT = 64
BF = jnp.bfloat16
F32 = jnp.float32


def cols(j, width=GROUP):
    return pl.ds(pl.multiple_of(j * width, width), width)


def dot(a, b):
    return lax.dot_general(a, b, (((1,), (0,)), ((), ())), preferred_element_type=F32)


def dot_t(a, b):
    return lax.dot_general(a, b, (((1,), (1,)), ((), ())), preferred_element_type=F32)


def t_dot(a, b):
    return lax.dot_general(a, b, (((0,), (0,)), ((), ())), preferred_element_type=F32)


def fill_swap(ref, images):
    rows, columns = ref.shape
    block = 128

    @pl.loop(0, rows // block)
    def _(b):
        r = lax.broadcasted_iota(jnp.int32, (block, columns), 0) + b * block
        c = lax.broadcasted_iota(jnp.int32, (block, columns), 1)
        image, position = lax.div(r, SLOT), lax.rem(r, SLOT)
        hit = (c == position * images + image) & (position < 49)
        ref[pl.ds(pl.multiple_of(b * block, block), block), :] = jnp.where(hit, 1.0, 0.0).astype(BF)


def clear_border(pad, images):
    zero = jnp.zeros((9 * images, pad.shape[1]), pad.dtype)
    pad[0 : 9 * images, :] = zero
    pad[72 * images : 81 * images, :] = zero
    one = jnp.zeros((images, pad.shape[1]), pad.dtype)

    @pl.loop(1, 8)
    def _(r):
        pad[pl.ds(pl.multiple_of(r * 9 * images, 16), images), :] = one
        pad[pl.ds(pl.multiple_of((r * 9 + 8) * images, 16), images), :] = one


def inside(r, images):
    return pl.ds(pl.multiple_of(((r + 1) * 9 + 1) * images, 16), 7 * images)


def grid_row(r, images):
    return pl.ds(pl.multiple_of(r * 7 * images, 16), 7 * images)


def encode(pad, kernel, bias, out, images):
    @pl.loop(0, pad.shape[1] // 128)
    def _(lane):
        ls = cols(lane, 128)
        taps = [jnp.broadcast_to(kernel[pl.ds(t, 1), ls], (images, 128)) for t in range(9)]
        shift = jnp.broadcast_to(bias[:, ls], (images, 128))

        @pl.loop(0, 7)
        def _(r):
            for c in range(7):
                total = shift
                for t in range(9):
                    at = pl.multiple_of(((r + t // 3) * 9 + c + t % 3) * images, 16)
                    piece = pad[pl.ds(at, images), ls]
                    total = total + piece * taps[t]
                    if t == 4:
                        total = total + piece
                out[pl.ds(pl.multiple_of((r * 7 + c) * images, 16), images), ls] = total


def normalise(stream, gain, bias, out, images):
    @pl.loop(0, 49, unroll=7)
    def _(p):
        rows = pl.ds(pl.multiple_of(p * images, 16), images)
        s = stream[rows, :]
        centered = s - jnp.mean(s, axis=-1, keepdims=True)
        spread = jnp.mean(centered * centered, axis=-1, keepdims=True)
        out[rows, :] = (centered * lax.rsqrt(spread + 1e-5) * gain[...] + bias[...]).astype(BF)


def head_mask(rows_per, count, lanes):
    shape = (count * rows_per, lanes)
    r = lax.broadcasted_iota(jnp.int32, shape, 0)
    c = lax.broadcasted_iota(jnp.int32, shape, 1)
    return lax.div(r, rows_per) == lax.div(c, HEAD)


def spread_heads(x, mask):
    count = mask.shape[0] // x.shape[0]
    return jnp.where(mask, jnp.concatenate([x] * count, axis=0), jnp.zeros((), x.dtype))


def fold_heads(x, mask, rows_per):
    kept = jnp.where(mask, x, 0.0)
    total = kept[0:rows_per]
    for h in range(1, x.shape[0] // rows_per):
        total = total + kept[h * rows_per : (h + 1) * rows_per]
    return total


def soft_down(scores, valid):
    if valid < scores.shape[0]:
        r = lax.broadcasted_iota(jnp.int32, scores.shape, 0)
        scores = jnp.where(r < valid, scores, -jnp.inf)
    e = jnp.exp(scores - jnp.max(scores, axis=0, keepdims=True))
    return e / jnp.sum(e, axis=0, keepdims=True)


def spatial_forward(packed, mixed, soft, images):
    width = mixed.shape[1]
    groups = width // GROUP

    @pl.loop(0, images, unroll=4)
    def _(i):
        rows = pl.ds(pl.multiple_of(i * SLOT, SLOT), SLOT)
        mask = head_mask(SLOT, GROUP // HEAD, GROUP)
        for g in range(groups):
            q, k, v = (packed[rows, part * width + g * GROUP : part * width + (g + 1) * GROUP] for part in range(3))
            weights = soft_down(dot_t(k, spread_heads(q, mask)), 49).astype(BF)
            soft[i, g] = weights
            mixed[rows, g * GROUP : (g + 1) * GROUP] = fold_heads(t_dot(weights, v), mask, SLOT).astype(BF)


def channel_forward(packed, mixed, soft, images):
    width = mixed.shape[1]

    @pl.loop(0, images, unroll=4)
    def _(i):
        rows = pl.ds(pl.multiple_of(i * SLOT, SLOT), SLOT)
        mask = head_mask(HEAD, 128 // HEAD, 128)
        for g in range(width // 128):
            q, k, v = (packed[rows, part * width + g * 128 : part * width + (g + 1) * 128] for part in range(3))
            weights = soft_down(fold_heads(t_dot(k, q), mask, HEAD), HEAD).astype(BF)
            soft[i, g // 2, g % 2 * HEAD : (g % 2 + 1) * HEAD, 0:128] = weights
            mixed[rows, g * 128 : (g + 1) * 128] = dot(v, spread_heads(weights, mask)).astype(BF)


def gelu_both(x):
    half = 0.5 + 0.5 * lax.erf(x * 0.7071067811865476)
    return x * half, half + x * (0.3989422804014327 * jnp.exp(-0.5 * x * x))


def forward_kernel(images, role, x, conv_w, conv_b, gain, shift, b_proj, b_fc1, b_fc2,
                   w_qkv, w_proj, w_fc1, w_fc2, *refs):
    earlier = len(refs) - 32
    (result, o_one, o_mid, o_two, o_n1, o_packed, o_soft, o_mixed, o_n2, o_hidden, o_slope,
     v_qkv, v_proj, v_fc1, v_fc2, pad, one, mid, two, n1, swap, n1s, packed, soft, mixed_s, mixed,
     n2, hidden, slope, end, load, store) = refs[earlier:]
    rows = 49 * images
    width = x.shape[1]
    loads = [pltpu.make_async_copy(src, dst, load.at[at]) for at, (src, dst) in enumerate(
        ((w_qkv, v_qkv), (w_proj, v_proj), (w_fc1, v_fc1), (w_fc2, v_fc2)))]
    stores = [pltpu.make_async_copy(src, dst, store.at[at]) for at, (src, dst) in enumerate(
        ((one, o_one), (mid, o_mid), (two, o_two), (n1, o_n1), (packed, o_packed), (soft, o_soft),
         (mixed, o_mixed), (n2, o_n2), (hidden, o_hidden), (slope, o_slope), (end, result)))]

    @pl.when(role[1] == 1)
    def _():
        for copy in loads:
            copy.start()
        fill_swap(swap, images)
        clear_border(pad, images)

        @pl.loop(0, 7)
        def _(r):
            pad[inside(r, images), :] = x[grid_row(r, images), :].astype(F32)
        encode(pad, conv_w.at[0], conv_b.at[pl.ds(0, 1)], one, images)
        stores[0].start()
        normalise(one, gain.at[pl.ds(0, 1)], shift.at[pl.ds(0, 1)], n1, images)
        stores[3].start()

        @pl.loop(0, width // GROUP)
        def _(j):
            n1s[:, cols(j)] = dot(swap[...], n1[:, cols(j)]).astype(BF)
        loads[0].wait()

        @pl.loop(0, 3 * width // GROUP)
        def _(j):
            scale = jnp.where(j < width // GROUP, HEAD ** -0.5, 1.0)
            packed[:, cols(j)] = (dot(n1s[...], v_qkv[:, cols(j)]) * scale).astype(BF)
        stores[4].start()

        @pl.when(role[0] == 1)
        def _():
            spatial_forward(packed, mixed_s, soft, images)

        @pl.when(role[0] == 0)
        def _():
            channel_forward(packed, mixed_s, soft, images)
        stores[5].start()

        @pl.loop(0, width // GROUP)
        def _(j):
            mixed[:, cols(j)] = t_dot(swap[...], mixed_s[:, cols(j)]).astype(BF)
        stores[6].start()
        loads[1].wait()

        @pl.loop(0, width // GROUP)
        def _(j):
            mid[:, cols(j)] = one[:, cols(j)] + dot(mixed[...], v_proj[:, cols(j)]) + b_proj[:, cols(j)]
        stores[1].start()

        @pl.loop(0, 7)
        def _(r):
            pad[inside(r, images), :] = mid[grid_row(r, images), :]
        encode(pad, conv_w.at[1], conv_b.at[pl.ds(1, 1)], two, images)
        stores[2].start()
        normalise(two, gain.at[pl.ds(1, 1)], shift.at[pl.ds(1, 1)], n2, images)
        stores[7].start()
        loads[2].wait()

        @pl.loop(0, v_fc1.shape[1] // GROUP)
        def _(j):
            pre = dot(n2[...], v_fc1[:, cols(j)]) + b_fc1[:, cols(j)]
            value, rate = gelu_both(pre)
            hidden[:, cols(j)] = value.astype(BF)
            slope[:, cols(j)] = rate.astype(BF)
        stores[8].start()
        stores[9].start()
        loads[3].wait()

        @pl.loop(0, width // GROUP)
        def _(j):
            end[:, cols(j)] = two[:, cols(j)] + dot(hidden[...], v_fc2[:, cols(j)]) + b_fc2[:, cols(j)]
        stores[10].start()
        for copy in stores:
            copy.wait()


def forward_block(role, x, params, images, earlier=()):
    conv_w, conv_b, gain, shift, w_qkv, w_proj, b_proj, w_fc1, b_fc1, w_fc2, b_fc2 = params
    rows, width = x.shape
    wide = w_fc1.shape[1]
    slots = images * SLOT
    any_space = pl.BlockSpec(memory_space=pl.ANY)
    vmem = pl.BlockSpec(memory_space=pltpu.VMEM)
    outs = [((rows, width), F32), ((rows, width), F32), ((rows, width), F32), ((rows, width), F32),
            ((rows, width), BF), ((slots, 3 * width), BF), ((images, width // GROUP, SLOT, 2 * GROUP), BF),
            ((rows, width), BF), ((rows, width), BF), ((rows, wide), BF), ((rows, wide), BF)]
    scratch = [w_qkv, w_proj, w_fc1, w_fc2]
    return pl.pallas_call(
        functools.partial(forward_kernel, images),
        out_shape=[jax.ShapeDtypeStruct(*o) for o in outs],
        in_specs=[pl.BlockSpec(memory_space=pltpu.SMEM)] + [vmem] * 8 + [any_space] * (4 + len(earlier)),
        out_specs=[any_space] * len(outs),
        input_output_aliases={13 + at: at for at in range(len(earlier))},
        scratch_shapes=[pltpu.VMEM(w.shape, w.dtype) for w in scratch] + [
            pltpu.VMEM((81 * images, width), F32),
            pltpu.VMEM((rows, width), F32), pltpu.VMEM((rows, width), F32), pltpu.VMEM((rows, width), F32),
            pltpu.VMEM((rows, width), BF), pltpu.VMEM((slots, rows), BF), pltpu.VMEM((slots, width), BF),
            pltpu.VMEM((slots, 3 * width), BF), pltpu.VMEM((images, width // GROUP, SLOT, 2 * GROUP), BF),
            pltpu.VMEM((slots, width), BF), pltpu.VMEM((rows, width), BF), pltpu.VMEM((rows, width), BF),
            pltpu.VMEM((rows, wide), BF), pltpu.VMEM((rows, wide), BF), pltpu.VMEM((rows, width), F32),
            pltpu.SemaphoreType.DMA((4,)), pltpu.SemaphoreType.DMA((11,)),
        ],
        compiler_params=pltpu.CompilerParams(vmem_limit_bytes=62 * 2**20),
    )(role, x, conv_w, conv_b, gain, shift, b_proj, b_fc1, b_fc2, w_qkv, w_proj, w_fc1, w_fc2, *earlier)


def dp_dims(n):
    sizes = [1, 1, 1]
    at = 0
    left = n
    while left > 1:
        factor = 2 if left % 2 == 0 else left
        sizes[at % 3] *= factor
        left //= factor
        at += 1
    return tuple(sizes), (sizes[1] * sizes[2], sizes[2], 1)


class Place:
    def __init__(self, dp, size, stride):
        self.size = size
        pos = lax.rem(lax.div(dp, stride), size)
        low = pos < (size + 1) // 2
        self.outer = jnp.where(low, pos, size - 1 - pos)
        self.pos = pos
        self.low = low
        step = jnp.where(low, stride, -stride)
        self.inner_peer = dp + step
        self.outer_peer = dp - step


def pick(flag, a, b):
    out = object.__new__(Place)
    out.size = a.size
    for name in ("pos", "low", "outer", "inner_peer", "outer_peer"):
        setattr(out, name, jnp.where(flag, getattr(a, name), getattr(b, name)))
    return out


class Ring:
    def __init__(self, dp, dims, rows, grad, land, out, out_at, send, recv, local):
        (s0, s1, s2), (t0, t1, t2) = dims
        self.mids = Place(dp, s0, t0)
        self.fast, self.slow = Place(dp, s2, t2), Place(dp, s1, t1)
        self.grad, self.land, self.out, self.out_at = grad, land, out, out_at
        self.grads, self.lands = grad.shape[0], land.shape[0]
        self.send, self.recv, self.local = send, recv, local
        self.sizes, self.lens, self.starts, _ = Ring.shape(rows, dims)

    @staticmethod
    def shape(rows, dims):
        s0, s1, s2 = dims[0]
        sizes = (s2, s0, s1)
        lens = (rows // s2, rows // s2 // s0, rows // (s0 * s1 * s2))
        total, starts = 0, []
        for n, length in zip(sizes, lens):
            starts.append(total)
            total += length * (1 if n == 2 else 5)
        return sizes, lens, starts, total

    def level(self, c, i):
        flag = lax.rem(c, 2) == 0
        if i == 1:
            return self.mids
        return pick(flag, self.fast, self.slow) if i == 0 else pick(flag, self.slow, self.fast)

    def base(self, c, i):
        start = 0
        for j in range(i):
            start = start + self.level(c, j).pos * self.lens[j]
        return start

    def span(self, c, i, a, b):
        place, length, n = self.level(c, i), self.lens[i], self.sizes[i]
        start = self.base(c, i) + jnp.where(place.low, a * length, (n - b) * length)
        return pl.ds(pl.multiple_of(start, 8), (b - a) * length)

    def mine(self, c, rows):
        return self.grad.at[lax.rem(c, self.grads), rows]

    def landing(self, c, i, at, length):
        return self.land.at[lax.rem(c, self.lands), pl.ds(self.starts[i] + at, length)]

    def copy(self, c, ev, src, dst, peer):
        return pltpu.make_async_remote_copy(
            src_ref=src, dst_ref=dst, send_sem=self.send.at[c, ev], recv_sem=self.recv.at[c, ev],
            device_id={"dp": peer}, device_id_type=MESH)

    def add(self, c, i, a, b, at):
        rows = self.span(c, i, a, b)
        slot = lax.rem(c, self.grads)
        got = self.landing(c, i, at, (b - a) * self.lens[i])
        self.grad[slot, rows] = self.grad[slot, rows] + got[...]

    def give(self, c, i, ev, a, b, at, peer):
        return self.copy(c, ev, self.mine(c, self.span(c, i, a, b)), self.landing(c, i, at, (b - a) * self.lens[i]), peer)

    def reduce_stages(self, i):
        n, length = self.sizes[i], self.lens[i]
        ein, eout = 2 * i, 2 * i + 1
        if n == 1:
            return []
        if n == 2:
            def first(c):
                self.give(c, i, eout, 1, 2, 0, self.level(c, i).inner_peer).start()

            def last(c):
                self.give(c, i, eout, 0, 1, 0, self.level(c, i).inner_peer).wait_recv()
                self.add(c, i, 0, 1, 0)
            return [first, last]

        def zero(c):
            place = self.level(c, i)

            @pl.when(place.outer == 0)
            def _():
                self.give(c, i, ein, 1, 4, 0, place.inner_peer).start()

        def one(c):
            place = self.level(c, i)

            @pl.when(place.outer == 1)
            def _():
                self.give(c, i, ein, 1, 4, 0, place.inner_peer).wait_recv()
                self.add(c, i, 2, 4, jnp.where(place.low, length, 0))
                self.give(c, i, eout, 2, 4, 3 * length, place.inner_peer).start()
                self.add(c, i, 1, 2, jnp.where(place.low, 0, 2 * length))

        def two(c):
            place = self.level(c, i)

            @pl.when(place.outer == 1)
            def _():
                self.give(c, i, eout, 0, 2, 3 * length, place.inner_peer).wait_recv()
                self.add(c, i, 0, 2, 3 * length)
                self.give(c, i, ein, 0, 1, 3 * length, place.outer_peer).start()

        def three(c):
            place = self.level(c, i)

            @pl.when(place.outer == 0)
            def _():
                self.give(c, i, ein, 0, 1, 3 * length, place.inner_peer).wait_recv()
                self.add(c, i, 0, 1, 3 * length)
        return [zero, one, two, three]

    def reduce_ends(self, c):
        for i in range(3):
            n, place = self.sizes[i], self.level(c, i)
            ein, eout = 2 * i, 2 * i + 1
            if n == 2:
                self.give(c, i, eout, 1, 2, 0, place.inner_peer).wait_send()
            elif n == 4:
                @pl.when(place.outer == 0)
                def _():
                    self.give(c, i, ein, 1, 4, 0, place.inner_peer).wait_send()

                @pl.when(place.outer == 1)
                def _():
                    self.give(c, i, eout, 2, 4, 0, place.inner_peer).wait_send()
                    self.give(c, i, ein, 0, 1, 0, place.outer_peer).wait_send()

    def spread(self, c, i, ev, a, b, peer):
        dst = self.out.at[self.out_at(c), self.span(c, i, a, b)]
        return self.copy(c, ev, dst, dst, peer)

    def gather_stages(self, i):
        n = self.sizes[i]
        ein, eout = 6 + 2 * i, 7 + 2 * i
        if n == 1:
            return []
        if n == 2:
            def first(c):
                self.spread(c, i, eout, 0, 1, self.level(c, i).inner_peer).start()

            def last(c):
                self.spread(c, i, eout, 1, 2, self.level(c, i).inner_peer).wait_recv()
            return [first, last]

        def zero(c):
            place = self.level(c, i)

            @pl.when(place.outer == 0)
            def _():
                self.spread(c, i, ein, 0, 1, place.inner_peer).start()

        def one(c):
            place = self.level(c, i)

            @pl.when(place.outer == 1)
            def _():
                self.spread(c, i, ein, 0, 1, place.outer_peer).wait_recv()
                self.spread(c, i, eout, 0, 2, place.inner_peer).start()

        def two(c):
            place = self.level(c, i)

            @pl.when(place.outer == 1)
            def _():
                self.spread(c, i, eout, 2, 4, place.inner_peer).wait_recv()
                self.spread(c, i, ein, 1, 4, place.outer_peer).start()

        def three(c):
            place = self.level(c, i)

            @pl.when(place.outer == 0)
            def _():
                self.spread(c, i, ein, 1, 4, place.inner_peer).wait_recv()
        return [zero, one, two, three]

    def gather_ends(self, c):
        for i in range(3):
            n, place = self.sizes[i], self.level(c, i)
            ein, eout = 6 + 2 * i, 7 + 2 * i
            if n == 2:
                self.spread(c, i, eout, 0, 1, place.inner_peer).wait_send()
            elif n == 4:
                @pl.when(place.outer == 0)
                def _():
                    self.spread(c, i, ein, 0, 1, place.inner_peer).wait_send()

                @pl.when(place.outer == 1)
                def _():
                    self.spread(c, i, eout, 0, 2, place.inner_peer).wait_send()
                    self.spread(c, i, ein, 1, 4, place.outer_peer).wait_send()

    def settle(self, c):
        rows = pl.ds(pl.multiple_of(self.base(c, 3), 8), self.lens[2])
        copy = pltpu.make_async_copy(self.mine(c, rows), self.out.at[self.out_at(c), rows], self.local)
        copy.start()
        copy.wait()

    def stages(self, first, last):
        groups = [self.reduce_stages(0), self.reduce_stages(1), self.reduce_stages(2), [self.settle],
                  self.gather_stages(2), self.gather_stages(1), self.gather_stages(0), [last]]
        joined = [[first]]
        for group in groups:
            if group:
                joined[-1].append(group[0])
                joined += [[stage] for stage in group[1:]]
        return [functools.partial(run_all, stages) for stages in joined]

    def greet(self):
        barrier = pltpu.get_barrier_semaphore()
        pl.semaphore_signal(barrier, inc=1, device_id={"pipe": 1 - lax.axis_index("pipe")}, device_id_type=MESH)
        count = jnp.int32(1)
        for place in (self.fast, self.mids, self.slow):
            if place.size == 1:
                continue
            pl.semaphore_signal(barrier, inc=1, device_id={"dp": place.inner_peer}, device_id_type=MESH)
            count = count + 1
            if place.size == 4:
                @pl.when(place.outer == 1)
                def _():
                    pl.semaphore_signal(barrier, inc=1, device_id={"dp": place.outer_peer}, device_id_type=MESH)
                count = count + jnp.where(place.outer == 1, 1, 0)
        pl.semaphore_wait(barrier, count)


def run_all(stages, c):
    for stage in stages:
        stage(c)


def encode_back(gpad, given, kernel, out, put, first_row, bias_row, images):
    @pl.loop(0, gpad.shape[1] // 128)
    def _(lane):
        ls = cols(lane, 128)
        taps = [jnp.broadcast_to(kernel[pl.ds(8 - t, 1), ls], (images, 128)) for t in range(9)]

        def row(r, totals):
            totals = list(totals)
            for c in range(7):
                at = pl.ds(pl.multiple_of((r * 7 + c) * images, 16), images)
                source = given[at, ls].astype(F32)
                total = None
                for t in range(9):
                    near = pl.ds(pl.multiple_of(((r + t // 3) * 9 + c + t % 3) * images, 16), images)
                    piece = gpad[near, ls]
                    if t == 4:
                        totals[9] = totals[9] + piece
                        total = total + piece
                    total = piece * taps[t] if total is None else total + piece * taps[t]
                    totals[8 - t] = totals[8 - t] + source * piece
                out[at, ls] = total
            return tuple(totals)
        totals = lax.fori_loop(0, 7, row, (jnp.zeros((images, 128), F32),) * 10)
        for t in range(9):
            put(first_row + t, lane, jnp.sum(totals[t], axis=0, keepdims=True))
        put(bias_row, lane, jnp.sum(totals[9], axis=0, keepdims=True))


def normalise_back(stream, grad, base, gain, gpad, put, gain_row, shift_row, acc, images):
    acc[...] = jnp.zeros_like(acc)

    @pl.loop(0, 49, unroll=7)
    def _(p):
        rows = pl.ds(pl.multiple_of(p * images, 16), images)
        s, dy = stream[rows, :], grad[rows, :]
        centered = s - jnp.mean(s, axis=-1, keepdims=True)
        rate = lax.rsqrt(jnp.mean(centered * centered, axis=-1, keepdims=True) + 1e-5)
        unit = centered * rate
        acc[0] += dy * unit
        acc[1] += dy
        dg = dy * gain[...]
        m1 = jnp.mean(dg, axis=-1, keepdims=True)
        m2 = jnp.mean(dg * unit, axis=-1, keepdims=True)
        at = ((lax.div(p, 7) + 1) * 9 + lax.rem(p, 7) + 1) * images
        gpad[pl.ds(pl.multiple_of(at, 16), images), :] = base[rows, :].astype(F32) + rate * (dg - m1 - unit * m2)
    for row, total in ((gain_row, acc[0]), (shift_row, acc[1])):
        total = jnp.sum(total, axis=0, keepdims=True)
        for lane in range(total.shape[1] // 128):
            put(row, lane, total[:, lane * 128 : (lane + 1) * 128])


def spatial_backward(packed, grad_mixed, soft, images):
    width = grad_mixed.shape[1]

    @pl.loop(0, images)
    def _(i):
        rows = pl.ds(pl.multiple_of(i * SLOT, SLOT), SLOT)
        mask = head_mask(SLOT, GROUP // HEAD, GROUP)
        made = []
        for g in range(width // GROUP):
            at = [slice(part * width + g * GROUP, part * width + (g + 1) * GROUP) for part in range(3)]
            made.append((at, [packed[rows, a] for a in at], soft[i, g], grad_mixed[rows, g * GROUP : (g + 1) * GROUP]))
        ready = []
        for at, (q, k, v), weights, do in made:
            out_spread = spread_heads(do, mask)
            w = weights.astype(F32)
            dw = dot_t(v, out_spread)
            ds = (w * (dw - jnp.sum(dw * w, axis=0, keepdims=True))).astype(BF)
            dq = (fold_heads(t_dot(ds, k), mask, SLOT) * HEAD ** -0.5).astype(BF)
            ready += zip(at, (dq, dot(ds, spread_heads(q, mask)).astype(BF), dot(weights, out_spread).astype(BF)))
        for at, value in ready:
            packed[rows, at] = value


def channel_backward(packed, grad_mixed, soft, images):
    width = grad_mixed.shape[1]

    @pl.loop(0, images)
    def _(i):
        rows = pl.ds(pl.multiple_of(i * SLOT, SLOT), SLOT)
        mask = head_mask(HEAD, 128 // HEAD, 128)
        made = []
        for g in range(width // 128):
            at = [slice(part * width + g * 128, part * width + (g + 1) * 128) for part in range(3)]
            weights = soft[i, g // 2, g % 2 * HEAD : (g % 2 + 1) * HEAD, 0:128]
            made.append((at, [packed[rows, a] for a in at], weights, grad_mixed[rows, g * 128 : (g + 1) * 128]))
        ready = []
        for at, (q, k, v), weights, do in made:
            w = weights.astype(F32)
            dw = fold_heads(t_dot(v, do), mask, HEAD)
            ds = spread_heads((w * (dw - jnp.sum(dw * w, axis=0, keepdims=True))).astype(BF), mask)
            dq = (dot(k, ds) * HEAD ** -0.5).astype(BF)
            ready += zip(at, (dq, dot_t(q, ds).astype(BF), dot_t(do, spread_heads(weights, mask)).astype(BF)))
        for at, value in ready:
            packed[rows, at] = value


class Plan:
    def __init__(self, width, wide, n):
        self.chunk = 384 if n <= 16 else 128
        per = width // self.chunk
        self.fc2, self.fc1 = wide // SIDE * per, wide // self.chunk
        self.proj, self.qkv = per, 3 * per
        self.total = self.fc2 + self.fc1 + self.proj + self.qkv
        self.lent = self.fc2 + self.fc1 // 2
        self.taken = self.fc2 + self.fc1
        self.count = (self.lent + self.proj + self.qkv, self.total - self.lent + self.taken)
        self.slots = self.total + self.taken
        self.most = max(self.count)

    def where(self, first, c):
        theirs = jnp.where(first, c < self.lent, c >= self.total - self.lent)
        number = jnp.where(first, jnp.where(theirs, c, c - self.lent + self.taken),
                           jnp.where(theirs, c - (self.total - self.lent), c + self.lent))
        return theirs, number

    def out_at(self, first, c):
        theirs, number = self.where(first, c)
        return jnp.where(theirs, self.total + number, number)


def back_kernel(images, dims, rows, lags, early, plan,
                own, x, conv_w, gain, w_qkv, w_proj, w_fc1, w_fc2, one, mid, two, h_packed, h_soft, h_slope, hidden, n2, mixed, n1,
                o_grad, out, small_out, g_packed, g_att, g_pre, x_hidden, x_n2, x_cot, x_pre,
                v_a, v_fc1, gpad, stream, packed, soft, slope, swap, gm_s, gn, gmid, gatt, cot, acc, small_grad,
                grad, land, small_land, left_buf, right_buf,
                load, store, push_send, push_recv, fetch_sem, send, recv, local, ssend, srecv, slocal, bring_send, bring_recv):
    pipe, dp = lax.axis_index("pipe"), lax.axis_index("dp")
    first = pipe == 0
    width, wide = x.shape[1], w_fc1.shape[1]
    chunk = plan.chunk
    rank = width // GROUP
    main = Ring(dp, dims, rows, grad, land, out, functools.partial(plan.out_at, first), send, recv, local)
    small = Ring(dp, dims, small_grad.shape[1], small_grad, small_land, small_out, lambda c: 0, ssend, srecv, slocal)
    count = jnp.where(first, plan.count[0], plan.count[1])
    opening = jnp.where(first, plan.lent, 0)

    def to_core(at, src, dst):
        return pltpu.make_async_remote_copy(src_ref=src, dst_ref=dst, send_sem=push_send.at[at], recv_sem=push_recv.at[at],
                                            device_id={"pipe": 1 - pipe}, device_id_type=MESH)
    blocks = wide // SIDE
    push_hidden = [to_core(k, hidden.at[:, pl.ds(k * SIDE, SIDE)], x_hidden.at[:, pl.ds(k * SIDE, SIDE)]) for k in range(blocks)]
    push_n2 = to_core(blocks, n2, x_n2)
    push_pre = to_core(blocks + 1, slope, x_pre)
    push_cot = to_core(blocks + 2, own, x_cot)
    push_grad = to_core(blocks + 3, gatt, cot)

    def get(c, left, right):
        slot = lax.rem(c, 2)
        pltpu.make_async_copy(left, left_buf.at[slot], fetch_sem.at[slot, 0]).start()
        pltpu.make_async_copy(right, right_buf.at[slot], fetch_sem.at[slot, 1]).start()

    def fetch(c):
        theirs, number = plan.where(first, c)
        per = width // chunk
        at2, at1 = number, number - plan.fc2
        at_p, at_q = number - plan.taken, number - plan.taken - plan.proj

        @pl.when(theirs & (at1 < 0))
        def _():
            for k in range(blocks):
                @pl.when(at2 == k * per)
                def _():
                    push_hidden[k].wait_recv()

            @pl.when((at2 == 0) & first)
            def _():
                push_cot.wait_recv()
            get(c, x_hidden.at[:, cols(lax.div(at2, per), SIDE)], x_cot.at[:, cols(lax.rem(at2, per), chunk)])

        @pl.when(theirs & (at1 >= 0))
        def _():
            @pl.when(at1 == 0)
            def _():
                push_n2.wait_recv()
                push_pre.wait_recv()
            get(c, x_n2, x_pre.at[:, cols(at1, chunk)])

        @pl.when(jnp.logical_not(theirs) & (at_p < 0))
        def _():
            get(c, n2, g_pre.at[:, cols(at1, chunk)])

        @pl.when(jnp.logical_not(theirs) & (at_p >= 0) & (at_q < 0))
        def _():
            get(c, mixed, g_att.at[:, cols(at_p, chunk)])

        @pl.when(jnp.logical_not(theirs) & (at_q >= 0))
        def _():
            get(c, n1, g_packed.at[:, cols(at_q, chunk)])

    def make(end, c):
        slot = lax.rem(c, 2)
        pltpu.make_async_copy(n2, left_buf.at[slot], fetch_sem.at[slot, 0]).wait()
        pltpu.make_async_copy(n2.at[:, pl.ds(0, chunk)], right_buf.at[slot], fetch_sem.at[slot, 1]).wait()

        @pl.when(c + 1 < end)
        def _():
            fetch(c + 1)

        @pl.when(c >= main.grads)
        def _():
            main.reduce_ends(c - main.grads)
        place = lax.rem(c, main.grads)
        for j in range(SIDE // GROUP):
            part = slice(j * GROUP, (j + 1) * GROUP)
            grad[place, part] = t_dot(left_buf[slot, :, part], right_buf[slot]).astype(BF)
        if rows > SIDE:
            grad[place, SIDE:rows] = jnp.zeros((rows - SIDE, chunk), BF)

    def bring(c):
        _, number = plan.where(first, c)
        return pltpu.make_async_remote_copy(
            src_ref=out.at[plan.out_at(first, c)], dst_ref=out.at[number], send_sem=bring_send.at[number], recv_sem=bring_recv.at[number],
            device_id={"pipe": 1 - pipe}, device_id_type=MESH)

    def hand_over(c):
        @pl.when(plan.where(first, c)[0])
        def _():
            bring(c).start()

    def tick(t, start, end, with_small):
        stages = main.stages(functools.partial(make, end), hand_over)
        small_stages = small.stages(lambda c: None, lambda c: None)
        for s in reversed(range(len(stages))):
            c = t - lags[s]

            @pl.when((c >= start) & (c < end))
            def _():
                stages[s](c)
            if with_small:
                @pl.when(c == end)
                def _():
                    small_stages[s](0)

    def put(row, lane, value):
        small_grad[0, pl.ds(lane * 32 + row, 1), :] = value

    main.greet()
    for copy in push_hidden:
        copy.start()
    push_n2.start()
    load_cot = pltpu.make_async_copy(own, cot, load.at[10])

    @pl.when(jnp.logical_not(first))
    def _():
        push_cot.start()
        load_cot.start()
    v_qkv = [(w_qkv.at[:, pl.ds(part * width, width)], v_a.at[pl.ds(part * width, width)]) for part in range(3)]
    loads = {at: pltpu.make_async_copy(src, dst, load.at[at]) for at, (src, dst) in enumerate(
        [(w_fc2, v_a), (h_slope, slope), (w_fc1, v_fc1), (two, stream), (mid, gmid), (h_soft, soft), (h_packed, packed)]
        + v_qkv)}
    load_proj = pltpu.make_async_copy(w_proj, v_a.at[pl.ds(3 * width, width)], load.at[11])
    load_one = pltpu.make_async_copy(one, stream, load.at[12])
    for at in range(7):
        loads[at].start()
    fill_swap(swap, images)
    clear_border(gpad, images)
    small_grad[...] = jnp.zeros_like(small_grad)

    @pl.when(first)
    def _():
        fetch(0)

        @pl.loop(0, plan.lent + early)
        def _(t):
            tick(t, 0, plan.lent, False)
        push_grad.wait_recv()

    @pl.when(jnp.logical_not(first))
    def _():
        load_cot.wait()
    loads[0].wait()
    loads[1].wait()
    steps = wide // GROUP
    left_over = lags[-1] + 1 - early
    each = -(-left_over // steps)

    @pl.loop(0, steps)
    def _(j):
        if each > 0:
            @pl.when(first)
            def _():
                @pl.loop(0, each)
                def _(k):
                    tick(plan.lent + early + j * each + k, 0, plan.lent, False)
        pre = dot_t(cot[...], v_a[cols(j), :]) * slope[:, cols(j)].astype(F32)
        slope[:, cols(j)] = pre.astype(BF)
        total = jnp.sum(pre, axis=0, keepdims=True)
        for half in range(GROUP // 128):
            at = j * (GROUP // 128) + half
            put(25 + lax.div(at, width // 128), lax.rem(at, width // 128), total[:, half * 128 : (half + 1) * 128])
    push_pre.start()
    store_pre = pltpu.make_async_copy(slope, g_pre, store.at[0])
    store_pre.start()
    for at in range(7, 10):
        loads[at].start()
    load_proj.start()
    for lane in range(width // 128):
        put(29, lane, jnp.sum(cot[:, lane * 128 : (lane + 1) * 128].astype(F32), axis=0, keepdims=True))
    loads[2].wait()

    @pl.loop(0, rank)
    def _(j):
        gn[:, cols(j)] = dot_t(slope[...], v_fc1[cols(j), :])
    loads[3].wait()
    normalise_back(stream, gn, cot, gain.at[pl.ds(1, 1)], gpad, put, 21, 23, acc, images)
    load_one.start()
    loads[4].wait()
    encode_back(gpad, gmid, conv_w.at[1], gmid, put, 9, 19, images)
    for lane in range(width // 128):
        part = gmid[:, lane * 128 : (lane + 1) * 128]
        put(24, lane, jnp.sum(part, axis=0, keepdims=True))
        gatt[:, lane * 128 : (lane + 1) * 128] = part.astype(BF)
    store_att = pltpu.make_async_copy(gatt, g_att, store.at[1])
    store_att.start()
    push_pre.wait_send()
    store_pre.wait()
    load_proj.wait()

    @pl.loop(0, rank)
    def _(j):
        at = pl.ds(pl.multiple_of(3 * width + j * GROUP, GROUP), GROUP)
        slope[:, cols(j)] = dot_t(gatt[...], v_a[at, :]).astype(BF)

    @pl.loop(0, rank)
    def _(j):
        gm_s[:, cols(j)] = dot(swap[...], slope[:, cols(j)]).astype(BF)
    loads[5].wait()
    loads[6].wait()

    @pl.when(first)
    def _():
        spatial_backward(packed, gm_s, soft, images)

    @pl.when(jnp.logical_not(first))
    def _():
        channel_backward(packed, gm_s, soft, images)

    @pl.loop(0, 3 * rank)
    def _(j):
        slope[:, cols(j)] = t_dot(swap[...], packed[:, cols(j)]).astype(BF)
    grad_packed = slope.at[:, pl.ds(0, 3 * width)]
    store_packed = pltpu.make_async_copy(grad_packed, g_packed, store.at[2])
    store_packed.start()
    for at in range(7, 10):
        loads[at].wait()

    @pl.loop(0, rank)
    def _(j):
        w = jnp.concatenate([v_a[pl.ds(pl.multiple_of(part * width + j * GROUP, GROUP), GROUP), :] for part in range(3)], axis=1)
        gn[:, cols(j)] = dot_t(slope[:, 0 : 3 * width], w)
    load_one.wait()
    normalise_back(stream, gn, gmid, gain.at[pl.ds(0, 1)], gpad, put, 20, 22, acc, images)
    encode_back(gpad, x, conv_w.at[0], gmid, put, 0, 18, images)
    store_att.wait()
    store_packed.wait()
    store_grad = pltpu.make_async_copy(gmid, o_grad, store.at[3])
    store_grad.start()

    @pl.when(jnp.logical_not(first))
    def _():
        gatt[...] = gmid[...].astype(BF)
        push_grad.start()
        keep = pltpu.make_async_copy(gatt, x_cot, store.at[4])
        keep.start()
        keep.wait()

    fetch(opening)

    @pl.loop(opening, count + 1 + lags[-1])
    def _(t):
        tick(t, opening, count, True)

    @pl.loop(jnp.maximum(count - main.grads, 0), count)
    def _(c):
        main.reduce_ends(c)

    @pl.loop(0, count)
    def _(c):
        main.gather_ends(c)

        @pl.when(plan.where(first, c)[0])
        def _():
            bring(c).wait_send()
    small.reduce_ends(0)
    small.gather_ends(0)
    for copy in push_hidden:
        copy.wait_send()
    push_n2.wait_send()
    store_grad.wait()

    @pl.when(jnp.logical_not(first))
    def _():
        push_cot.wait_send()
        push_grad.wait_send()

    @pl.loop(0, jnp.where(first, plan.taken, plan.lent))
    def _(k):
        pltpu.make_async_remote_copy(
            src_ref=out.at[k], dst_ref=out.at[k], send_sem=bring_send.at[k], recv_sem=bring_recv.at[k],
            device_id={"pipe": 1 - pipe}, device_id_type=MESH).wait_recv()


def backward(own, x, saved, params, images, n, early=12, collective_id=0):
    conv_w, conv_b, gain, shift, w_qkv, w_proj, b_proj, w_fc1, b_fc1, w_fc2, b_fc2 = params
    one, mid, two, n1, packed, soft, mixed, n2, hidden, slope = saved
    tokens, width = x.shape
    wide = w_fc1.shape[1]
    slots = images * SLOT
    dims = dp_dims(n)
    plan = Plan(width, wide, n)
    rows = -(-SIDE // (16 * n)) * 16 * n
    small_rows = 16 * n
    _, _, _, land = Ring.shape(rows, dims)
    _, _, _, small_land = Ring.shape(small_rows, dims)
    hops = sum(0 if s == 1 else 1 if s == 2 else 3 for s in dims[0])
    gaps = [3] + [2] * (2 * hops - 2) + [3]
    lags = [sum(gaps[:s]) for s in range(2 * hops + 1)]
    grads, lands = lags[hops] + 3, 2 * gaps[0] + 4
    lands += lands % 2
    any_space = pl.BlockSpec(memory_space=pl.ANY)
    vmem = pl.BlockSpec(memory_space=pltpu.VMEM)
    outs = [((tokens, width), F32), ((plan.slots, rows, plan.chunk), BF), ((1, small_rows, 128), F32),
            ((tokens, 3 * width), BF), ((tokens, width), BF), ((tokens, wide), BF),
            ((tokens, wide), BF), ((tokens, width), BF), ((tokens, width), BF), ((tokens, wide), BF)]
    dma = pltpu.SemaphoreType.DMA
    results = pl.pallas_call(
        functools.partial(back_kernel, images, dims, rows, lags, early, plan),
        out_shape=[jax.ShapeDtypeStruct(*o) for o in outs],
        in_specs=[any_space] + [vmem] * 3 + [any_space] * 14,
        out_specs=[any_space] * len(outs),
        scratch_shapes=[
            pltpu.VMEM(w_fc2.shape, BF), pltpu.VMEM(w_fc1.shape, BF), pltpu.VMEM((81 * images, width), F32),
            pltpu.VMEM((tokens, width), F32), pltpu.VMEM(packed.shape, BF), pltpu.VMEM(soft.shape, BF), pltpu.VMEM((tokens, wide), BF),
            pltpu.VMEM((slots, tokens), BF), pltpu.VMEM((slots, width), BF),
            pltpu.VMEM((tokens, width), F32), pltpu.VMEM((tokens, width), F32), pltpu.VMEM((tokens, width), BF), pltpu.VMEM((tokens, width), BF),
            pltpu.VMEM((2, images, width), F32), pltpu.VMEM((1, small_rows, 128), F32),
            pltpu.VMEM((grads, rows, plan.chunk), BF), pltpu.VMEM((lands, land, plan.chunk), BF), pltpu.VMEM((1, small_land, 128), F32),
            pltpu.VMEM((2, tokens, SIDE), BF), pltpu.VMEM((2, tokens, plan.chunk), BF),
            dma((13,)), dma((5,)), dma((wide // SIDE + 4,)), dma((wide // SIDE + 4,)), dma((2, 2)),
            dma((plan.most, 12)), dma((plan.most, 12)), dma, dma((1, 12)), dma((1, 12)), dma, dma((plan.taken,)), dma((plan.taken,)),
        ],
        compiler_params=pltpu.CompilerParams(collective_id=collective_id, has_side_effects=True, vmem_limit_bytes=63 * 2**20),
    )(own, x, conv_w, gain, w_qkv, w_proj, w_fc1, w_fc2, one, mid, two, packed, soft, slope, hidden, n2, mixed, n1)
    return results[0], results[1], results[2], plan


def shifted(x, axis, by):
    count = lax.axis_size(axis)
    pairs = [(i, i + by) for i in range(count) if 0 <= i + by < count]
    return lax.ppermute(x, axis, pairs)


def widen(src, dst):
    dst[...] = src[0].astype(F32)


def from_chunks(done, start, shape):
    rows, columns = shape
    chunk = done.shape[2]
    across = columns // chunk
    return pl.pallas_call(
        widen,
        grid=(rows // SIDE, across),
        in_specs=[pl.BlockSpec((1, SIDE, chunk), lambda r, j: (start + r * across + j, 0, 0))],
        out_specs=pl.BlockSpec((SIDE, chunk), lambda r, j: (r, j)),
        out_shape=jax.ShapeDtypeStruct(shape, F32),
    )(done)


def on_device(section_inputs, conv_weight, conv_bias, norm_gain, norm_bias, w_qkv, w_proj, b_proj, w_fc1, b_fc1, w_fc2, b_fc2):
    pipe, n = lax.axis_index("pipe"), lax.axis_size("dp")
    is_first = pipe == 0
    weights = (conv_weight, conv_bias, norm_gain, norm_bias, w_qkv, w_proj, b_proj, w_fc1, b_fc1, w_fc2, b_fc2)
    conv_w, conv_b, gain, shift, wq, wp, bp, w1, b1, w2, b2 = (weight[0] for weight in weights)
    params = (conv_w, conv_b, gain, shift, wq, wp, bp[None], w1, b1[None], w2, b2[None])
    images, _, width = section_inputs.shape[1:]

    def role(first):
        return jnp.stack([is_first.astype(jnp.int32), (is_first == first).astype(jnp.int32)])

    own = jnp.swapaxes(section_inputs[0], 0, 1).reshape(-1, width)
    first_out = forward_block(role(True), own, params, images)
    middle = shifted(first_out[0].astype(BF), "pipe", 1)
    second_out = forward_block(role(False), middle, params, images, first_out)
    x = jnp.where(is_first, own, middle)
    result, *saved = second_out
    grad_in, done, small_done, plan = backward(own, x, saved, params, images, n)
    ends = jnp.where(is_first, grad_in, result).reshape(49, images, width)
    section_ends = jnp.swapaxes(ends, 0, 1)[None]
    grads, at = [], 0
    for shape in (w2.shape, w1.shape, wp.shape, wq.shape):
        grads.append(from_chunks(done, at, shape)[None])
        at += shape[0] // SIDE * shape[1] // plan.chunk
    grad_fc2, grad_fc1, grad_proj, grad_qkv = grads
    lanes = width // 128
    sums = jnp.swapaxes(small_done[0, : 32 * lanes].reshape(lanes, 32, 128), 0, 1).reshape(32, width)
    return (section_ends, sums[:18].reshape(conv_weight.shape), sums[18:20][None], sums[20:22][None], sums[22:24][None],
            grad_qkv, grad_proj, sums[24:25], grad_fc1, sums[25:29].reshape(b_fc1.shape), grad_fc2, sums[29:30])


def solution(mesh):
    return jax.shard_map(
        on_device,
        mesh=mesh,
        in_specs=(
            P("pipe", "dp", None, None),
            P("pipe", None, None, None),
            P("pipe", None, None),
            P("pipe", None, None),
            P("pipe", None, None),
            P("pipe", None, None),
            P("pipe", None, None),
            P("pipe", None),
            P("pipe", None, None),
            P("pipe", None),
            P("pipe", None, None),
            P("pipe", None),
        ),
        out_specs=(
            P("pipe", "dp", None, None),
            P("pipe", None, None, None),
            P("pipe", None, None),
            P("pipe", None, None),
            P("pipe", None, None),
            P("pipe", None, None),
            P("pipe", None, None),
            P("pipe", None),
            P("pipe", None, None),
            P("pipe", None),
            P("pipe", None, None),
            P("pipe", None),
        ),
        check_vma=False,
    )
```

```python
import functools

import jax
import jax.numpy as jnp
from jax import lax
from jax.experimental import pallas as pl
from jax.experimental.pallas import tpu as pltpu
from jax.sharding import PartitionSpec as P

MESH = pl.DeviceIdType.MESH
SIDE = 768


HEAD = 32
GROUP = 256
SLOT = 64
BF = jnp.bfloat16
F32 = jnp.float32


def cols(j, width=GROUP):
    return pl.ds(pl.multiple_of(j * width, width), width)


def dot(a, b):
    return lax.dot_general(a, b, (((1,), (0,)), ((), ())), preferred_element_type=F32)


def dot_t(a, b):
    return lax.dot_general(a, b, (((1,), (1,)), ((), ())), preferred_element_type=F32)


def t_dot(a, b):
    return lax.dot_general(a, b, (((0,), (0,)), ((), ())), preferred_element_type=F32)


def fill_swap(ref, images):
    rows, columns = ref.shape
    block = 128

    @pl.loop(0, rows // block)
    def _(b):
        r = lax.broadcasted_iota(jnp.int32, (block, columns), 0) + b * block
        c = lax.broadcasted_iota(jnp.int32, (block, columns), 1)
        image, position = lax.div(r, SLOT), lax.rem(r, SLOT)
        hit = (c == position * images + image) & (position < 49)
        ref[pl.ds(pl.multiple_of(b * block, block), block), :] = jnp.where(hit, 1.0, 0.0).astype(BF)


def clear_border(pad, images):
    zero = jnp.zeros((9 * images, pad.shape[1]), pad.dtype)
    pad[0 : 9 * images, :] = zero
    pad[72 * images : 81 * images, :] = zero
    one = jnp.zeros((images, pad.shape[1]), pad.dtype)

    @pl.loop(1, 8)
    def _(r):
        pad[pl.ds(pl.multiple_of(r * 9 * images, 8), images), :] = one
        pad[pl.ds(pl.multiple_of((r * 9 + 8) * images, 8), images), :] = one


def head_mask(rows_per, count, lanes):
    shape = (count * rows_per, lanes)
    r = lax.broadcasted_iota(jnp.int32, shape, 0)
    c = lax.broadcasted_iota(jnp.int32, shape, 1)
    return lax.div(r, rows_per) == lax.div(c, HEAD)


def spread_heads(x, mask):
    count = mask.shape[0] // x.shape[0]
    return jnp.where(mask, jnp.concatenate([x] * count, axis=0), jnp.zeros((), x.dtype))


def fold_heads(x, mask, rows_per):
    kept = jnp.where(mask, x, 0.0)
    total = kept[0:rows_per]
    for h in range(1, x.shape[0] // rows_per):
        total = total + kept[h * rows_per : (h + 1) * rows_per]
    return total


def soft_down(scores, valid):
    if valid < scores.shape[0]:
        r = lax.broadcasted_iota(jnp.int32, scores.shape, 0)
        scores = jnp.where(r < valid, scores, -jnp.inf)
    e = jnp.exp(scores - jnp.max(scores, axis=0, keepdims=True))
    return e / jnp.sum(e, axis=0, keepdims=True)


def gelu_both(x):
    half = 0.5 + 0.5 * lax.erf(x * 0.7071067811865476)
    return x * half, half + x * (0.3989422804014327 * jnp.exp(-0.5 * x * x))


def dp_dims(n):
    sizes = [1, 1, 1]
    at = 0
    left = n
    while left > 1:
        factor = 2 if left % 2 == 0 else left
        sizes[at % 3] *= factor
        left //= factor
        at += 1
    return tuple(sizes), (sizes[1] * sizes[2], sizes[2], 1)


class Place:
    def __init__(self, dp, size, stride):
        self.size = size
        pos = lax.rem(lax.div(dp, stride), size)
        low = pos < (size + 1) // 2
        self.outer = jnp.where(low, pos, size - 1 - pos)
        self.pos = pos
        self.low = low
        step = jnp.where(low, stride, -stride)
        self.inner_peer = dp + step
        self.outer_peer = dp - step


def pick(flag, a, b):
    out = object.__new__(Place)
    out.size = a.size
    for name in ("pos", "low", "outer", "inner_peer", "outer_peer"):
        setattr(out, name, jnp.where(flag, getattr(a, name), getattr(b, name)))
    return out


class Ring:
    def __init__(self, dp, dims, rows, grad, land, out, out_at, send, recv, local):
        (s0, s1, s2), (t0, t1, t2) = dims
        self.mids = Place(dp, s0, t0)
        self.fast, self.slow = Place(dp, s2, t2), Place(dp, s1, t1)
        self.grad, self.land, self.out, self.out_at = grad, land, out, out_at
        self.grads, self.lands = grad.shape[0], land.shape[0]
        self.send, self.recv, self.local = send, recv, local
        self.sizes, self.lens, self.starts, _ = Ring.shape(rows, dims)

    @staticmethod
    def shape(rows, dims):
        s0, s1, s2 = dims[0]
        sizes = (s2, s0, s1)
        lens = (rows // s2, rows // s2 // s0, rows // (s0 * s1 * s2))
        total, starts = 0, []
        for n, length in zip(sizes, lens):
            starts.append(total)
            total += length * (1 if n == 2 else 5)
        return sizes, lens, starts, total

    def level(self, c, i):
        flag = lax.rem(c + lax.axis_index("pipe"), 2) == 0
        if i == 1:
            return self.mids
        return pick(flag, self.fast, self.slow) if i == 0 else pick(flag, self.slow, self.fast)

    def base(self, c, i):
        start = 0
        for j in range(i):
            start = start + self.level(c, j).pos * self.lens[j]
        return start

    def span(self, c, i, a, b):
        place, length, n = self.level(c, i), self.lens[i], self.sizes[i]
        start = self.base(c, i) + jnp.where(place.low, a * length, (n - b) * length)
        return pl.ds(pl.multiple_of(start, 8), (b - a) * length)

    def mine(self, c, rows):
        return self.grad.at[lax.rem(c, self.grads), rows]

    def landing(self, c, i, at, length):
        return self.land.at[lax.rem(c, self.lands), pl.ds(self.starts[i] + at, length)]

    def copy(self, c, ev, src, dst, peer):
        return pltpu.make_async_remote_copy(
            src_ref=src, dst_ref=dst, send_sem=self.send.at[c, ev], recv_sem=self.recv.at[c, ev],
            device_id={"dp": peer}, device_id_type=MESH)

    def add(self, c, i, a, b, at):
        rows = self.span(c, i, a, b)
        slot = lax.rem(c, self.grads)
        got = self.landing(c, i, at, (b - a) * self.lens[i])
        self.grad[slot, rows] = self.grad[slot, rows] + got[...]

    def give(self, c, i, ev, a, b, at, peer):
        return self.copy(c, ev, self.mine(c, self.span(c, i, a, b)), self.landing(c, i, at, (b - a) * self.lens[i]), peer)

    def reduce_stages(self, i):
        n, length = self.sizes[i], self.lens[i]
        ein, eout = 2 * i, 2 * i + 1
        if n == 1:
            return []
        if n == 2:
            def first(c):
                self.give(c, i, eout, 1, 2, 0, self.level(c, i).inner_peer).start()

            def last(c):
                self.give(c, i, eout, 0, 1, 0, self.level(c, i).inner_peer).wait_recv()
                self.add(c, i, 0, 1, 0)
            return [first, last]

        def zero(c):
            place = self.level(c, i)

            @pl.when(place.outer == 0)
            def _():
                self.give(c, i, ein, 1, 4, 0, place.inner_peer).start()

        def one(c):
            place = self.level(c, i)

            @pl.when(place.outer == 1)
            def _():
                self.give(c, i, ein, 1, 4, 0, place.inner_peer).wait_recv()
                self.add(c, i, 2, 4, jnp.where(place.low, length, 0))
                self.give(c, i, eout, 2, 4, 3 * length, place.inner_peer).start()
                self.add(c, i, 1, 2, jnp.where(place.low, 0, 2 * length))

        def two(c):
            place = self.level(c, i)

            @pl.when(place.outer == 1)
            def _():
                self.give(c, i, eout, 0, 2, 3 * length, place.inner_peer).wait_recv()
                self.add(c, i, 0, 2, 3 * length)
                self.give(c, i, ein, 0, 1, 3 * length, place.outer_peer).start()

        def three(c):
            place = self.level(c, i)

            @pl.when(place.outer == 0)
            def _():
                self.give(c, i, ein, 0, 1, 3 * length, place.inner_peer).wait_recv()
                self.add(c, i, 0, 1, 3 * length)
        return [zero, one, two, three]

    def reduce_ends(self, c):
        for i in range(3):
            n, place = self.sizes[i], self.level(c, i)
            ein, eout = 2 * i, 2 * i + 1
            if n == 2:
                self.give(c, i, eout, 1, 2, 0, place.inner_peer).wait_send()
            elif n == 4:
                @pl.when(place.outer == 0)
                def _():
                    self.give(c, i, ein, 1, 4, 0, place.inner_peer).wait_send()

                @pl.when(place.outer == 1)
                def _():
                    self.give(c, i, eout, 2, 4, 0, place.inner_peer).wait_send()
                    self.give(c, i, ein, 0, 1, 0, place.outer_peer).wait_send()

    def spread(self, c, i, ev, a, b, peer):
        dst = self.out.at[self.out_at(c), self.span(c, i, a, b)]
        return self.copy(c, ev, dst, dst, peer)

    def gather_stages(self, i):
        n = self.sizes[i]
        ein, eout = 6 + 2 * i, 7 + 2 * i
        if n == 1:
            return []
        if n == 2:
            def first(c):
                self.spread(c, i, eout, 0, 1, self.level(c, i).inner_peer).start()

            def last(c):
                self.spread(c, i, eout, 1, 2, self.level(c, i).inner_peer).wait_recv()
            return [first, last]

        def zero(c):
            place = self.level(c, i)

            @pl.when(place.outer == 0)
            def _():
                self.spread(c, i, ein, 0, 1, place.inner_peer).start()

        def one(c):
            place = self.level(c, i)

            @pl.when(place.outer == 1)
            def _():
                self.spread(c, i, ein, 0, 1, place.outer_peer).wait_recv()
                self.spread(c, i, eout, 0, 2, place.inner_peer).start()

        def two(c):
            place = self.level(c, i)

            @pl.when(place.outer == 1)
            def _():
                self.spread(c, i, eout, 2, 4, place.inner_peer).wait_recv()
                self.spread(c, i, ein, 1, 4, place.outer_peer).start()

        def three(c):
            place = self.level(c, i)

            @pl.when(place.outer == 0)
            def _():
                self.spread(c, i, ein, 1, 4, place.inner_peer).wait_recv()
        return [zero, one, two, three]

    def gather_ends(self, c):
        for i in range(3):
            n, place = self.sizes[i], self.level(c, i)
            ein, eout = 6 + 2 * i, 7 + 2 * i
            if n == 2:
                self.spread(c, i, eout, 0, 1, place.inner_peer).wait_send()
            elif n == 4:
                @pl.when(place.outer == 0)
                def _():
                    self.spread(c, i, ein, 0, 1, place.inner_peer).wait_send()

                @pl.when(place.outer == 1)
                def _():
                    self.spread(c, i, eout, 0, 2, place.inner_peer).wait_send()
                    self.spread(c, i, ein, 1, 4, place.outer_peer).wait_send()

    def settle(self, c):
        rows = pl.ds(pl.multiple_of(self.base(c, 3), 8), self.lens[2])
        copy = pltpu.make_async_copy(self.mine(c, rows), self.out.at[self.out_at(c), rows], self.local)
        copy.start()
        copy.wait()

    def stages(self, first, second, last):
        groups = [self.reduce_stages(0), self.reduce_stages(1), self.reduce_stages(2), [self.settle],
                  self.gather_stages(2), self.gather_stages(1), self.gather_stages(0), [last]]
        joined = [[first], [second]]
        for group in groups:
            if group:
                joined[-1].append(group[0])
                joined += [[stage] for stage in group[1:]]
        return [functools.partial(run_all, stages) for stages in joined]

    def greet(self):
        barrier = pltpu.get_barrier_semaphore()
        pl.semaphore_signal(barrier, inc=1, device_id={"pipe": 1 - lax.axis_index("pipe")}, device_id_type=MESH)
        count = jnp.int32(1)
        for place in (self.fast, self.mids, self.slow):
            if place.size == 1:
                continue
            pl.semaphore_signal(barrier, inc=1, device_id={"dp": place.inner_peer}, device_id_type=MESH)
            count = count + 1
            if place.size == 4:
                @pl.when(place.outer == 1)
                def _():
                    pl.semaphore_signal(barrier, inc=1, device_id={"dp": place.outer_peer}, device_id_type=MESH)
                count = count + jnp.where(place.outer == 1, 1, 0)
        pl.semaphore_wait(barrier, count)


def run_all(stages, c):
    for stage in stages:
        stage(c)


def spatial_forward(packed, mixed, soft, images):
    width = mixed.shape[1]

    @pl.loop(0, images, unroll=4)
    def _(i):
        rows = pl.ds(pl.multiple_of(i * SLOT, SLOT), SLOT)
        mask = head_mask(SLOT, GROUP // HEAD, GROUP)
        for g in range(width // GROUP):
            q, k, v = (packed[rows, part * width + g * GROUP : part * width + (g + 1) * GROUP] for part in range(3))
            weights = soft_down(dot_t(k, spread_heads(q, mask)), 49).astype(BF)
            soft[i, g] = weights
            mixed[rows, g * GROUP : (g + 1) * GROUP] = fold_heads(t_dot(weights, v), mask, SLOT).astype(BF)


def channel_forward(packed, mixed, soft, images):
    width = mixed.shape[1]

    @pl.loop(0, images, unroll=4)
    def _(i):
        rows = pl.ds(pl.multiple_of(i * SLOT, SLOT), SLOT)
        mask = head_mask(HEAD, 128 // HEAD, 128)
        for g in range(width // 128):
            q, k, v = (packed[rows, part * width + g * 128 : part * width + (g + 1) * 128] for part in range(3))
            weights = soft_down(fold_heads(t_dot(k, q), mask, HEAD), HEAD).astype(BF)
            soft[i, g // 2, g % 2 * HEAD : (g % 2 + 1) * HEAD, 0:128] = weights
            mixed[rows, g * 128 : (g + 1) * 128] = dot(v, spread_heads(weights, mask)).astype(BF)


def spatial_backward(packed, grad_mixed, soft, start, stop):
    width = grad_mixed.shape[1]

    @pl.loop(start, stop)
    def _(i):
        rows = pl.ds(pl.multiple_of(i * SLOT, SLOT), SLOT)
        mask = head_mask(SLOT, GROUP // HEAD, GROUP)
        made = []
        for g in range(width // GROUP):
            at = [slice(part * width + g * GROUP, part * width + (g + 1) * GROUP) for part in range(3)]
            made.append((at, [packed[rows, a] for a in at], soft[i, g], grad_mixed[rows, g * GROUP : (g + 1) * GROUP]))
        ready = []
        for at, (q, k, v), weights, do in made:
            out_spread = spread_heads(do, mask)
            w = weights.astype(F32)
            dw = dot_t(v, out_spread)
            ds = (w * (dw - jnp.sum(dw * w, axis=0, keepdims=True))).astype(BF)
            dq = (fold_heads(t_dot(ds, k), mask, SLOT) * HEAD ** -0.5).astype(BF)
            ready += zip(at, (dq, dot(ds, spread_heads(q, mask)).astype(BF), dot(weights, out_spread).astype(BF)))
        for at, value in ready:
            packed[rows, at] = value


def channel_backward(packed, grad_mixed, soft, start, stop):
    width = grad_mixed.shape[1]

    @pl.loop(start, stop)
    def _(i):
        rows = pl.ds(pl.multiple_of(i * SLOT, SLOT), SLOT)
        mask = head_mask(HEAD, 128 // HEAD, 128)
        made = []
        for g in range(width // 128):
            at = [slice(part * width + g * 128, part * width + (g + 1) * 128) for part in range(3)]
            weights = soft[i, g // 2, g % 2 * HEAD : (g % 2 + 1) * HEAD, 0:128]
            made.append((at, [packed[rows, a] for a in at], weights, grad_mixed[rows, g * 128 : (g + 1) * 128]))
        ready = []
        for at, (q, k, v), weights, do in made:
            w = weights.astype(F32)
            dw = fold_heads(t_dot(v, do), mask, HEAD)
            ds = spread_heads((w * (dw - jnp.sum(dw * w, axis=0, keepdims=True))).astype(BF), mask)
            dq = (dot(k, ds) * HEAD ** -0.5).astype(BF)
            ready += zip(at, (dq, dot_t(q, ds).astype(BF), dot_t(do, spread_heads(weights, mask)).astype(BF)))
        for at, value in ready:
            packed[rows, at] = value


def encode(pad, kernel, bias, out, images):
    @pl.loop(0, pad.shape[1] // 128)
    def _(lane):
        ls = cols(lane, 128)
        taps = [jnp.broadcast_to(kernel(t, ls), (images, 128)) for t in range(9)]
        shift = jnp.broadcast_to(bias(ls), (images, 128))

        @pl.loop(0, 7, unroll=7)
        def _(r):
            for c in range(7):
                total = shift
                for t in range(9):
                    at = pl.multiple_of(((r + t // 3) * 9 + c + t % 3) * images, 8)
                    piece = pad[pl.ds(at, images), ls]
                    total = total + piece * taps[t]
                    if t == 4:
                        total = total + piece
                out[pl.ds(pl.multiple_of((r * 7 + c) * images, 8), images), ls] = total


def normalise(stream, gain, bias, out):
    @pl.loop(0, stream.shape[0] // 16, unroll=5)
    def _(p):
        rows = pl.ds(pl.multiple_of(p * 16, 16), 16)
        s = stream[rows, :]
        centered = s - jnp.mean(s, axis=-1, keepdims=True)
        spread = jnp.mean(centered * centered, axis=-1, keepdims=True)
        out[rows, :] = (centered * lax.rsqrt(spread + 1e-5) * gain + bias).astype(BF)


def encode_back(gpad, given, kernel, out, put, first_row, bias_row, images):
    @pl.loop(0, gpad.shape[1] // 128)
    def _(lane):
        ls = cols(lane, 128)
        taps = [jnp.broadcast_to(kernel(8 - t, ls), (images, 128)) for t in range(9)]

        def row(r, totals):
            totals = list(totals)
            for c in range(7):
                at = pl.ds(pl.multiple_of((r * 7 + c) * images, 8), images)
                source = given[at, ls]
                total = None
                for t in range(9):
                    near = pl.ds(pl.multiple_of(((r + t // 3) * 9 + c + t % 3) * images, 8), images)
                    piece = gpad[near, ls]
                    if t == 4:
                        totals[9] = totals[9] + piece
                        total = total + piece
                    total = piece * taps[t] if total is None else total + piece * taps[t]
                    totals[8 - t] = totals[8 - t] + source * piece
                out[at, ls] = total
            return tuple(totals)
        totals = lax.fori_loop(0, 7, row, (jnp.zeros((images, 128), F32),) * 10, unroll=True)
        for t in range(9):
            put(first_row + t, lane, jnp.sum(totals[t], axis=0, keepdims=True))
        put(bias_row, lane, jnp.sum(totals[9], axis=0, keepdims=True))


def normalise_back(stream, grad, base, gain, gpad, put, gain_row, shift_row, acc, images):
    acc[...] = jnp.zeros_like(acc)

    @pl.loop(0, 49, unroll=7)
    def _(p):
        rows = pl.ds(pl.multiple_of(p * images, 8), images)
        s, dy = stream[rows, :], grad[rows, :]
        centered = s - jnp.mean(s, axis=-1, keepdims=True)
        rate = lax.rsqrt(jnp.mean(centered * centered, axis=-1, keepdims=True) + 1e-5)
        unit = centered * rate
        acc[0] += dy * unit
        acc[1] += dy
        dg = dy * gain
        m1 = jnp.mean(dg, axis=-1, keepdims=True)
        m2 = jnp.mean(dg * unit, axis=-1, keepdims=True)
        at = ((lax.div(p, 7) + 1) * 9 + lax.rem(p, 7) + 1) * images
        gpad[pl.ds(pl.multiple_of(at, 8), images), :] = base[rows, :] + rate * (dg - m1 - unit * m2)
    for row, total in ((gain_row, acc[0]), (shift_row, acc[1])):
        total = jnp.sum(total, axis=0, keepdims=True)
        for lane in range(total.shape[1] // 128):
            put(row, lane, total[:, lane * 128 : (lane + 1) * 128])


def fill_pad(pad, source, images):
    @pl.loop(0, 7)
    def _(r):
        inner = pl.ds(pl.multiple_of(((r + 1) * 9 + 1) * images, 8), 7 * images)
        pad[inner, :] = source[pl.ds(pl.multiple_of(r * 7 * images, 8), 7 * images), :]


CONV, CONV_BIAS, GAIN, SHIFT, B_PROJ, B_FC1, B_FC2 = 0, 18, 20, 22, 24, 25, 29
HIDDEN, COT, N2, PRE, MIXED, ATT, N1, PACKED = 0, 4, 5, 6, 10, 11, 12, 13
SEGMENTS = 12


def section_kernel(images, dims, rows, lags, chunk,
                   halves, conv_w, conv_b, gain, shift, b_proj, b_fc1, b_fc2, w_qkv, w_proj, w_fc1, w_fc2,
                   ends, out, small_out, acts, k_one, k_mid, k_two, k_packed, k_soft, k_slope, x_qkv, x_proj, x_fc1, x_fc2,
                   v_qkv, v_proj, v_fc1, v_fc2, params, xb, cot, pad, one, stream, gmid, gn, packed, soft, slope, hidden,
                   swap, gm_s, n1, n2, mixed, gatt, acc, small_grad, small_pair,
                   grad, land, pair_out, pair_in, small_land, left_buf, right_buf,
                   load, store, push_send, push_recv, fetch_sem, pair_send, pair_recv, send, recv, local, ssend, srecv, slocal,
                   bring_send, bring_recv):
    pipe, dp = lax.axis_index("pipe"), lax.axis_index("dp")
    other = 1 - pipe
    first = pipe == 0
    tokens, width = gn.shape
    wide = v_fc1.shape[1]
    real = 49 * images
    per = SIDE // (2 * chunk)
    block_pairs = SEGMENTS * per
    pairs = 2 * block_pairs
    weights = ((w_qkv, x_qkv, v_qkv), (w_proj, x_proj, v_proj), (w_fc1, x_fc1, v_fc1), (w_fc2, x_fc2, v_fc2))
    QKV, PROJ, FC1, FC2 = range(4)

    def to_core(at, src, dst):
        return pltpu.make_async_remote_copy(src_ref=src, dst_ref=dst, send_sem=push_send.at[at], recv_sem=push_recv.at[at],
                                            device_id={"pipe": other}, device_id_type=MESH)
    push_params = to_core(0, params.at[pipe], params.at[pipe])
    push_x = to_core(1, halves.at[1], xb.at[0])
    push_cot = to_core(1, halves.at[0], cot)
    push_weights = [to_core(2 + at, own, far) for at, (own, far, _) in enumerate(weights)]
    lanes = [pl.ds(lane * 128, 128) for lane in range(width // 128)]
    push_result = [to_core(8 + at, gn.at[:, ls], ends.at[0, at]) for at, ls in enumerate(lanes)]
    push_grad = [to_core(8 + at, gmid.at[:, ls], ends.at[1, at]) for at, ls in enumerate(lanes)]

    def load_weight(b, at, fresh):
        own, far, near = weights[at]

        @pl.when(b == pipe)
        def _():
            pltpu.make_async_copy(own, near, load.at[at]).start()

        @pl.when(b != pipe)
        def _():
            if fresh:
                push_weights[at].wait_recv()
            pltpu.make_async_copy(far, near, load.at[at]).start()

    def wait_weight(at):
        own, _, near = weights[at]
        pltpu.make_async_copy(own, near, load.at[at]).wait()

    def keep(at, src, dst):
        return pltpu.make_async_copy(src, dst, store.at[at])

    def block_stores(b):
        return [keep(0, one, k_one.at[b]), keep(1, gmid, k_mid.at[b]), keep(2, stream, k_two.at[b]), keep(3, packed, k_packed.at[b]),
                keep(4, soft, k_soft.at[b]), keep(5, slope, k_slope.at[b]), keep(6, n1, acts.at[b, N1]), keep(7, mixed, acts.at[b, MIXED]),
                keep(8, n2, acts.at[b, N2])] + [
                    keep(9 + s, hidden.at[:, pl.ds(s * SIDE, SIDE)], acts.at[b, HIDDEN + s]) for s in range(wide // SIDE)]

    def row_of(b, row):
        return params[b, row : row + 1, :]

    def taps_of(b, j):
        return (lambda t, ls: params[b, pl.ds(CONV + 9 * j + t, 1), ls]), (lambda ls: params[b, pl.ds(CONV_BIAS + j, 1), ls])

    def block_of(k):
        return jnp.where(k < block_pairs, 1, 0)

    def number_of(k, core):
        return 2 * lax.rem(k, block_pairs) + core

    def out_at(k):
        return jnp.where(block_of(k) == pipe, number_of(k, pipe), 2 * block_pairs + lax.rem(k, block_pairs))

    main = Ring(dp, dims, rows, grad, land, out, out_at, send, recv, local)
    small = Ring(dp, dims, small_grad.shape[1], small_pair, small_land, small_out, lambda c: 0, ssend, srecv, slocal)

    def slots_of(k):
        at = lax.div(lax.rem(k, block_pairs), per)
        left = jnp.where(at < 4, HIDDEN + at, jnp.where(at < 8, N2, jnp.where(at < 9, MIXED, N1)))
        right = jnp.where(at < 4, COT, jnp.where(at < 8, PRE + at - 4, jnp.where(at < 9, ATT, PACKED + at - 9)))
        return left, right, lax.rem(lax.rem(k, block_pairs), per)

    def fetches(k):
        left, right, part = slots_of(k)
        slot, b = lax.rem(k, 2), block_of(k)
        return (pltpu.make_async_copy(acts.at[b, left], left_buf.at[slot], fetch_sem.at[slot, 0]),
                pltpu.make_async_copy(acts.at[b, right, :, cols(part, 2 * chunk)], right_buf.at[slot], fetch_sem.at[slot, 1]))

    def pair_copy(k):
        return pltpu.make_async_remote_copy(
            src_ref=pair_out.at[lax.rem(k, pair_out.shape[0])], dst_ref=pair_in.at[lax.rem(k, pair_in.shape[0])],
            send_sem=pair_send.at[k], recv_sem=pair_recv.at[k], device_id={"pipe": other}, device_id_type=MESH)

    def make(k):
        for copy in fetches(k):
            copy.wait()

        @pl.when(k >= pair_out.shape[0])
        def _():
            pair_copy(k - pair_out.shape[0]).wait_send()

        @pl.when(k >= main.grads)
        def _():
            main.reduce_ends(k - main.grads)
        slot, place, far = lax.rem(k, 2), lax.rem(k, main.grads), lax.rem(k, pair_out.shape[0])
        both = t_dot(left_buf[slot], right_buf[slot]).astype(BF)

        @pl.when(first)
        def _():
            grad[place, 0:SIDE] = both[:, :chunk]
            pair_out[far] = both[:, chunk:]

        @pl.when(jnp.logical_not(first))
        def _():
            pair_out[far] = both[:, :chunk]
            grad[place, 0:SIDE] = both[:, chunk:]
        pair_copy(k).start()
        if rows > SIDE:
            grad[place, SIDE:rows] = jnp.zeros((rows - SIDE, chunk), BF)

    def join(k):
        pair_copy(k).wait_recv()
        place = lax.rem(k, main.grads)
        grad[place, 0:SIDE] = grad[place, 0:SIDE] + pair_in[lax.rem(k, pair_in.shape[0])]

    def bring(k):
        number = number_of(k, pipe)
        at = lax.rem(k, block_pairs)
        return pltpu.make_async_remote_copy(
            src_ref=out.at[out_at(k)], dst_ref=out.at[number], send_sem=bring_send.at[at], recv_sem=bring_recv.at[at],
            device_id={"pipe": other}, device_id_type=MESH)

    def hand_over(k):
        @pl.when(block_of(k) != pipe)
        def _():
            bring(k).start()
    small_copy = to_core(7, small_grad.at[other], small_pair.at[1])

    def small_make(k):
        small_copy.start()
        small_pair[0] = small_grad[pipe]

    def small_join(k):
        small_copy.wait_recv()
        small_pair[0] = small_pair[0] + small_pair[1]

    def tick(t):
        stages = main.stages(make, join, hand_over)
        small_stages = small.stages(small_make, small_join, lambda k: None)
        for s in reversed(range(len(stages))):
            k = t - lags[s]

            @pl.when((k >= 0) & (k < pairs))
            def _():
                stages[s](k)

            @pl.when(k == pairs)
            def _():
                small_stages[s](0)

    main.greet()
    for j in range(2):
        params[pipe, CONV + 9 * j : CONV + 9 * (j + 1), :] = conv_w[j]
    for row, ref in ((CONV_BIAS, conv_b), (GAIN, gain), (SHIFT, shift), (B_PROJ, b_proj), (B_FC2, b_fc2)):
        params[pipe, row : row + ref.shape[0], :] = ref[...]
    for j in range(wide // width):
        params[pipe, B_FC1 + j : B_FC1 + j + 1, :] = b_fc1[:, j * width : (j + 1) * width]
    x_copy = pltpu.make_async_copy(halves.at[0], xb.at[0], load.at[5])
    cot_copy = pltpu.make_async_copy(halves.at[1], cot, load.at[5])
    push_params.start()

    @pl.when(first)
    def _():
        push_x.start()
        x_copy.start()

    @pl.when(jnp.logical_not(first))
    def _():
        push_cot.start()
        cot_copy.start()
    push_weights[QKV].start()
    fill_swap(swap, images)
    clear_border(pad, images)
    small_grad[...] = jnp.zeros_like(small_grad)
    one[real:tokens, :] = jnp.zeros((tokens - real, width), F32)
    stream[real:tokens, :] = jnp.zeros((tokens - real, width), F32)
    push_params.wait_recv()

    @pl.when(first)
    def _():
        x_copy.wait()

    @pl.when(jnp.logical_not(first))
    def _():
        push_x.wait_recv()

    @pl.loop(0, 2)
    def _(b):
        stores = block_stores(b)

        @pl.when(b > 0)
        def _():
            for copy in stores:
                copy.wait()
        load_weight(b, QKV, True)
        gn[...] = xb[b].astype(F32)
        fill_pad(pad, gn, images)
        kernel, bias = taps_of(b, 0)
        encode(pad, kernel, bias, one, images)
        stores[0].start()
        normalise(one, row_of(b, GAIN), row_of(b, SHIFT), n1)
        stores[6].start()

        @pl.when(b == 0)
        def _():
            push_weights[PROJ].start()
            push_weights[FC1].start()

        gm_s[...] = dot(swap[...], n1[...]).astype(BF)
        wait_weight(QKV)

        @pl.loop(0, 3)
        def _(j):
            scale = jnp.where(j == 0, HEAD ** -0.5, 1.0)
            packed[:, cols(j, width)] = (dot(gm_s[...], v_qkv[:, cols(j, width)]) * scale).astype(BF)
        stores[3].start()

        @pl.when(b == 0)
        def _():
            push_weights[FC2].start()
        load_weight(b, PROJ, True)

        @pl.when(b == 0)
        def _():
            spatial_forward(packed, gm_s, soft, images)

        @pl.when(b == 1)
        def _():
            channel_forward(packed, gm_s, soft, images)
        stores[4].start()
        load_weight(b, FC1, True)

        mixed[...] = t_dot(swap[...], gm_s[...]).astype(BF)
        stores[7].start()
        wait_weight(PROJ)

        gmid[...] = one[...] + dot(mixed[...], v_proj[...]) + row_of(b, B_PROJ)
        stores[1].start()
        fill_pad(pad, gmid, images)
        kernel, bias = taps_of(b, 1)
        encode(pad, kernel, bias, stream, images)
        stores[2].start()
        normalise(stream, row_of(b, GAIN + 1), row_of(b, SHIFT + 1), n2)
        stores[8].start()
        wait_weight(FC1)
        load_weight(b, FC2, True)

        @pl.loop(0, wide // width)
        def _(j):
            at = cols(j, width)
            value, rate = gelu_both(dot(n2[...], v_fc1[:, at]) + params[b, pl.ds(B_FC1 + j, 1), :])
            hidden[:, at] = value.astype(BF)
            slope[:, at] = rate.astype(BF)
        stores[5].start()
        for copy in stores[9:]:
            copy.start()
        wait_weight(FC2)

        gn[...] = stream[...] + dot(hidden[...], v_fc2[...]) + row_of(b, B_FC2)

        @pl.when(b == 0)
        def _():
            xb[1] = gn[...].astype(BF)

    end_copy = [pltpu.make_async_copy(gn.at[:, ls], ends.at[1, at], load.at[13 + at]) for at, ls in enumerate(lanes)]
    last_copy = [pltpu.make_async_copy(gmid.at[:, ls], ends.at[0, at], load.at[13 + at]) for at, ls in enumerate(lanes)]

    @pl.when(first)
    def _():
        for copy in push_result:
            copy.start()
        push_cot.wait_recv()

    @pl.when(jnp.logical_not(first))
    def _():
        for copy in end_copy:
            copy.start()
        cot_copy.wait()
    keep_cot = keep(13, cot, acts.at[1, COT])
    keep_cot.start()
    for copy in block_stores(1):
        copy.wait()
    keep_cot.wait()
    for copy in fetches(0):
        copy.start()

    def put(b):
        def at(row, lane, value):
            small_grad[b, pl.ds(lane * 32 + row, 1), :] = value
        return at

    loads = [pltpu.make_async_copy(k_slope.at[0], slope, load.at[7]), pltpu.make_async_copy(k_packed.at[0], packed, load.at[8]),
             pltpu.make_async_copy(k_soft.at[0], soft, load.at[9]), pltpu.make_async_copy(k_two.at[0], stream, load.at[10]),
             pltpu.make_async_copy(k_mid.at[0], gmid, load.at[11])]

    def later(b, at):
        @pl.when(b == 0)
        def _():
            loads[at].wait()

    def later_weight(b, at):
        @pl.when(b == 0)
        def _():
            wait_weight(at)

    def ahead(b, do):
        pl.when(b == 1)(do)

    def pre_part(part):
        def run(b):
            if part == 0:
                later(b, 0)
                later_weight(b, FC2)
                one[...] = cot[...].astype(F32)
            each = wide // 3
            at = slice(part * each, (part + 1) * each)
            pre = dot_t(cot[...], v_fc2[at, :]) * slope[:, at].astype(F32)
            slope[:, at] = pre.astype(BF)
            total = jnp.sum(pre, axis=0, keepdims=True)
            for piece in range(each // 128):
                lane = part * each // 128 + piece
                put(b)(B_FC1 + lane // (width // 128), lane % (width // 128), total[:, piece * 128 : (piece + 1) * 128])
            if part == 2:
                ahead(b, lambda: load_weight(0, FC2, False))
                copies = [keep(s, slope.at[:, pl.ds(s * SIDE, SIDE)], acts.at[b, PRE + s]) for s in range(wide // SIDE)]
                for copy in copies:
                    copy.start()
                for lane in range(width // 128):
                    put(b)(B_FC2, lane, jnp.sum(one[:, lane * 128 : (lane + 1) * 128], axis=0, keepdims=True))
                for copy in copies:
                    copy.wait()
        return run

    def through_fc1(b):
        @pl.when(b == 1)
        def _():
            @pl.when(first)
            def _():
                for copy in push_result:
                    copy.wait_send()

            @pl.when(jnp.logical_not(first))
            def _():
                for copy in end_copy:
                    copy.wait()
        later_weight(b, FC1)

        gn[...] = dot_t(slope[...], v_fc1[...])
        ahead(b, lambda: load_weight(0, FC1, False))

    def through_second(b):
        later(b, 3)
        normalise_back(stream, gn, one, row_of(b, GAIN + 1), pad, put(b), GAIN + 1, SHIFT + 1, acc, images)
        pltpu.make_async_copy(k_one.at[b], stream, load.at[12]).start()
        later(b, 4)
        encode_back(pad, gmid, taps_of(b, 1)[0], gmid, put(b), CONV + 9, CONV_BIAS + 1, images)
        gmid[real:tokens, :] = jnp.zeros((tokens - real, width), F32)
        for lane in range(width // 128):
            part = gmid[:, lane * 128 : (lane + 1) * 128]
            put(b)(B_PROJ, lane, jnp.sum(part, axis=0, keepdims=True))
            gatt[:, lane * 128 : (lane + 1) * 128] = part.astype(BF)
        keep(4, gatt, acts.at[b, ATT]).start()

    def through_proj(b):
        later_weight(b, PROJ)

        n2[...] = dot_t(gatt[...], v_proj[...]).astype(BF)
        ahead(b, lambda: load_weight(0, PROJ, False))
        gm_s[...] = dot(swap[...], n2[...]).astype(BF)
        later(b, 1)
        later(b, 2)

    def through_mix(part):
        def run(b):
            each = images // 2

            @pl.when(b == 0)
            def _():
                spatial_backward(packed, gm_s, soft, part * each, (part + 1) * each)

            @pl.when(b == 1)
            def _():
                channel_backward(packed, gm_s, soft, part * each, (part + 1) * each)
            if part == 1:
                keep(4, gatt, acts.at[b, ATT]).wait()
        return run

    def unswap(b):
        @pl.loop(0, 3)
        def _(j):
            slope[:, cols(j, width)] = t_dot(swap[...], packed[:, cols(j, width)]).astype(BF)
        copies = [keep(s, slope.at[:, pl.ds(s * SIDE, SIDE)], acts.at[b, PACKED + s]) for s in range(3)]
        for copy in copies:
            copy.start()
        for copy in copies:
            copy.wait()

    def through_qkv(b):
        later_weight(b, QKV)

        gn[...] = dot_t(slope[:, 0 : 3 * width], v_qkv[...])

        def prepare():
            load_weight(0, QKV, False)
            for at in range(3):
                loads[at].start()
        ahead(b, prepare)

    def through_first(b):
        pltpu.make_async_copy(k_one.at[b], stream, load.at[12]).wait()
        normalise_back(stream, gn, gmid, row_of(b, GAIN), pad, put(b), GAIN, SHIFT, acc, images)
        ahead(b, lambda: loads[3].start())

    def finish(b):
        gn[...] = xb[b].astype(F32)
        encode_back(pad, gn, taps_of(b, 0)[0], gmid, put(b), CONV, CONV_BIAS, images)

        @pl.when(b == 1)
        def _():
            cot[...] = gmid[...].astype(BF)
            copy = keep(5, cot, acts.at[0, COT])
            copy.start()
            loads[4].start()
            copy.wait()

        @pl.when((b == 0) & first)
        def _():
            for copy in last_copy:
                copy.start()

        @pl.when((b == 0) & jnp.logical_not(first))
        def _():
            for copy in push_grad:
                copy.start()
    segments = [pre_part(0), pre_part(1), pre_part(2), through_fc1, through_second, through_proj, through_mix(0), through_mix(1),
                unswap, through_qkv, through_first, finish]

    @pl.loop(0, pairs + 1 + lags[-1])
    def _(t):
        tick(t)

        @pl.when((t < pairs) & (lax.rem(t, per) == 0))
        def _():
            b, at = block_of(t), lax.div(lax.rem(t, block_pairs), per)
            for number, segment in enumerate(segments):
                @pl.when(at == number)
                def _():
                    segment(b)

        @pl.when(t + 1 < pairs)
        def _():
            for copy in fetches(t + 1):
                copy.start()

    @pl.loop(pairs - main.grads, pairs)
    def _(k):
        main.reduce_ends(k)

    @pl.loop(pairs - pair_out.shape[0], pairs)
    def _(k):
        pair_copy(k).wait_send()

    @pl.loop(0, pairs)
    def _(k):
        main.gather_ends(k)

        @pl.when(block_of(k) != pipe)
        def _():
            bring(k).wait_send()
    small.reduce_ends(0)
    small.gather_ends(0)
    small_copy.wait_send()
    push_params.wait_send()
    for copy in push_weights:
        copy.wait_send()

    @pl.when(first)
    def _():
        push_x.wait_send()
        for copy in last_copy:
            copy.wait()
        for copy in push_grad:
            copy.wait_recv()

    @pl.when(jnp.logical_not(first))
    def _():
        push_cot.wait_send()
        for copy in push_grad:
            copy.wait_send()
        for copy in push_result:
            copy.wait_recv()

    @pl.loop(0, block_pairs)
    def _(at):
        number = 2 * at + other
        pltpu.make_async_remote_copy(
            src_ref=out.at[number], dst_ref=out.at[number], send_sem=bring_send.at[at], recv_sem=bring_recv.at[at],
            device_id={"pipe": other}, device_id_type=MESH).wait_recv()


def section(halves, small, weights, images, n, collective_id=0):
    w_qkv, w_proj, w_fc1, w_fc2 = weights
    _, tokens, width = halves.shape
    wide = w_fc1.shape[1]
    slots = images * SLOT
    dims = dp_dims(n)
    chunk = 384 if n <= 16 else 128
    total = (wide // SIDE * 2 + 4) * SIDE // chunk
    pairs = total
    rows = -(-SIDE // (16 * n)) * 16 * n
    small_rows = 16 * n
    _, _, _, land = Ring.shape(rows, dims)
    _, _, _, small_land = Ring.shape(small_rows, dims)
    hops = sum(0 if s == 1 else 1 if s == 2 else 3 for s in dims[0])
    gaps = [1, 2] + [1] * (2 * hops - 2) + [2]
    lags = [sum(gaps[:s]) for s in range(2 * hops + 2)]
    grads, lands = lags[hops + 1] + 3, 10
    any_space = pl.BlockSpec(memory_space=pl.ANY)
    vmem = pl.BlockSpec(memory_space=pltpu.VMEM)
    soft = (images, width // GROUP, SLOT, 2 * GROUP)
    outs = [((2, width // 128, tokens, 128), F32), ((total + total // 2, rows, chunk), BF), ((1, small_rows, 128), F32),
            ((2, 16, tokens, SIDE), BF), ((2, tokens, width), F32), ((2, tokens, width), F32), ((2, tokens, width), F32),
            ((2, slots, 3 * width), BF), ((2, *soft), BF), ((2, tokens, wide), BF),
            (w_qkv.shape, BF), (w_proj.shape, BF), (w_fc1.shape, BF), (w_fc2.shape, BF)]
    dma = pltpu.SemaphoreType.DMA

    def plain(shape):
        return pltpu.VMEM(shape, F32)

    def low(shape):
        return pltpu.VMEM(shape, BF)
    results = pl.pallas_call(
        functools.partial(section_kernel, images, dims, rows, lags, chunk),
        out_shape=[jax.ShapeDtypeStruct(*o) for o in outs],
        in_specs=[any_space] + [vmem] * 7 + [any_space] * 4,
        out_specs=[any_space] * len(outs),
        scratch_shapes=[low(w.shape) for w in weights] + [
            plain((2, 32, width)), low((2, tokens, width)), low((tokens, width)), plain((81 * images, width)),
            plain((tokens, width)), plain((tokens, width)), plain((tokens, width)), plain((tokens, width)),
            low((slots, 3 * width)), low(soft), low((tokens, wide)), low((tokens, wide)),
            low((slots, tokens)), low((slots, width)), low((tokens, width)), low((tokens, width)), low((tokens, width)), low((tokens, width)),
            plain((2, images, width)), plain((2, small_rows, 128)), plain((2, small_rows, 128)),
            low((grads, rows, chunk)), low((lands, land, chunk)), low((4, SIDE, chunk)), low((6, SIDE, chunk)), plain((1, small_land, 128)),
            low((2, tokens, SIDE)), low((2, tokens, 2 * chunk)),
            dma((13 + width // 128,)), dma((14,)), dma((8 + width // 128,)), dma((8 + width // 128,)), dma((2, 2)), dma((pairs,)), dma((pairs,)),
            dma((pairs, 12)), dma((pairs, 12)), dma, dma((1, 12)), dma((1, 12)), dma, dma((pairs // 2,)), dma((pairs // 2,)),
        ],
        compiler_params=pltpu.CompilerParams(collective_id=collective_id, has_side_effects=True, vmem_limit_bytes=63 * 2**20),
    )(halves, *small, w_qkv, w_proj, w_fc1, w_fc2)
    return results[:3]


def finish_kernel(images, chunk, done, sums, ends, fc2, fc1, proj, qkv, conv_w, conv_b, gain, shift, b_proj, b_fc1, b_fc2, section,
                  low_buf, wide_buf, end_buf, read, write, end_sem):
    depth = low_buf.shape[0]
    jobs, start = [], 0
    for dst in (fc2, fc1, proj, qkv):
        across = dst.shape[2] // chunk
        number = dst.shape[1] // SIDE * across
        jobs.append((start, number, across, dst))
        start += number
    end_copy = pltpu.make_async_copy(ends, end_buf, end_sem)
    end_copy.start()

    def get(c):
        return pltpu.make_async_copy(done.at[c, pl.ds(0, SIDE)], low_buf.at[lax.rem(c, depth)], read.at[lax.rem(c, depth)])

    def give(c, dst, across, at):
        rows = pl.ds(pl.multiple_of(lax.div(at, across) * SIDE, SIDE), SIDE)
        return pltpu.make_async_copy(wide_buf.at[lax.rem(c, depth)], dst.at[0, rows, cols(lax.rem(at, across), chunk)],
                                     write.at[lax.rem(c, depth)])

    @pl.loop(0, depth)
    def _(c):
        get(c).start()
    for begin, number, across, dst in jobs:
        @pl.loop(0, number)
        def _(at):
            c = begin + at
            slot = lax.rem(c, depth)
            get(c).wait()

            @pl.when(c >= depth)
            def _():
                give(c, dst, across, at).wait()
            for r in range(0, SIDE, 128):
                wide_buf[slot, r : r + 128] = low_buf[slot, r : r + 128].astype(F32)
            give(c, dst, across, at).start()

            @pl.when(c + depth < start)
            def _():
                get(c + depth).start()
    lanes = fc2.shape[2] // 128
    width = fc2.shape[2]

    def take(first_row, ref, index, rows):
        for lane in range(lanes):
            ref[index + (slice(lane * 128, (lane + 1) * 128),)] = sums[0, lane * 32 + first_row : lane * 32 + first_row + rows, :]
    for j in range(2):
        take(CONV + 9 * j, conv_w, (0, j, slice(0, 9)), 9)
    take(CONV_BIAS, conv_b, (0, slice(0, 2)), 2)
    take(GAIN, gain, (0, slice(0, 2)), 2)
    take(SHIFT, shift, (0, slice(0, 2)), 2)
    take(B_PROJ, b_proj, (slice(0, 1),), 1)
    take(B_FC2, b_fc2, (slice(0, 1),), 1)
    for lane in range(b_fc1.shape[1] // 128):
        at = lane % lanes * 32 + B_FC1 + lane // lanes
        b_fc1[0:1, lane * 128 : (lane + 1) * 128] = sums[0, at : at + 1, :]
    end_copy.wait()
    for half in range(2):
        for lane in range(lanes):
            for i in range(images):
                section[0, half * images + i, :, lane * 128 : (lane + 1) * 128] = end_buf[half, lane, pl.ds(i, 49, stride=images), :]

    @pl.loop(start - depth, start)
    def _(c):
        give(c, fc2, 1, 0).wait()


def finish(done, sums, ends, shapes, images):
    any_space = pl.BlockSpec(memory_space=pl.ANY)
    vmem = pl.BlockSpec(memory_space=pltpu.VMEM)
    chunk, depth = done.shape[2], 6
    return pl.pallas_call(
        functools.partial(finish_kernel, images, chunk),
        out_shape=[jax.ShapeDtypeStruct(s, F32) for s in shapes],
        in_specs=[any_space, vmem, any_space],
        out_specs=[any_space] * 4 + [vmem] * 8,
        scratch_shapes=[pltpu.VMEM((depth, SIDE, chunk), BF), pltpu.VMEM((depth, SIDE, chunk), F32), pltpu.VMEM(ends.shape, F32),
                        pltpu.SemaphoreType.DMA((depth,)), pltpu.SemaphoreType.DMA((depth,)), pltpu.SemaphoreType.DMA],
        compiler_params=pltpu.CompilerParams(vmem_limit_bytes=48 * 2**20),
    )(done, sums, ends)


def on_device(section_inputs, conv_weight, conv_bias, norm_gain, norm_bias, w_qkv, w_proj, b_proj, w_fc1, b_fc1, w_fc2, b_fc2):
    n = lax.axis_size("dp")
    images, positions, width = section_inputs.shape[1:]
    half = images // 2
    spare = -(-positions * half // 16) * 16 // half - positions
    halves = jnp.pad(section_inputs.reshape(2, half, positions, width), ((0, 0), (0, 0), (0, spare), (0, 0)))
    halves = jnp.swapaxes(halves, 1, 2).reshape(2, -1, width)
    small = (conv_weight[0], conv_bias[0], norm_gain[0], norm_bias[0], b_proj, b_fc1, b_fc2)
    ends, done, sums = section(halves, small, (w_qkv[0], w_proj[0], w_fc1[0], w_fc2[0]), half, n)
    shapes = [a.shape for a in (w_fc2, w_fc1, w_proj, w_qkv, conv_weight, conv_bias, norm_gain, norm_bias, b_proj, b_fc1, b_fc2, section_inputs)]
    fc2, fc1, proj, qkv, conv_w, conv_b, gain, shift, g_proj, g_fc1, g_fc2, section_ends = finish(done, sums, ends, shapes, half)
    return section_ends, conv_w, conv_b, gain, shift, qkv, proj, g_proj, fc1, g_fc1, fc2, g_fc2


def solution(mesh):
    return jax.shard_map(
        on_device,
        mesh=mesh,
        in_specs=(
            P("pipe", "dp", None, None),
            P("pipe", None, None, None),
            P("pipe", None, None),
            P("pipe", None, None),
            P("pipe", None, None),
            P("pipe", None, None),
            P("pipe", None, None),
            P("pipe", None),
            P("pipe", None, None),
            P("pipe", None),
            P("pipe", None, None),
            P("pipe", None),
        ),
        out_specs=(
            P("pipe", "dp", None, None),
            P("pipe", None, None, None),
            P("pipe", None, None),
            P("pipe", None, None),
            P("pipe", None, None),
            P("pipe", None, None),
            P("pipe", None, None),
            P("pipe", None),
            P("pipe", None, None),
            P("pipe", None),
            P("pipe", None, None),
            P("pipe", None),
        ),
        check_vma=False,
    )
```

```python
import functools

import jax
import jax.numpy as jnp
from jax import lax
from jax.experimental import pallas as pl
from jax.experimental.pallas import tpu as pltpu
from jax.sharding import PartitionSpec as P

MESH = pl.DeviceIdType.MESH
SIDE = 768


HEAD = 32
GROUP = 256
SLOT = 64
BF = jnp.bfloat16
F32 = jnp.float32


def cols(j, width=GROUP):
    return pl.ds(pl.multiple_of(j * width, width), width)


def dot(a, b):
    return lax.dot_general(a, b, (((1,), (0,)), ((), ())), preferred_element_type=F32)


def dot_t(a, b):
    return lax.dot_general(a, b, (((1,), (1,)), ((), ())), preferred_element_type=F32)


def t_dot(a, b):
    return lax.dot_general(a, b, (((0,), (0,)), ((), ())), preferred_element_type=F32)


def fill_swap(ref, images):
    rows, columns = ref.shape
    block = 128

    @pl.loop(0, rows // block)
    def _(b):
        r = lax.broadcasted_iota(jnp.int32, (block, columns), 0) + b * block
        c = lax.broadcasted_iota(jnp.int32, (block, columns), 1)
        image, position = lax.div(r, SLOT), lax.rem(r, SLOT)
        hit = (c == position * images + image) & (position < 49)
        ref[pl.ds(pl.multiple_of(b * block, block), block), :] = jnp.where(hit, 1.0, 0.0).astype(BF)


def clear_border(pad, images):
    zero = jnp.zeros((9 * images, pad.shape[1]), pad.dtype)
    pad[0 : 9 * images, :] = zero
    pad[72 * images : 81 * images, :] = zero
    one = jnp.zeros((images, pad.shape[1]), pad.dtype)

    @pl.loop(1, 8)
    def _(r):
        pad[pl.ds(pl.multiple_of(r * 9 * images, 8), images), :] = one
        pad[pl.ds(pl.multiple_of((r * 9 + 8) * images, 8), images), :] = one


def head_mask(rows_per, count, lanes):
    shape = (count * rows_per, lanes)
    r = lax.broadcasted_iota(jnp.int32, shape, 0)
    c = lax.broadcasted_iota(jnp.int32, shape, 1)
    return lax.div(r, rows_per) == lax.div(c, HEAD)


def spread_heads(x, mask):
    count = mask.shape[0] // x.shape[0]
    return jnp.where(mask, jnp.concatenate([x] * count, axis=0), jnp.zeros((), x.dtype))


def fold_heads(x, mask, rows_per):
    kept = jnp.where(mask, x, 0.0)
    total = kept[0:rows_per]
    for h in range(1, x.shape[0] // rows_per):
        total = total + kept[h * rows_per : (h + 1) * rows_per]
    return total


def soft_down(scores, valid):
    if valid < scores.shape[0]:
        r = lax.broadcasted_iota(jnp.int32, scores.shape, 0)
        scores = jnp.where(r < valid, scores, -jnp.inf)
    e = jnp.exp(scores - jnp.max(scores, axis=0, keepdims=True))
    return e / jnp.sum(e, axis=0, keepdims=True)


def gelu_both(x):
    half = 0.5 + 0.5 * lax.erf(x * 0.7071067811865476)
    return x * half, half + x * (0.3989422804014327 * jnp.exp(-0.5 * x * x))


def dp_dims(n):
    sizes = [1, 1, 1]
    at = 0
    left = n
    while left > 1:
        factor = 2 if left % 2 == 0 else left
        sizes[at % 3] *= factor
        left //= factor
        at += 1
    return tuple(sizes), (sizes[1] * sizes[2], sizes[2], 1)


class Place:
    def __init__(self, dp, size, stride):
        self.size = size
        pos = lax.rem(lax.div(dp, stride), size)
        low = pos < (size + 1) // 2
        self.outer = jnp.where(low, pos, size - 1 - pos)
        self.low = low
        step = jnp.where(low, stride, -stride)
        self.inner_peer = dp + step
        self.outer_peer = dp - step


def pick(flag, a, b):
    out = object.__new__(Place)
    out.size = a.size
    for name in ("low", "outer", "inner_peer", "outer_peer"):
        setattr(out, name, jnp.where(flag, getattr(a, name), getattr(b, name)))
    return out


class Shape:
    def __init__(self, rows, dims):
        s0, s1, s2 = dims[0]
        self.sizes = (s2, s0, s1)
        first = rows // s2
        mid = [first // s0] * s0
        tails = sorted(set(mid), reverse=True) if s0 == 4 else [mid[0]]

        def cut(parts):
            return [sum(parts[:j]) for j in range(len(parts) + 1)]
        self.cuts = ([cut([first] * s2)], [cut(mid)], [cut([tail // s1] * s1) for tail in tails])
        self.starts, total = [], 0
        for n, lists in zip(self.sizes, self.cuts):
            self.starts.append(total)
            at = lists[0]
            total += 0 if n == 1 else at[1] if n == 2 else at[4] + at[1]
        self.land = total
        self.events, self.first_event = 0, []
        for n in self.sizes * 2:
            self.first_event.append(self.events)
            self.events += {1: 0, 2: 1, 4: 4}[n]


class Ring:
    def __init__(self, dp, dims, shape, grad, land, out, out_at, send, recv, local):
        (s0, s1, s2), (t0, t1, t2) = dims
        self.mids = Place(dp, s0, t0)
        self.fast, self.slow = Place(dp, s2, t2), Place(dp, s1, t1)
        self.grad, self.land, self.out, self.out_at = grad, land, out, out_at
        self.grads, self.lands = grad.shape[0], land.shape[0]
        self.send, self.recv, self.local = send, recv, local
        self.shape, self.sizes, self.cuts = shape, shape.sizes, shape.cuts

    def level(self, c, i):
        if i == 1:
            return self.mids
        flag = lax.rem(c + lax.axis_index("pipe"), 2) == 0
        return pick(flag, self.fast, self.slow) if i == 0 else pick(flag, self.slow, self.fast)

    def each(self, i, do):
        if len(self.cuts[i]) == 1:
            do(0)
        else:
            for v in range(2):
                pl.when(self.mids.outer == v)(functools.partial(do, v))

    def own(self, c, i, v):
        place, at = self.level(c, i), self.cuts[i][v]
        near = jnp.where(place.low, at[0], at[-1] - at[1])
        if place.size != 4:
            return near
        return jnp.where(place.outer == 0, near, jnp.where(place.low, at[1], at[-1] - at[2]))

    def base(self, c, i):
        start = 0
        for j in range(i):
            start = start + self.own(c, j, 0)
        return start

    def span(self, c, i, v, a, b):
        at = self.cuts[i][v]
        start = self.base(c, i) + jnp.where(self.level(c, i).low, at[a], at[-1] - at[b])
        return pl.ds(pl.multiple_of(start, 8), at[b] - at[a])

    def mine(self, c, rows):
        return self.grad.at[lax.rem(c, self.grads), rows]

    def landing(self, c, i, at, length):
        return self.land.at[lax.rem(c, self.lands), pl.ds(self.shape.starts[i] + at, length)]

    def copy(self, c, ev, src, dst, peer):
        return pltpu.make_async_remote_copy(
            src_ref=src, dst_ref=dst, send_sem=self.send.at[c, ev], recv_sem=self.recv.at[c, ev],
            device_id={"dp": peer}, device_id_type=MESH)

    def add(self, c, i, v, a, b, at):
        rows = self.span(c, i, v, a, b)
        slot = lax.rem(c, self.grads)
        self.grad[slot, rows] = self.grad[slot, rows] + self.landing(c, i, at, rows.size)[...]

    def give(self, c, i, v, ev, a, b, at, peer):
        rows = self.span(c, i, v, a, b)
        return self.copy(c, ev, self.mine(c, rows), self.landing(c, i, at, rows.size), peer)

    def reduce_stages(self, i):
        n = self.sizes[i]
        ev = self.shape.first_event[i]
        if n == 1:
            return []
        if n == 2:
            def first(c):
                self.each(i, lambda v: self.give(c, i, v, ev, 1, 2, 0, self.level(c, i).inner_peer).start())

            def last(c):
                def do(v):
                    self.give(c, i, v, ev, 0, 1, 0, self.level(c, i).inner_peer).wait_recv()
                    self.add(c, i, v, 0, 1, 0)
                self.each(i, do)
            return [first, last]
        length = self.cuts[i][0][1]

        def zero(c):
            place = self.level(c, i)

            @pl.when(place.outer == 0)
            def _():
                self.give(c, i, 0, ev, 2, 4, 0, place.inner_peer).start()

        def one(c):
            place = self.level(c, i)

            @pl.when(place.outer == 0)
            def _():
                self.give(c, i, 0, ev + 1, 1, 2, 2 * length, place.inner_peer).start()

            @pl.when(place.outer == 1)
            def _():
                self.give(c, i, 0, ev, 2, 4, 0, place.inner_peer).wait_recv()
                self.add(c, i, 0, 2, 4, 0)
                self.give(c, i, 0, ev + 2, 3, 4, 3 * length, place.inner_peer).start()

        def two(c):
            place = self.level(c, i)

            @pl.when(place.outer == 1)
            def _():
                self.give(c, i, 0, ev + 2, 0, 1, 3 * length, place.inner_peer).wait_recv()
                self.add(c, i, 0, 0, 1, 3 * length)
                self.give(c, i, 0, ev, 0, 1, 3 * length, place.outer_peer).start()
                self.give(c, i, 0, ev + 3, 2, 3, 4 * length, place.inner_peer).start()

        def three(c):
            place = self.level(c, i)

            @pl.when(place.outer == 0)
            def _():
                self.give(c, i, 0, ev, 0, 1, 3 * length, place.inner_peer).wait_recv()
                self.add(c, i, 0, 0, 1, 3 * length)

            @pl.when(place.outer == 1)
            def _():
                self.give(c, i, 0, ev + 1, 1, 2, 2 * length, place.inner_peer).wait_recv()
                self.add(c, i, 0, 1, 2, 2 * length)
                self.give(c, i, 0, ev + 3, 1, 2, 4 * length, place.inner_peer).wait_recv()
                self.add(c, i, 0, 1, 2, 4 * length)
        return [zero, one, two, three]

    def reduce_ends(self, c):
        for i in range(3):
            n, place = self.sizes[i], self.level(c, i)
            ev = self.shape.first_event[i]
            if n == 2:
                self.each(i, lambda v: self.give(c, i, v, ev, 1, 2, 0, place.inner_peer).wait_send())
            elif n == 4:
                @pl.when(place.outer == 0)
                def _():
                    self.give(c, i, 0, ev, 2, 4, 0, place.inner_peer).wait_send()
                    self.give(c, i, 0, ev + 1, 1, 2, 0, place.inner_peer).wait_send()

                @pl.when(place.outer == 1)
                def _():
                    self.give(c, i, 0, ev + 2, 3, 4, 0, place.inner_peer).wait_send()
                    self.give(c, i, 0, ev, 0, 1, 0, place.outer_peer).wait_send()
                    self.give(c, i, 0, ev + 3, 2, 3, 0, place.inner_peer).wait_send()

    def spread(self, c, i, v, ev, a, b, peer):
        dst = self.out.at[self.out_at(c), self.span(c, i, v, a, b)]
        return self.copy(c, ev, dst, dst, peer)

    def gather_stages(self, i):
        n = self.sizes[i]
        ev = self.shape.first_event[3 + i]
        if n == 1:
            return []
        if n == 2:
            def first(c):
                self.each(i, lambda v: self.spread(c, i, v, ev, 0, 1, self.level(c, i).inner_peer).start())

            def last(c):
                self.each(i, lambda v: self.spread(c, i, v, ev, 1, 2, self.level(c, i).inner_peer).wait_recv())
            return [first, last]

        def zero(c):
            place = self.level(c, i)

            @pl.when(place.outer == 0)
            def _():
                self.spread(c, i, 0, ev, 0, 1, place.inner_peer).start()

            @pl.when(place.outer == 1)
            def _():
                self.spread(c, i, 0, ev + 2, 1, 2, place.inner_peer).start()
                self.spread(c, i, 0, ev, 1, 2, place.outer_peer).start()

        def one(c):
            place = self.level(c, i)

            @pl.when(place.outer == 1)
            def _():
                self.spread(c, i, 0, ev, 0, 1, place.outer_peer).wait_recv()
                self.spread(c, i, 0, ev + 3, 0, 1, place.inner_peer).start()

        def two(c):
            place = self.level(c, i)

            @pl.when(place.outer == 1)
            def _():
                self.spread(c, i, 0, ev + 2, 2, 3, place.inner_peer).wait_recv()
                self.spread(c, i, 0, ev + 3, 3, 4, place.inner_peer).wait_recv()
                self.spread(c, i, 0, ev + 1, 2, 4, place.outer_peer).start()

        def three(c):
            place = self.level(c, i)

            @pl.when(place.outer == 0)
            def _():
                self.spread(c, i, 0, ev, 1, 2, place.inner_peer).wait_recv()
                self.spread(c, i, 0, ev + 1, 2, 4, place.inner_peer).wait_recv()
        return [zero, one, two, three]

    def gather_ends(self, c):
        for i in range(3):
            n, place = self.sizes[i], self.level(c, i)
            ev = self.shape.first_event[3 + i]
            if n == 2:
                self.each(i, lambda v: self.spread(c, i, v, ev, 0, 1, place.inner_peer).wait_send())
            elif n == 4:
                @pl.when(place.outer == 0)
                def _():
                    self.spread(c, i, 0, ev, 0, 1, place.inner_peer).wait_send()

                @pl.when(place.outer == 1)
                def _():
                    self.spread(c, i, 0, ev + 2, 1, 2, place.inner_peer).wait_send()
                    self.spread(c, i, 0, ev, 1, 2, place.outer_peer).wait_send()
                    self.spread(c, i, 0, ev + 3, 0, 1, place.inner_peer).wait_send()
                    self.spread(c, i, 0, ev + 1, 2, 4, place.outer_peer).wait_send()

    def settle(self, c):
        def do(v):
            at = self.cuts[2][v]
            rows = pl.ds(pl.multiple_of(self.base(c, 2) + self.own(c, 2, v), 8), at[1])
            copy = pltpu.make_async_copy(self.mine(c, rows), self.out.at[self.out_at(c), rows], self.local)
            copy.start()
            copy.wait()
        self.each(2, do)

    def stages(self, first, second, last):
        groups = [self.reduce_stages(0), self.reduce_stages(1), self.reduce_stages(2), [self.settle],
                  self.gather_stages(2), self.gather_stages(1), self.gather_stages(0), [last]]
        joined = [[first], [second]]
        for group in groups:
            if group:
                joined[-1].append(group[0])
                joined += [[stage] for stage in group[1:]]
        return [functools.partial(run_all, stages) for stages in joined]

    def greet(self):
        barrier = pltpu.get_barrier_semaphore()
        pl.semaphore_signal(barrier, inc=1, device_id={"pipe": 1 - lax.axis_index("pipe")}, device_id_type=MESH)
        count = jnp.int32(1)
        for place in (self.fast, self.mids, self.slow):
            if place.size == 1:
                continue
            pl.semaphore_signal(barrier, inc=1, device_id={"dp": place.inner_peer}, device_id_type=MESH)
            count = count + 1
            if place.size == 4:
                @pl.when(place.outer == 1)
                def _():
                    pl.semaphore_signal(barrier, inc=1, device_id={"dp": place.outer_peer}, device_id_type=MESH)
                count = count + jnp.where(place.outer == 1, 1, 0)
        pl.semaphore_wait(barrier, count)


def run_all(stages, c):
    for stage in stages:
        stage(c)


def spatial_forward(packed, mixed, soft, images):
    width = mixed.shape[1]

    @pl.loop(0, images, unroll=4)
    def _(i):
        rows = pl.ds(pl.multiple_of(i * SLOT, SLOT), SLOT)
        mask = head_mask(SLOT, GROUP // HEAD, GROUP)
        for g in range(width // GROUP):
            q, k, v = (packed[rows, part * width + g * GROUP : part * width + (g + 1) * GROUP] for part in range(3))
            weights = soft_down(dot_t(k, spread_heads(q, mask)), 49).astype(BF)
            soft[i, g] = weights
            mixed[rows, g * GROUP : (g + 1) * GROUP] = fold_heads(t_dot(weights, v), mask, SLOT).astype(BF)


def channel_forward(packed, mixed, soft, images):
    width = mixed.shape[1]

    @pl.loop(0, images, unroll=4)
    def _(i):
        rows = pl.ds(pl.multiple_of(i * SLOT, SLOT), SLOT)
        mask = head_mask(HEAD, 128 // HEAD, 128)
        for g in range(width // 128):
            q, k, v = (packed[rows, part * width + g * 128 : part * width + (g + 1) * 128] for part in range(3))
            weights = soft_down(fold_heads(t_dot(k, q), mask, HEAD), HEAD).astype(BF)
            soft[i, g // 2, g % 2 * HEAD : (g % 2 + 1) * HEAD, 0:128] = weights
            mixed[rows, g * 128 : (g + 1) * 128] = dot(v, spread_heads(weights, mask)).astype(BF)


def spatial_backward(packed, made, grad_mixed, soft, start, stop):
    width = grad_mixed.shape[1]

    @pl.loop(start, stop, unroll=stop - start)
    def _(i):
        rows = pl.ds(pl.multiple_of(i * SLOT, SLOT), SLOT)
        mask = head_mask(SLOT, GROUP // HEAD, GROUP)
        for g in range(width // GROUP):
            at = [slice(part * width + g * GROUP, part * width + (g + 1) * GROUP) for part in range(3)]
            q, k, v = (packed[rows, a] for a in at)
            weights = soft[i, g]
            out_spread = spread_heads(grad_mixed[rows, g * GROUP : (g + 1) * GROUP], mask)
            w = weights.astype(F32)
            dw = dot_t(v, out_spread)
            ds = (w * (dw - jnp.sum(dw * w, axis=0, keepdims=True))).astype(BF)
            made[rows, at[2]] = dot(weights, out_spread).astype(BF)
            made[rows, at[1]] = dot(ds, spread_heads(q, mask)).astype(BF)
            made[rows, at[0]] = (fold_heads(t_dot(ds, k), mask, SLOT) * HEAD ** -0.5).astype(BF)


def channel_backward(packed, made, grad_mixed, soft, start, stop):
    width = grad_mixed.shape[1]

    @pl.loop(start, stop, unroll=stop - start)
    def _(i):
        rows = pl.ds(pl.multiple_of(i * SLOT, SLOT), SLOT)
        mask = head_mask(HEAD, 128 // HEAD, 128)
        for g in range(width // 128):
            at = [slice(part * width + g * 128, part * width + (g + 1) * 128) for part in range(3)]
            q, k, v = (packed[rows, a] for a in at)
            weights = soft[i, g // 2, g % 2 * HEAD : (g % 2 + 1) * HEAD, 0:128]
            do = grad_mixed[rows, g * 128 : (g + 1) * 128]
            w = weights.astype(F32)
            dw = fold_heads(t_dot(v, do), mask, HEAD)
            ds = spread_heads((w * (dw - jnp.sum(dw * w, axis=0, keepdims=True))).astype(BF), mask)
            made[rows, at[2]] = dot_t(do, spread_heads(weights, mask)).astype(BF)
            made[rows, at[1]] = dot_t(q, ds).astype(BF)
            made[rows, at[0]] = (dot(k, ds) * HEAD ** -0.5).astype(BF)


def encode(pad, kernel, bias, out, images):
    @pl.loop(0, pad.shape[1] // 128)
    def _(lane):
        ls = cols(lane, 128)
        taps = [jnp.broadcast_to(kernel(t, ls), (images, 128)) for t in range(9)]
        shift = jnp.broadcast_to(bias(ls), (images, 128))

        @pl.loop(0, 7, unroll=7)
        def _(r):
            for c in range(7):
                total = shift
                for t in range(9):
                    at = pl.multiple_of(((r + t // 3) * 9 + c + t % 3) * images, 8)
                    piece = pad[pl.ds(at, images), ls]
                    total = total + piece * taps[t]
                    if t == 4:
                        total = total + piece
                out[pl.ds(pl.multiple_of((r * 7 + c) * images, 8), images), ls] = total


def normalise(stream, gain, bias, out):
    @pl.loop(0, stream.shape[0] // 16, unroll=5)
    def _(p):
        rows = pl.ds(pl.multiple_of(p * 16, 16), 16)
        s = stream[rows, :]
        centered = s - jnp.mean(s, axis=-1, keepdims=True)
        spread = jnp.mean(centered * centered, axis=-1, keepdims=True)
        out[rows, :] = (centered * lax.rsqrt(spread + 1e-5) * gain + bias).astype(BF)


def encode_back(gpad, given, kernel, out, put, first_row, bias_row, images):
    @pl.loop(0, gpad.shape[1] // 128)
    def _(lane):
        ls = cols(lane, 128)
        taps = [jnp.broadcast_to(kernel(8 - t, ls), (images, 128)) for t in range(9)]

        def row(r, totals):
            totals = list(totals)
            for c in range(7):
                at = pl.ds(pl.multiple_of((r * 7 + c) * images, 8), images)
                source = given[at, ls]
                total = None
                for t in range(9):
                    near = pl.ds(pl.multiple_of(((r + t // 3) * 9 + c + t % 3) * images, 8), images)
                    piece = gpad[near, ls]
                    if t == 4:
                        totals[9] = totals[9] + piece
                        total = total + piece
                    total = piece * taps[t] if total is None else total + piece * taps[t]
                    totals[8 - t] = totals[8 - t] + source * piece
                out[at, ls] = total
            return tuple(totals)
        totals = lax.fori_loop(0, 7, row, (jnp.zeros((images, 128), F32),) * 10, unroll=True)
        for t in range(9):
            put(first_row + t, lane, jnp.sum(totals[t], axis=0, keepdims=True))
        put(bias_row, lane, jnp.sum(totals[9], axis=0, keepdims=True))


def normalise_back(stream, grad, base, gain, gpad, put, gain_row, shift_row, acc, images):
    acc[...] = jnp.zeros_like(acc)

    @pl.loop(0, 49, unroll=7)
    def _(p):
        rows = pl.ds(pl.multiple_of(p * images, 8), images)
        s, dy = stream[rows, :], grad[rows, :]
        centered = s - jnp.mean(s, axis=-1, keepdims=True)
        rate = lax.rsqrt(jnp.mean(centered * centered, axis=-1, keepdims=True) + 1e-5)
        unit = centered * rate
        acc[0] += dy * unit
        acc[1] += dy
        dg = dy * gain
        m1 = jnp.mean(dg, axis=-1, keepdims=True)
        m2 = jnp.mean(dg * unit, axis=-1, keepdims=True)
        at = ((lax.div(p, 7) + 1) * 9 + lax.rem(p, 7) + 1) * images
        gpad[pl.ds(pl.multiple_of(at, 8), images), :] = base[rows, :] + rate * (dg - m1 - unit * m2)
    for row, total in ((gain_row, acc[0]), (shift_row, acc[1])):
        total = jnp.sum(total, axis=0, keepdims=True)
        for lane in range(total.shape[1] // 128):
            put(row, lane, total[:, lane * 128 : (lane + 1) * 128])


def fill_pad(pad, source, images):
    @pl.loop(0, 7)
    def _(r):
        inner = pl.ds(pl.multiple_of(((r + 1) * 9 + 1) * images, 8), 7 * images)
        pad[inner, :] = source[pl.ds(pl.multiple_of(r * 7 * images, 8), 7 * images), :]


CONV, CONV_BIAS, GAIN, SHIFT, B_PROJ, B_FC1, B_FC2 = 0, 18, 20, 22, 24, 25, 29
HIDDEN, COT, N2, PRE, MIXED, ATT, N1, PACKED = 0, 4, 5, 6, 10, 11, 12, 13
SEGMENTS = 12


def section_kernel(images, dims, shapes, rows, lags, beat, chunk,
                   halves, conv_w, conv_b, gain, shift, b_proj, b_fc1, b_fc2, w_qkv, w_proj, w_fc1, w_fc2,
                   ends, out, small_out, acts, k_one, k_mid, k_two, k_packed, k_soft, k_slope, x_qkv, x_proj, x_fc1, x_fc2,
                   v_qkv, v_proj, v_fc1, v_fc2, params, xb, cot, pad, one, stream, gmid, gn, packed, soft, slope, hidden,
                   swap, gm_s, n1, n2, mixed, gatt, acc, small_grad, small_pair,
                   grad, land, pair_out, pair_in, small_land, left_buf, right_buf,
                   load, store, push_send, push_recv, fetch_sem, pair_send, pair_recv, send, recv, local, ssend, srecv, slocal,
                   bring_send, bring_recv):
    pipe, dp = lax.axis_index("pipe"), lax.axis_index("dp")
    other = 1 - pipe
    first = pipe == 0
    tokens, width = gn.shape
    wide = v_fc1.shape[1]
    real = 49 * images
    per = SIDE // (2 * chunk)
    block_pairs = SEGMENTS * per
    pairs = 2 * block_pairs
    weights = ((w_qkv, x_qkv, v_qkv), (w_proj, x_proj, v_proj), (w_fc1, x_fc1, v_fc1), (w_fc2, x_fc2, v_fc2))
    QKV, PROJ, FC1, FC2 = range(4)

    def to_core(at, src, dst):
        return pltpu.make_async_remote_copy(src_ref=src, dst_ref=dst, send_sem=push_send.at[at], recv_sem=push_recv.at[at],
                                            device_id={"pipe": other}, device_id_type=MESH)
    push_params = to_core(0, params.at[pipe], params.at[pipe])
    push_x = to_core(1, halves.at[1], xb.at[0])
    push_cot = to_core(1, halves.at[0], cot)
    push_weights = [to_core(2 + at, own, far) for at, (own, far, _) in enumerate(weights)]
    push_result = to_core(6, gn, ends.at[0])
    push_grad = to_core(6, gmid, ends.at[1])

    def load_weight(b, at, fresh):
        own, far, near = weights[at]

        @pl.when(b == pipe)
        def _():
            pltpu.make_async_copy(own, near, load.at[at]).start()

        @pl.when(b != pipe)
        def _():
            if fresh:
                push_weights[at].wait_recv()
            pltpu.make_async_copy(far, near, load.at[at]).start()

    def wait_weight(at):
        own, _, near = weights[at]
        pltpu.make_async_copy(own, near, load.at[at]).wait()

    def keep(at, src, dst):
        return pltpu.make_async_copy(src, dst, store.at[at])

    def block_stores(b):
        return [keep(0, one, k_one.at[b]), keep(1, gmid, k_mid.at[b]), keep(2, stream, k_two.at[b]), keep(3, packed, k_packed.at[b]),
                keep(4, soft, k_soft.at[b]), keep(5, slope, k_slope.at[b]), keep(6, n1, acts.at[b, N1]), keep(7, mixed, acts.at[b, MIXED]),
                keep(8, n2, acts.at[b, N2])] + [
                    keep(9 + s, hidden.at[pl.ds(0, tokens), pl.ds(s * SIDE, SIDE)], acts.at[b, HIDDEN + s]) for s in range(wide // SIDE)]

    def row_of(b, row):
        return params[b, row : row + 1, :]

    def taps_of(b, j):
        return (lambda t, ls: params[b, pl.ds(CONV + 9 * j + t, 1), ls]), (lambda ls: params[b, pl.ds(CONV_BIAS + j, 1), ls])

    def block_of(k):
        return jnp.where(k < block_pairs, 1, 0)

    def number_of(k, core):
        return 2 * lax.rem(k, block_pairs) + core

    def out_at(k):
        return jnp.where(block_of(k) == pipe, number_of(k, pipe), 2 * block_pairs + lax.rem(k, block_pairs))

    main = Ring(dp, dims, shapes[0], grad, land, out, out_at, send, recv, local)
    small = Ring(dp, dims, shapes[1], small_pair, small_land, small_out, lambda c: 0, ssend, srecv, slocal)

    def slots_of(k):
        at = lax.div(lax.rem(k, block_pairs), per)
        left = jnp.where(at < 4, HIDDEN + at, jnp.where(at < 8, N2, jnp.where(at < 9, MIXED, N1)))
        right = jnp.where(at < 4, COT, jnp.where(at < 8, PRE + at - 4, jnp.where(at < 9, ATT, PACKED + at - 9)))
        return left, right, lax.rem(lax.rem(k, block_pairs), per)

    def fetches(k):
        left, right, part = slots_of(k)
        slot, b = lax.rem(k, 2), block_of(k)
        return (pltpu.make_async_copy(acts.at[b, left], left_buf.at[slot], fetch_sem.at[slot, 0]),
                pltpu.make_async_copy(acts.at[b, right, :, cols(part, 2 * chunk)], right_buf.at[slot], fetch_sem.at[slot, 1]))

    def pair_copy(k):
        return pltpu.make_async_remote_copy(
            src_ref=pair_out.at[lax.rem(k, pair_out.shape[0])], dst_ref=pair_in.at[lax.rem(k, pair_in.shape[0])],
            send_sem=pair_send.at[k], recv_sem=pair_recv.at[k], device_id={"pipe": other}, device_id_type=MESH)

    def make(k):
        for copy in fetches(k):
            copy.wait()

        @pl.when(k >= pair_out.shape[0])
        def _():
            pair_copy(k - pair_out.shape[0]).wait_send()

        @pl.when(k >= main.grads)
        def _():
            main.reduce_ends(k - main.grads)
        slot, place, far = lax.rem(k, 2), lax.rem(k, main.grads), lax.rem(k, pair_out.shape[0])
        both = t_dot(left_buf[slot], right_buf[slot]).astype(BF)

        @pl.when(first)
        def _():
            grad[place, 0:SIDE] = both[:, :chunk]
            pair_out[far] = both[:, chunk:]

        @pl.when(jnp.logical_not(first))
        def _():
            pair_out[far] = both[:, :chunk]
            grad[place, 0:SIDE] = both[:, chunk:]
        pair_copy(k).start()
        if rows > SIDE:
            grad[place, SIDE:rows] = jnp.zeros((rows - SIDE, chunk), BF)

    def join(k):
        pair_copy(k).wait_recv()
        place = lax.rem(k, main.grads)
        grad[place, 0:SIDE] = grad[place, 0:SIDE] + pair_in[lax.rem(k, pair_in.shape[0])]

    def bring(k):
        number = number_of(k, pipe)
        at = lax.rem(k, block_pairs)
        return pltpu.make_async_remote_copy(
            src_ref=out.at[out_at(k)], dst_ref=out.at[number], send_sem=bring_send.at[at], recv_sem=bring_recv.at[at],
            device_id={"pipe": other}, device_id_type=MESH)

    def hand_over(k):
        @pl.when(block_of(k) != pipe)
        def _():
            bring(k).start()

    def leave(k):
        main.gather_ends(k)

        @pl.when(block_of(k) != pipe)
        def _():
            bring(k).wait_send()

        @pl.when(block_of(k) == pipe)
        def _():
            arrival = pltpu.make_async_remote_copy(
                src_ref=out.at[number_of(k, other)], dst_ref=out.at[number_of(k, other)], send_sem=bring_send.at[lax.rem(k, block_pairs)],
                recv_sem=bring_recv.at[lax.rem(k, block_pairs)], device_id={"pipe": other}, device_id_type=MESH)
            arrival.wait_recv()
    small_copy = to_core(7, small_grad.at[other], small_pair.at[1])

    def small_make(k):
        small_copy.start()
        small_pair[0] = small_grad[pipe]

    def small_join(k):
        small_copy.wait_recv()
        small_pair[0] = small_pair[0] + small_pair[1]

    def tick(t):
        stages = main.stages(make, join, hand_over)
        small_stages = small.stages(small_make, small_join, lambda k: None)
        for s in reversed(range(len(stages))):
            since = t - lags[s]
            k = lax.div(since, beat)
            due = (since >= 0) & (lax.rem(since, beat) == 0)

            @pl.when(due & (k < pairs))
            def _():
                stages[s](k)

            @pl.when(since == pairs * beat)
            def _():
                small_stages[s](0)

    main.greet()
    for j in range(2):
        for t in range(9):
            params[pipe, CONV + 9 * j + t : CONV + 9 * j + t + 1, :] = conv_w[t, j : j + 1, :]
    for row, ref in ((CONV_BIAS, conv_b), (GAIN, gain), (SHIFT, shift), (B_PROJ, b_proj), (B_FC2, b_fc2)):
        params[pipe, row : row + ref.shape[0], :] = ref[...]
    for j in range(wide // width):
        params[pipe, B_FC1 + j : B_FC1 + j + 1, :] = b_fc1[:, j * width : (j + 1) * width]
    x_copy = pltpu.make_async_copy(halves.at[0], xb.at[0], load.at[5])
    cot_copy = pltpu.make_async_copy(halves.at[1], cot, load.at[5])
    push_params.start()

    @pl.when(first)
    def _():
        push_x.start()
        x_copy.start()

    @pl.when(jnp.logical_not(first))
    def _():
        push_cot.start()
        cot_copy.start()
    push_weights[QKV].start()
    fill_swap(swap, images)
    clear_border(pad, images)
    small_grad[...] = jnp.zeros_like(small_grad)
    one[real:tokens, :] = jnp.zeros((tokens - real, width), F32)
    stream[real:tokens, :] = jnp.zeros((tokens - real, width), F32)
    push_params.wait_recv()

    @pl.when(first)
    def _():
        x_copy.wait()

    @pl.when(jnp.logical_not(first))
    def _():
        push_x.wait_recv()

    @pl.loop(0, 2)
    def _(b):
        stores = block_stores(b)

        @pl.when(b > 0)
        def _():
            for copy in stores:
                copy.wait()
        load_weight(b, QKV, True)
        gn[...] = xb[b].astype(F32)
        fill_pad(pad, gn, images)
        kernel, bias = taps_of(b, 0)
        encode(pad, kernel, bias, one, images)
        stores[0].start()
        normalise(one, row_of(b, GAIN), row_of(b, SHIFT), n1)
        stores[6].start()

        @pl.when(b == 0)
        def _():
            push_weights[PROJ].start()
            push_weights[FC1].start()

        gm_s[...] = dot(swap[...], n1[...]).astype(BF)
        wait_weight(QKV)

        @pl.loop(0, 3)
        def _(j):
            scale = jnp.where(j == 0, HEAD ** -0.5, 1.0)
            packed[:, cols(j, width)] = (dot(gm_s[...], v_qkv[:, cols(j, width)]) * scale).astype(BF)
        stores[3].start()

        @pl.when(b == 0)
        def _():
            push_weights[FC2].start()
        load_weight(b, PROJ, True)

        @pl.when(b == 0)
        def _():
            spatial_forward(packed, gm_s, soft, images)

        @pl.when(b == 1)
        def _():
            channel_forward(packed, gm_s, soft, images)
        stores[4].start()
        load_weight(b, FC1, True)

        mixed[...] = t_dot(swap[...], gm_s[...]).astype(BF)
        stores[7].start()
        wait_weight(PROJ)

        gmid[...] = one[...] + dot(mixed[...], v_proj[...]) + row_of(b, B_PROJ)
        stores[1].start()
        fill_pad(pad, gmid, images)
        kernel, bias = taps_of(b, 1)
        encode(pad, kernel, bias, stream, images)
        stores[2].start()
        normalise(stream, row_of(b, GAIN + 1), row_of(b, SHIFT + 1), n2)
        stores[8].start()
        wait_weight(FC1)
        load_weight(b, FC2, True)

        @pl.loop(0, wide // width)
        def _(j):
            at = cols(j, width)
            value, rate = gelu_both(dot(n2[...], v_fc1[:, at]) + params[b, pl.ds(B_FC1 + j, 1), :])
            hidden[0:tokens, at] = value.astype(BF)
            slope[:, at] = rate.astype(BF)
        stores[5].start()
        for copy in stores[9:]:
            copy.start()
        wait_weight(FC2)

        gn[...] = stream[...] + dot(hidden[0:tokens, :], v_fc2[...]) + row_of(b, B_FC2)

        @pl.when(b == 0)
        def _():
            xb[1] = gn[...].astype(BF)

    end_copy = pltpu.make_async_copy(gn, ends.at[1], load.at[6])
    last_copy = pltpu.make_async_copy(gmid, ends.at[0], load.at[6])

    @pl.when(first)
    def _():
        push_result.start()
        push_cot.wait_recv()

    @pl.when(jnp.logical_not(first))
    def _():
        end_copy.start()
        cot_copy.wait()
    keep_cot = keep(13, cot, acts.at[1, COT])
    keep_cot.start()
    for copy in block_stores(1):
        copy.wait()
    keep_cot.wait()
    for copy in fetches(0):
        copy.start()

    def put(b):
        def at(row, lane, value):
            small_grad[b, pl.ds(lane * 32 + row, 1), :] = value
        return at

    loads = [pltpu.make_async_copy(k_slope.at[0], slope, load.at[7]), pltpu.make_async_copy(k_packed.at[0], packed, load.at[8]),
             pltpu.make_async_copy(k_soft.at[0], soft, load.at[9]), pltpu.make_async_copy(k_two.at[0], stream, load.at[10]),
             pltpu.make_async_copy(k_mid.at[0], gmid, load.at[11])]

    def later(b, at):
        @pl.when(b == 0)
        def _():
            loads[at].wait()

    def later_weight(b, at):
        @pl.when(b == 0)
        def _():
            wait_weight(at)

    def ahead(b, do):
        pl.when(b == 1)(do)

    def pre_part(part):
        def run(b):
            if part == 0:
                later(b, 0)
                later_weight(b, FC2)
                one[...] = cot[...].astype(F32)
            each = wide // 3
            at = slice(part * each, (part + 1) * each)
            pre = dot_t(cot[...], v_fc2[at, :]) * slope[:, at].astype(F32)
            slope[:, at] = pre.astype(BF)
            total = jnp.sum(pre, axis=0, keepdims=True)
            for piece in range(each // 128):
                lane = part * each // 128 + piece
                put(b)(B_FC1 + lane // (width // 128), lane % (width // 128), total[:, piece * 128 : (piece + 1) * 128])
            if part == 2:
                ahead(b, lambda: load_weight(0, FC2, False))
                copies = [keep(s, slope.at[:, pl.ds(s * SIDE, SIDE)], acts.at[b, PRE + s]) for s in range(wide // SIDE)]
                for copy in copies:
                    copy.start()
                for lane in range(width // 128):
                    put(b)(B_FC2, lane, jnp.sum(one[:, lane * 128 : (lane + 1) * 128], axis=0, keepdims=True))
                for copy in copies:
                    copy.wait()
        return run

    def through_fc1(b):
        @pl.when(b == 1)
        def _():
            @pl.when(first)
            def _():
                push_result.wait_send()

            @pl.when(jnp.logical_not(first))
            def _():
                end_copy.wait()
        later_weight(b, FC1)

        gn[...] = dot_t(slope[...], v_fc1[...])
        ahead(b, lambda: load_weight(0, FC1, False))

    def through_second(b):
        later(b, 3)
        normalise_back(stream, gn, one, row_of(b, GAIN + 1), pad, put(b), GAIN + 1, SHIFT + 1, acc, images)
        pltpu.make_async_copy(k_one.at[b], stream, load.at[12]).start()
        later(b, 4)
        encode_back(pad, gmid, taps_of(b, 1)[0], gmid, put(b), CONV + 9, CONV_BIAS + 1, images)
        gmid[real:tokens, :] = jnp.zeros((tokens - real, width), F32)
        for lane in range(width // 128):
            part = gmid[:, lane * 128 : (lane + 1) * 128]
            put(b)(B_PROJ, lane, jnp.sum(part, axis=0, keepdims=True))
            gatt[:, lane * 128 : (lane + 1) * 128] = part.astype(BF)
        keep(4, gatt, acts.at[b, ATT]).start()

    def through_proj(b):
        later_weight(b, PROJ)

        n2[...] = dot_t(gatt[...], v_proj[...]).astype(BF)
        ahead(b, lambda: load_weight(0, PROJ, False))
        gm_s[...] = dot(swap[...], n2[...]).astype(BF)
        later(b, 1)
        later(b, 2)

    def through_mix(part):
        def run(b):
            each = images // 2

            @pl.when(b == 0)
            def _():
                spatial_backward(packed, hidden, gm_s, soft, part * each, (part + 1) * each)

            @pl.when(b == 1)
            def _():
                channel_backward(packed, hidden, gm_s, soft, part * each, (part + 1) * each)
            if part == 1:
                keep(4, gatt, acts.at[b, ATT]).wait()
        return run

    def unswap(b):
        @pl.loop(0, 3)
        def _(j):
            slope[:, cols(j, width)] = t_dot(swap[...], hidden[:, cols(j, width)]).astype(BF)
        copies = [keep(s, slope.at[:, pl.ds(s * SIDE, SIDE)], acts.at[b, PACKED + s]) for s in range(3)]
        for copy in copies:
            copy.start()
        for copy in copies:
            copy.wait()

    def through_qkv(b):
        later_weight(b, QKV)

        gn[...] = dot_t(slope[:, 0 : 3 * width], v_qkv[...])

        def prepare():
            load_weight(0, QKV, False)
            for at in range(3):
                loads[at].start()
        ahead(b, prepare)

    def through_first(b):
        pltpu.make_async_copy(k_one.at[b], stream, load.at[12]).wait()
        normalise_back(stream, gn, gmid, row_of(b, GAIN), pad, put(b), GAIN, SHIFT, acc, images)
        ahead(b, lambda: loads[3].start())

    def finish(b):
        gn[...] = xb[b].astype(F32)
        encode_back(pad, gn, taps_of(b, 0)[0], gmid, put(b), CONV, CONV_BIAS, images)

        @pl.when(b == 1)
        def _():
            cot[...] = gmid[...].astype(BF)
            copy = keep(5, cot, acts.at[0, COT])
            copy.start()
            loads[4].start()
            copy.wait()

        @pl.when((b == 0) & first)
        def _():
            last_copy.start()

        @pl.when((b == 0) & jnp.logical_not(first))
        def _():
            push_grad.start()
    segments = [pre_part(0), pre_part(1), pre_part(2), through_fc1, through_second, through_proj, through_mix(0), through_mix(1),
                unswap, through_qkv, through_first, finish]

    @pl.loop(0, pairs * beat + 1 + lags[-1])
    def _(t):
        tick(t)
        since = t - lags[-1] - 1
        k = lax.div(t, beat)
        on_beat = (lax.rem(t, beat) == 0) & (k < pairs)

        @pl.when((since >= 0) & (lax.rem(since, beat) == 0) & (since < pairs * beat))
        def _():
            leave(lax.div(since, beat))

        @pl.when(on_beat & (lax.rem(k, per) == 0))
        def _():
            b, at = block_of(k), lax.div(lax.rem(k, block_pairs), per)
            for number, segment in enumerate(segments):
                @pl.when(at == number)
                def _():
                    segment(b)

        @pl.when(on_beat & (k + 1 < pairs))
        def _():
            for copy in fetches(k + 1):
                copy.start()

    @pl.loop(pairs - main.grads, pairs)
    def _(k):
        main.reduce_ends(k)

    @pl.loop(pairs - pair_out.shape[0], pairs)
    def _(k):
        pair_copy(k).wait_send()

    small.reduce_ends(0)
    small.gather_ends(0)
    small_copy.wait_send()
    push_params.wait_send()
    for copy in push_weights:
        copy.wait_send()

    @pl.when(first)
    def _():
        push_x.wait_send()
        last_copy.wait()
        push_grad.wait_recv()

    @pl.when(jnp.logical_not(first))
    def _():
        push_cot.wait_send()
        push_grad.wait_send()
        push_result.wait_recv()


def section(halves, small, weights, images, n, collective_id=0):
    w_qkv, w_proj, w_fc1, w_fc2 = weights
    _, tokens, width = halves.shape
    wide = w_fc1.shape[1]
    slots = images * SLOT
    dims = dp_dims(n)
    chunk = 384 if n <= 16 else 128
    total = (wide // SIDE * 2 + 4) * SIDE // chunk
    pairs = total
    rows = -(-SIDE // (16 * n)) * 16 * n
    small_rows = 16 * n
    shapes = (Shape(rows, dims), Shape(small_rows, dims))
    events = shapes[0].events
    hops = sum(0 if s == 1 else 1 if s == 2 else 3 for s in dims[0])
    beat = 1
    gaps = [1, 2] + [1] * (2 * hops - 2) + [2]
    lags = [sum(gaps[:s]) for s in range(2 * hops + 2)]
    grads, lands = -(-lags[hops + 1] // beat) + 3, 10
    any_space = pl.BlockSpec(memory_space=pl.ANY)
    vmem = pl.BlockSpec(memory_space=pltpu.VMEM)
    soft = (images, width // GROUP, SLOT, 2 * GROUP)
    outs = [((2, tokens, width), F32), ((total + total // 2, rows, chunk), BF), ((1, small_rows, 128), F32),
            ((2, 16, tokens, SIDE), BF), ((2, tokens, width), F32), ((2, tokens, width), F32), ((2, tokens, width), F32),
            ((2, slots, 3 * width), BF), ((2, *soft), BF), ((2, tokens, wide), BF),
            (w_qkv.shape, BF), (w_proj.shape, BF), (w_fc1.shape, BF), (w_fc2.shape, BF)]
    dma = pltpu.SemaphoreType.DMA

    def plain(shape):
        return pltpu.VMEM(shape, F32)

    def low(shape):
        return pltpu.VMEM(shape, BF)
    results = pl.pallas_call(
        functools.partial(section_kernel, images, dims, shapes, rows, lags, beat, chunk),
        out_shape=[jax.ShapeDtypeStruct(*o) for o in outs],
        in_specs=[any_space] + [vmem] * 7 + [any_space] * 4,
        out_specs=[any_space] * len(outs),
        scratch_shapes=[low(w.shape) for w in weights] + [
            plain((2, 32, width)), low((2, tokens, width)), low((tokens, width)), plain((81 * images, width)),
            plain((tokens, width)), plain((tokens, width)), plain((tokens, width)), plain((tokens, width)),
            low((slots, 3 * width)), low(soft), low((tokens, wide)), low((slots, wide)),
            low((slots, tokens)), low((slots, width)), low((tokens, width)), low((tokens, width)), low((tokens, width)), low((tokens, width)),
            plain((2, images, width)), plain((2, small_rows, 128)), plain((2, small_rows, 128)),
            low((grads, rows, chunk)), low((lands, shapes[0].land, chunk)), low((4, SIDE, chunk)), low((6, SIDE, chunk)), plain((1, shapes[1].land, 128)),
            low((2, tokens, SIDE)), low((2, tokens, 2 * chunk)),
            dma((13,)), dma((14,)), dma((8,)), dma((8,)), dma((2, 2)), dma((pairs,)), dma((pairs,)),
            dma((pairs, events)), dma((pairs, events)), dma, dma((1, events)), dma((1, events)), dma, dma((pairs // 2,)), dma((pairs // 2,)),
        ],
        compiler_params=pltpu.CompilerParams(collective_id=collective_id, has_side_effects=True, vmem_limit_bytes=63 * 2**20),
    )(halves, *small, w_qkv, w_proj, w_fc1, w_fc2)
    return results[:3]


def finish_kernel(images, chunk, done, sums, ends, fc2, fc1, proj, qkv, conv_w, conv_b, gain, shift, b_proj, b_fc1, b_fc2, section,
                  low_buf, wide_buf, end_buf, section_buf, read, write, end_sem):
    depth = low_buf.shape[0]
    jobs, start = [], 0
    for dst in (fc2, fc1, proj, qkv):
        across = dst.shape[2] // chunk
        number = dst.shape[1] // SIDE * across
        jobs.append((start, number, across, dst))
        start += number
    end_copy = pltpu.make_async_copy(ends, end_buf, end_sem.at[0])
    end_copy.start()

    def get(c):
        return pltpu.make_async_copy(done.at[c, pl.ds(0, SIDE)], low_buf.at[lax.rem(c, depth)], read.at[lax.rem(c, depth)])

    def give(c, dst, across, at):
        rows = pl.ds(pl.multiple_of(lax.div(at, across) * SIDE, SIDE), SIDE)
        return pltpu.make_async_copy(wide_buf.at[lax.rem(c, depth)], dst.at[0, rows, cols(lax.rem(at, across), chunk)],
                                     write.at[lax.rem(c, depth)])

    @pl.loop(0, depth)
    def _(c):
        get(c).start()
    for begin, number, across, dst in jobs:
        @pl.loop(0, number)
        def _(at):
            c = begin + at
            slot = lax.rem(c, depth)
            get(c).wait()

            @pl.when(c >= depth)
            def _():
                give(c, dst, across, at).wait()
            for r in range(0, SIDE, 128):
                wide_buf[slot, r : r + 128] = low_buf[slot, r : r + 128].astype(F32)
            give(c, dst, across, at).start()

            @pl.when(c + depth < start)
            def _():
                get(c + depth).start()
        if begin == 0:
            end_copy.wait()
            for half in range(2):
                section_buf[:, half * images : (half + 1) * images, :] = end_buf[half, 0:49]
            section_copy = pltpu.make_async_copy(section_buf, section.at[0], end_sem.at[1])
            section_copy.start()
    lanes = fc2.shape[2] // 128
    width = fc2.shape[2]

    def take(first_row, ref, index, rows):
        for lane in range(lanes):
            ref[index + (slice(lane * 128, (lane + 1) * 128),)] = sums[0, lane * 32 + first_row : lane * 32 + first_row + rows, :]
    for j in range(2):
        for t in range(9):
            take(CONV + 9 * j + t, conv_w, (0, t, slice(j, j + 1)), 1)
    take(CONV_BIAS, conv_b, (0, slice(0, 2)), 2)
    take(GAIN, gain, (0, slice(0, 2)), 2)
    take(SHIFT, shift, (0, slice(0, 2)), 2)
    take(B_PROJ, b_proj, (slice(0, 1),), 1)
    take(B_FC2, b_fc2, (slice(0, 1),), 1)
    for lane in range(b_fc1.shape[1] // 128):
        at = lane % lanes * 32 + B_FC1 + lane // lanes
        b_fc1[0:1, lane * 128 : (lane + 1) * 128] = sums[0, at : at + 1, :]
    @pl.loop(start - depth, start)
    def _(c):
        give(c, fc2, 1, 0).wait()
    section_copy.wait()


def finish(done, sums, ends, shapes, images):
    any_space = pl.BlockSpec(memory_space=pl.ANY)
    vmem = pl.BlockSpec(memory_space=pltpu.VMEM)
    chunk, depth = done.shape[2], 6
    return pl.pallas_call(
        functools.partial(finish_kernel, images, chunk),
        out_shape=[jax.ShapeDtypeStruct(s, F32) for s in shapes],
        in_specs=[any_space, vmem, any_space],
        out_specs=[any_space] * 4 + [vmem] * 7 + [any_space],
        scratch_shapes=[pltpu.VMEM((depth, SIDE, chunk), BF), pltpu.VMEM((depth, SIDE, chunk), F32), pltpu.VMEM(ends.shape, F32),
                        pltpu.VMEM(shapes[-1][1:], F32),
                        pltpu.SemaphoreType.DMA((depth,)), pltpu.SemaphoreType.DMA((depth,)), pltpu.SemaphoreType.DMA((2,))],
        compiler_params=pltpu.CompilerParams(vmem_limit_bytes=62 * 2**20),
    )(done, sums, ends)


def on_device(section_inputs, conv_weight, conv_bias, norm_gain, norm_bias, w_qkv, w_proj, b_proj, w_fc1, b_fc1, w_fc2, b_fc2):
    n = lax.axis_size("dp")
    images, positions, width = section_inputs.shape[1:]
    half = images // 2
    spare = -(-positions * half // 16) * 16 // half - positions
    halves = jnp.pad(section_inputs.reshape(2, half, positions, width), ((0, 0), (0, 0), (0, spare), (0, 0)))
    halves = jnp.swapaxes(halves, 1, 2).reshape(2, -1, width)
    small = (jnp.swapaxes(conv_weight[0], 0, 1), conv_bias[0], norm_gain[0], norm_bias[0], b_proj, b_fc1, b_fc2)
    ends, done, sums = section(halves, small, (w_qkv[0], w_proj[0], w_fc1[0], w_fc2[0]), half, n)
    ends = ends.reshape(2, -1, half, width)
    arrays = (w_fc2, w_fc1, w_proj, w_qkv, jnp.swapaxes(conv_weight, 1, 2), conv_bias, norm_gain, norm_bias, b_proj, b_fc1, b_fc2,
              jnp.swapaxes(section_inputs, 1, 2))
    fc2, fc1, proj, qkv, conv_w, conv_b, gain, shift, g_proj, g_fc1, g_fc2, section_ends = finish(done, sums, ends, [a.shape for a in arrays], half)
    return (jnp.swapaxes(section_ends, 1, 2), jnp.swapaxes(conv_w, 1, 2), conv_b, gain, shift, qkv, proj, g_proj, fc1, g_fc1, fc2, g_fc2)


def solution(mesh):
    return jax.shard_map(
        on_device,
        mesh=mesh,
        in_specs=(
            P("pipe", "dp", None, None),
            P("pipe", None, None, None),
            P("pipe", None, None),
            P("pipe", None, None),
            P("pipe", None, None),
            P("pipe", None, None),
            P("pipe", None, None),
            P("pipe", None),
            P("pipe", None, None),
            P("pipe", None),
            P("pipe", None, None),
            P("pipe", None),
        ),
        out_specs=(
            P("pipe", "dp", None, None),
            P("pipe", None, None, None),
            P("pipe", None, None),
            P("pipe", None, None),
            P("pipe", None, None),
            P("pipe", None, None),
            P("pipe", None, None),
            P("pipe", None),
            P("pipe", None, None),
            P("pipe", None),
            P("pipe", None, None),
            P("pipe", None),
        ),
        check_vma=False,
    )
```

```python
import functools

import jax
import jax.numpy as jnp
from jax import lax
from jax.experimental import pallas as pl
from jax.experimental.pallas import tpu as pltpu
from jax.sharding import PartitionSpec as P

MESH = pl.DeviceIdType.MESH
SIDE = 768


HEAD = 32
GROUP = 256
SLOT = 64
BF = jnp.bfloat16
F32 = jnp.float32


def cols(j, width=GROUP):
    return pl.ds(pl.multiple_of(j * width, width), width)


def dot(a, b):
    return lax.dot_general(a, b, (((1,), (0,)), ((), ())), preferred_element_type=F32)


def dot_t(a, b):
    return lax.dot_general(a, b, (((1,), (1,)), ((), ())), preferred_element_type=F32)


def t_dot(a, b):
    return lax.dot_general(a, b, (((0,), (0,)), ((), ())), preferred_element_type=F32)


def fill_swap(ref, images):
    rows, columns = ref.shape
    block = 128

    @pl.loop(0, rows // block)
    def _(b):
        r = lax.broadcasted_iota(jnp.int32, (block, columns), 0) + b * block
        c = lax.broadcasted_iota(jnp.int32, (block, columns), 1)
        image, position = lax.div(r, SLOT), lax.rem(r, SLOT)
        hit = (c == position * images + image) & (position < 49)
        ref[pl.ds(pl.multiple_of(b * block, block), block), :] = jnp.where(hit, 1.0, 0.0).astype(BF)


def clear_border(pad, images):
    zero = jnp.zeros((9 * images, pad.shape[1]), pad.dtype)
    pad[0 : 9 * images, :] = zero
    pad[72 * images : 81 * images, :] = zero
    one = jnp.zeros((images, pad.shape[1]), pad.dtype)

    @pl.loop(1, 8)
    def _(r):
        pad[pl.ds(pl.multiple_of(r * 9 * images, 8), images), :] = one
        pad[pl.ds(pl.multiple_of((r * 9 + 8) * images, 8), images), :] = one


def head_mask(rows_per, count, lanes):
    shape = (count * rows_per, lanes)
    r = lax.broadcasted_iota(jnp.int32, shape, 0)
    c = lax.broadcasted_iota(jnp.int32, shape, 1)
    return lax.div(r, rows_per) == lax.div(c, HEAD)


def spread_heads(x, mask):
    count = mask.shape[0] // x.shape[0]
    return jnp.where(mask, jnp.concatenate([x] * count, axis=0), jnp.zeros((), x.dtype))


def fold_heads(x, mask, rows_per):
    kept = jnp.where(mask, x, 0.0)
    total = kept[0:rows_per]
    for h in range(1, x.shape[0] // rows_per):
        total = total + kept[h * rows_per : (h + 1) * rows_per]
    return total


def soft_down(scores, valid):
    if valid < scores.shape[0]:
        r = lax.broadcasted_iota(jnp.int32, scores.shape, 0)
        scores = jnp.where(r < valid, scores, -jnp.inf)
    e = jnp.exp(scores - jnp.max(scores, axis=0, keepdims=True))
    return e / jnp.sum(e, axis=0, keepdims=True)


def gelu_both(x):
    half = 0.5 + 0.5 * lax.erf(x * 0.7071067811865476)
    return x * half, half + x * (0.3989422804014327 * jnp.exp(-0.5 * x * x))


def dp_dims(n):
    sizes = [1, 1, 1]
    at = 0
    left = n
    while left > 1:
        factor = 2 if left % 2 == 0 else left
        sizes[at % 3] *= factor
        left //= factor
        at += 1
    return tuple(sizes), (sizes[1] * sizes[2], sizes[2], 1)


class Place:
    def __init__(self, dp, size, stride):
        self.size = size
        pos = lax.rem(lax.div(dp, stride), size)
        low = pos < (size + 1) // 2
        self.outer = jnp.where(low, pos, size - 1 - pos)
        self.low = low
        step = jnp.where(low, stride, -stride)
        self.inner_peer = dp + step
        self.outer_peer = dp - step


def pick(flag, a, b):
    out = object.__new__(Place)
    out.size = a.size
    for name in ("low", "outer", "inner_peer", "outer_peer"):
        setattr(out, name, jnp.where(flag, getattr(a, name), getattr(b, name)))
    return out


class Shape:
    def __init__(self, rows, dims):
        s0, s1, s2 = dims[0]
        self.sizes = (s2, s0, s1)
        first = rows // s2
        mid = [first // s0] * s0
        tails = sorted(set(mid), reverse=True) if s0 == 4 else [mid[0]]

        def cut(parts):
            return [sum(parts[:j]) for j in range(len(parts) + 1)]
        self.cuts = ([cut([first] * s2)], [cut(mid)], [cut([tail // s1] * s1) for tail in tails])
        self.starts, total = [], 0
        for n, lists in zip(self.sizes, self.cuts):
            self.starts.append(total)
            at = lists[0]
            total += 0 if n == 1 else at[1] if n == 2 else at[4] + at[1]
        self.land = total
        self.events, self.first_event = 0, []
        for n in self.sizes * 2:
            self.first_event.append(self.events)
            self.events += {1: 0, 2: 1, 4: 4}[n]


class Ring:
    def __init__(self, dp, dims, shape, grad, land, out, out_at, send, recv, local):
        (s0, s1, s2), (t0, t1, t2) = dims
        self.mids = Place(dp, s0, t0)
        self.fast, self.slow = Place(dp, s2, t2), Place(dp, s1, t1)
        self.grad, self.land, self.out, self.out_at = grad, land, out, out_at
        self.grads, self.lands = grad.shape[0], land.shape[0]
        self.send, self.recv, self.local = send, recv, local
        self.shape, self.sizes, self.cuts = shape, shape.sizes, shape.cuts

    def level(self, c, i):
        if i == 1:
            return self.mids
        flag = lax.rem(c + lax.axis_index("pipe"), 2) == 0
        return pick(flag, self.fast, self.slow) if i == 0 else pick(flag, self.slow, self.fast)

    def each(self, i, do):
        if len(self.cuts[i]) == 1:
            do(0)
        else:
            for v in range(2):
                pl.when(self.mids.outer == v)(functools.partial(do, v))

    def own(self, c, i, v):
        place, at = self.level(c, i), self.cuts[i][v]
        near = jnp.where(place.low, at[0], at[-1] - at[1])
        if place.size != 4:
            return near
        return jnp.where(place.outer == 0, near, jnp.where(place.low, at[1], at[-1] - at[2]))

    def base(self, c, i):
        start = 0
        for j in range(i):
            start = start + self.own(c, j, 0)
        return start

    def span(self, c, i, v, a, b):
        at = self.cuts[i][v]
        start = self.base(c, i) + jnp.where(self.level(c, i).low, at[a], at[-1] - at[b])
        return pl.ds(pl.multiple_of(start, 8), at[b] - at[a])

    def mine(self, c, rows):
        return self.grad.at[lax.rem(c, self.grads), rows]

    def landing(self, c, i, at, length):
        return self.land.at[lax.rem(c, self.lands), pl.ds(self.shape.starts[i] + at, length)]

    def copy(self, c, ev, src, dst, peer):
        return pltpu.make_async_remote_copy(
            src_ref=src, dst_ref=dst, send_sem=self.send.at[c, ev], recv_sem=self.recv.at[c, ev],
            device_id={"dp": peer}, device_id_type=MESH)

    def add(self, c, i, v, a, b, at):
        rows = self.span(c, i, v, a, b)
        slot = lax.rem(c, self.grads)
        self.grad[slot, rows] = self.grad[slot, rows] + self.landing(c, i, at, rows.size)[...]

    def give(self, c, i, v, ev, a, b, at, peer):
        rows = self.span(c, i, v, a, b)
        return self.copy(c, ev, self.mine(c, rows), self.landing(c, i, at, rows.size), peer)

    def reduce_stages(self, i):
        n = self.sizes[i]
        ev = self.shape.first_event[i]
        if n == 1:
            return []
        if n == 2:
            def first(c):
                self.each(i, lambda v: self.give(c, i, v, ev, 1, 2, 0, self.level(c, i).inner_peer).start())

            def last(c):
                def do(v):
                    self.give(c, i, v, ev, 0, 1, 0, self.level(c, i).inner_peer).wait_recv()
                    self.add(c, i, v, 0, 1, 0)
                self.each(i, do)
            return [first, last]
        length = self.cuts[i][0][1]

        def zero(c):
            place = self.level(c, i)

            @pl.when(place.outer == 0)
            def _():
                self.give(c, i, 0, ev, 2, 4, 0, place.inner_peer).start()

        def one(c):
            place = self.level(c, i)

            @pl.when(place.outer == 0)
            def _():
                self.give(c, i, 0, ev + 1, 1, 2, 2 * length, place.inner_peer).start()

            @pl.when(place.outer == 1)
            def _():
                self.give(c, i, 0, ev, 2, 4, 0, place.inner_peer).wait_recv()
                self.add(c, i, 0, 2, 4, 0)
                self.give(c, i, 0, ev + 2, 3, 4, 3 * length, place.inner_peer).start()

        def two(c):
            place = self.level(c, i)

            @pl.when(place.outer == 1)
            def _():
                self.give(c, i, 0, ev + 2, 0, 1, 3 * length, place.inner_peer).wait_recv()
                self.add(c, i, 0, 0, 1, 3 * length)
                self.give(c, i, 0, ev, 0, 1, 3 * length, place.outer_peer).start()
                self.give(c, i, 0, ev + 3, 2, 3, 4 * length, place.inner_peer).start()

        def three(c):
            place = self.level(c, i)

            @pl.when(place.outer == 0)
            def _():
                self.give(c, i, 0, ev, 0, 1, 3 * length, place.inner_peer).wait_recv()
                self.add(c, i, 0, 0, 1, 3 * length)

            @pl.when(place.outer == 1)
            def _():
                self.give(c, i, 0, ev + 1, 1, 2, 2 * length, place.inner_peer).wait_recv()
                self.add(c, i, 0, 1, 2, 2 * length)
                self.give(c, i, 0, ev + 3, 1, 2, 4 * length, place.inner_peer).wait_recv()
                self.add(c, i, 0, 1, 2, 4 * length)
        return [zero, one, two, three]

    def reduce_ends(self, c):
        for i in range(3):
            n, place = self.sizes[i], self.level(c, i)
            ev = self.shape.first_event[i]
            if n == 2:
                self.each(i, lambda v: self.give(c, i, v, ev, 1, 2, 0, place.inner_peer).wait_send())
            elif n == 4:
                @pl.when(place.outer == 0)
                def _():
                    self.give(c, i, 0, ev, 2, 4, 0, place.inner_peer).wait_send()
                    self.give(c, i, 0, ev + 1, 1, 2, 0, place.inner_peer).wait_send()

                @pl.when(place.outer == 1)
                def _():
                    self.give(c, i, 0, ev + 2, 3, 4, 0, place.inner_peer).wait_send()
                    self.give(c, i, 0, ev, 0, 1, 0, place.outer_peer).wait_send()
                    self.give(c, i, 0, ev + 3, 2, 3, 0, place.inner_peer).wait_send()

    def spread(self, c, i, v, ev, a, b, peer):
        dst = self.out.at[self.out_at(c), self.span(c, i, v, a, b)]
        return self.copy(c, ev, dst, dst, peer)

    def gather_stages(self, i):
        n = self.sizes[i]
        ev = self.shape.first_event[3 + i]
        if n == 1:
            return []
        if n == 2:
            def first(c):
                self.each(i, lambda v: self.spread(c, i, v, ev, 0, 1, self.level(c, i).inner_peer).start())

            def last(c):
                self.each(i, lambda v: self.spread(c, i, v, ev, 1, 2, self.level(c, i).inner_peer).wait_recv())
            return [first, last]

        def zero(c):
            place = self.level(c, i)

            @pl.when(place.outer == 0)
            def _():
                self.spread(c, i, 0, ev, 0, 1, place.inner_peer).start()

            @pl.when(place.outer == 1)
            def _():
                self.spread(c, i, 0, ev + 2, 1, 2, place.inner_peer).start()
                self.spread(c, i, 0, ev, 1, 2, place.outer_peer).start()

        def one(c):
            place = self.level(c, i)

            @pl.when(place.outer == 1)
            def _():
                self.spread(c, i, 0, ev, 0, 1, place.outer_peer).wait_recv()
                self.spread(c, i, 0, ev + 3, 0, 1, place.inner_peer).start()

        def two(c):
            place = self.level(c, i)

            @pl.when(place.outer == 1)
            def _():
                self.spread(c, i, 0, ev + 2, 2, 3, place.inner_peer).wait_recv()
                self.spread(c, i, 0, ev + 3, 3, 4, place.inner_peer).wait_recv()
                self.spread(c, i, 0, ev + 1, 2, 4, place.outer_peer).start()

        def three(c):
            place = self.level(c, i)

            @pl.when(place.outer == 0)
            def _():
                self.spread(c, i, 0, ev, 1, 2, place.inner_peer).wait_recv()
                self.spread(c, i, 0, ev + 1, 2, 4, place.inner_peer).wait_recv()
        return [zero, one, two, three]

    def gather_ends(self, c):
        for i in range(3):
            n, place = self.sizes[i], self.level(c, i)
            ev = self.shape.first_event[3 + i]
            if n == 2:
                self.each(i, lambda v: self.spread(c, i, v, ev, 0, 1, place.inner_peer).wait_send())
            elif n == 4:
                @pl.when(place.outer == 0)
                def _():
                    self.spread(c, i, 0, ev, 0, 1, place.inner_peer).wait_send()

                @pl.when(place.outer == 1)
                def _():
                    self.spread(c, i, 0, ev + 2, 1, 2, place.inner_peer).wait_send()
                    self.spread(c, i, 0, ev, 1, 2, place.outer_peer).wait_send()
                    self.spread(c, i, 0, ev + 3, 0, 1, place.inner_peer).wait_send()
                    self.spread(c, i, 0, ev + 1, 2, 4, place.outer_peer).wait_send()

    def settle(self, c):
        def do(v):
            at = self.cuts[2][v]
            rows = pl.ds(pl.multiple_of(self.base(c, 2) + self.own(c, 2, v), 8), at[1])
            copy = pltpu.make_async_copy(self.mine(c, rows), self.out.at[self.out_at(c), rows], self.local)
            copy.start()
            copy.wait()
        self.each(2, do)

    def stages(self, first, second, last):
        groups = [self.reduce_stages(0), self.reduce_stages(1), self.reduce_stages(2), [self.settle],
                  self.gather_stages(2), self.gather_stages(1), self.gather_stages(0), [last]]
        joined = [[first], [second]]
        for group in groups:
            if group:
                joined[-1].append(group[0])
                joined += [[stage] for stage in group[1:]]
        return [functools.partial(run_all, stages) for stages in joined]

    def greet(self):
        barrier = pltpu.get_barrier_semaphore()
        pl.semaphore_signal(barrier, inc=1, device_id={"pipe": 1 - lax.axis_index("pipe")}, device_id_type=MESH)
        count = jnp.int32(1)
        for place in (self.fast, self.mids, self.slow):
            if place.size == 1:
                continue
            pl.semaphore_signal(barrier, inc=1, device_id={"dp": place.inner_peer}, device_id_type=MESH)
            count = count + 1
            if place.size == 4:
                @pl.when(place.outer == 1)
                def _():
                    pl.semaphore_signal(barrier, inc=1, device_id={"dp": place.outer_peer}, device_id_type=MESH)
                count = count + jnp.where(place.outer == 1, 1, 0)
        pl.semaphore_wait(barrier, count)


def run_all(stages, c):
    for stage in stages:
        stage(c)


def spatial_forward(packed, mixed, soft, images):
    width = mixed.shape[1]

    @pl.loop(0, images, unroll=8)
    def _(i):
        rows = pl.ds(pl.multiple_of(i * SLOT, SLOT), SLOT)
        mask = head_mask(SLOT, GROUP // HEAD, GROUP)
        for g in range(width // GROUP):
            q, k, v = (packed[rows, part * width + g * GROUP : part * width + (g + 1) * GROUP] for part in range(3))
            weights = soft_down(dot_t(k, spread_heads(q, mask)), 49).astype(BF)
            soft[i, g] = weights
            mixed[rows, g * GROUP : (g + 1) * GROUP] = fold_heads(t_dot(weights, v), mask, SLOT).astype(BF)


def channel_forward(packed, mixed, soft, images):
    width = mixed.shape[1]

    @pl.loop(0, images, unroll=8)
    def _(i):
        rows = pl.ds(pl.multiple_of(i * SLOT, SLOT), SLOT)
        mask = head_mask(HEAD, 128 // HEAD, 128)
        for g in range(width // 128):
            q, k, v = (packed[rows, part * width + g * 128 : part * width + (g + 1) * 128] for part in range(3))
            weights = soft_down(fold_heads(t_dot(k, q), mask, HEAD), HEAD).astype(BF)
            soft[i, g // 2, g % 2 * HEAD : (g % 2 + 1) * HEAD, 0:128] = weights
            mixed[rows, g * 128 : (g + 1) * 128] = dot(v, spread_heads(weights, mask)).astype(BF)


def spatial_backward(packed, made, grad_mixed, soft, start, stop):
    width = grad_mixed.shape[1]

    @pl.loop(start, stop, unroll=stop - start)
    def _(i):
        rows = pl.ds(pl.multiple_of(i * SLOT, SLOT), SLOT)
        mask = head_mask(SLOT, GROUP // HEAD, GROUP)
        for g in range(width // GROUP):
            at = [slice(part * width + g * GROUP, part * width + (g + 1) * GROUP) for part in range(3)]
            q, k, v = (packed[rows, a] for a in at)
            weights = soft[i, g]
            out_spread = spread_heads(grad_mixed[rows, g * GROUP : (g + 1) * GROUP], mask)
            w = weights.astype(F32)
            dw = dot_t(v, out_spread)
            ds = (w * (dw - jnp.sum(dw * w, axis=0, keepdims=True))).astype(BF)
            made[rows, at[2]] = dot(weights, out_spread).astype(BF)
            made[rows, at[1]] = dot(ds, spread_heads(q, mask)).astype(BF)
            made[rows, at[0]] = (fold_heads(t_dot(ds, k), mask, SLOT) * HEAD ** -0.5).astype(BF)


def channel_backward(packed, made, grad_mixed, soft, start, stop):
    width = grad_mixed.shape[1]

    @pl.loop(start, stop, unroll=stop - start)
    def _(i):
        rows = pl.ds(pl.multiple_of(i * SLOT, SLOT), SLOT)
        mask = head_mask(HEAD, 128 // HEAD, 128)
        for g in range(width // 128):
            at = [slice(part * width + g * 128, part * width + (g + 1) * 128) for part in range(3)]
            q, k, v = (packed[rows, a] for a in at)
            weights = soft[i, g // 2, g % 2 * HEAD : (g % 2 + 1) * HEAD, 0:128]
            do = grad_mixed[rows, g * 128 : (g + 1) * 128]
            w = weights.astype(F32)
            dw = fold_heads(t_dot(v, do), mask, HEAD)
            ds = spread_heads((w * (dw - jnp.sum(dw * w, axis=0, keepdims=True))).astype(BF), mask)
            made[rows, at[2]] = dot_t(do, spread_heads(weights, mask)).astype(BF)
            made[rows, at[1]] = dot_t(q, ds).astype(BF)
            made[rows, at[0]] = (dot(k, ds) * HEAD ** -0.5).astype(BF)


def encode(pad, kernel, bias, out, images):
    @pl.loop(0, pad.shape[1] // 128)
    def _(lane):
        ls = cols(lane, 128)
        taps = [jnp.broadcast_to(kernel(t, ls), (images, 128)) for t in range(9)]
        shift = jnp.broadcast_to(bias(ls), (images, 128))

        @pl.loop(0, 7, unroll=7)
        def _(r):
            for c in range(7):
                total = shift
                for t in range(9):
                    at = pl.multiple_of(((r + t // 3) * 9 + c + t % 3) * images, 8)
                    piece = pad[pl.ds(at, images), ls]
                    total = total + piece * taps[t]
                    if t == 4:
                        total = total + piece
                out[pl.ds(pl.multiple_of((r * 7 + c) * images, 8), images), ls] = total


def normalise(stream, gain, bias, out):
    @pl.loop(0, stream.shape[0] // 16, unroll=5)
    def _(p):
        rows = pl.ds(pl.multiple_of(p * 16, 16), 16)
        s = stream[rows, :]
        centered = s - jnp.mean(s, axis=-1, keepdims=True)
        spread = jnp.mean(centered * centered, axis=-1, keepdims=True)
        out[rows, :] = (centered * lax.rsqrt(spread + 1e-5) * gain + bias).astype(BF)


def encode_back(gpad, given, kernel, out, put, first_row, bias_row, images):
    @pl.loop(0, gpad.shape[1] // 128)
    def _(lane):
        ls = cols(lane, 128)
        taps = [jnp.broadcast_to(kernel(8 - t, ls), (images, 128)) for t in range(9)]

        def row(r, totals):
            totals = list(totals)
            for c in range(7):
                at = pl.ds(pl.multiple_of((r * 7 + c) * images, 8), images)
                source = given[at, ls]
                total = None
                for t in range(9):
                    near = pl.ds(pl.multiple_of(((r + t // 3) * 9 + c + t % 3) * images, 8), images)
                    piece = gpad[near, ls]
                    if t == 4:
                        totals[9] = totals[9] + piece
                        total = total + piece
                    total = piece * taps[t] if total is None else total + piece * taps[t]
                    totals[8 - t] = totals[8 - t] + source * piece
                out[at, ls] = total
            return tuple(totals)
        totals = lax.fori_loop(0, 7, row, (jnp.zeros((images, 128), F32),) * 10, unroll=True)
        for t in range(9):
            put(first_row + t, lane, jnp.sum(totals[t], axis=0, keepdims=True))
        put(bias_row, lane, jnp.sum(totals[9], axis=0, keepdims=True))


def normalise_back(stream, grad, base, gain, gpad, put, gain_row, shift_row, acc, images):
    acc[...] = jnp.zeros_like(acc)

    @pl.loop(0, 49, unroll=7)
    def _(p):
        rows = pl.ds(pl.multiple_of(p * images, 8), images)
        s, dy = stream[rows, :], grad[rows, :]
        centered = s - jnp.mean(s, axis=-1, keepdims=True)
        rate = lax.rsqrt(jnp.mean(centered * centered, axis=-1, keepdims=True) + 1e-5)
        unit = centered * rate
        acc[0] += dy * unit
        acc[1] += dy
        dg = dy * gain
        m1 = jnp.mean(dg, axis=-1, keepdims=True)
        m2 = jnp.mean(dg * unit, axis=-1, keepdims=True)
        at = ((lax.div(p, 7) + 1) * 9 + lax.rem(p, 7) + 1) * images
        gpad[pl.ds(pl.multiple_of(at, 8), images), :] = base[rows, :] + rate * (dg - m1 - unit * m2)
    for row, total in ((gain_row, acc[0]), (shift_row, acc[1])):
        total = jnp.sum(total, axis=0, keepdims=True)
        for lane in range(total.shape[1] // 128):
            put(row, lane, total[:, lane * 128 : (lane + 1) * 128])


def fill_pad(pad, source, images):
    @pl.loop(0, 7)
    def _(r):
        inner = pl.ds(pl.multiple_of(((r + 1) * 9 + 1) * images, 8), 7 * images)
        pad[inner, :] = source[pl.ds(pl.multiple_of(r * 7 * images, 8), 7 * images), :]


CONV, CONV_BIAS, GAIN, SHIFT, B_PROJ, B_FC1, B_FC2 = 0, 18, 20, 22, 24, 25, 29
HIDDEN, COT, N2, PRE, MIXED, ATT, N1, PACKED = 0, 4, 5, 6, 10, 11, 12, 13
SEGMENTS = 12


def section_kernel(images, dims, shapes, rows, lags, chunk,
                   halves, conv_w, conv_b, gain, shift, b_proj, b_fc1, b_fc2, w_qkv, w_proj, w_fc1, w_fc2,
                   ends, out, small_out, acts, k_one, k_mid, k_two, k_packed, k_soft, k_slope, x_qkv, x_proj, x_fc1, x_fc2,
                   v_qkv, v_proj, v_fc1, v_fc2, params, xb, cot, pad, one, stream, gmid, gn, packed, soft, slope, hidden,
                   swap, gm_s, n1, n2, mixed, gatt, acc, small_grad, small_pair,
                   grad, land, pair_out, pair_in, small_land, left_buf, right_buf,
                   load, store, push_send, push_recv, fetch_sem, pair_send, pair_recv, send, recv, local, ssend, srecv, slocal,
                   bring_send, bring_recv):
    pipe, dp = lax.axis_index("pipe"), lax.axis_index("dp")
    other = 1 - pipe
    first = pipe == 0
    tokens, width = gn.shape
    wide = v_fc1.shape[1]
    real = 49 * images
    per = SIDE // (2 * chunk)
    block_pairs = SEGMENTS * per
    pairs = 2 * block_pairs
    weights = ((w_qkv, x_qkv, v_qkv), (w_proj, x_proj, v_proj), (w_fc1, x_fc1, v_fc1), (w_fc2, x_fc2, v_fc2))
    QKV, PROJ, FC1, FC2 = range(4)

    def to_core(at, src, dst):
        return pltpu.make_async_remote_copy(src_ref=src, dst_ref=dst, send_sem=push_send.at[at], recv_sem=push_recv.at[at],
                                            device_id={"pipe": other}, device_id_type=MESH)
    push_params = to_core(0, params.at[pipe], params.at[pipe])
    push_x = to_core(1, halves.at[1], xb.at[0])
    push_cot = to_core(1, halves.at[0], cot)
    push_weights = [to_core(2 + at, own, far) for at, (own, far, _) in enumerate(weights)]
    push_result = to_core(6, gn, ends.at[0])
    push_grad = to_core(6, gmid, ends.at[1])

    def load_weight(b, at, fresh):
        own, far, near = weights[at]

        @pl.when(b == pipe)
        def _():
            pltpu.make_async_copy(own, near, load.at[at]).start()

        @pl.when(b != pipe)
        def _():
            if fresh:
                push_weights[at].wait_recv()
            pltpu.make_async_copy(far, near, load.at[at]).start()

    def wait_weight(at):
        own, _, near = weights[at]
        pltpu.make_async_copy(own, near, load.at[at]).wait()

    def keep(at, src, dst):
        return pltpu.make_async_copy(src, dst, store.at[at])

    def block_stores(b):
        return [keep(0, one, k_one.at[b]), keep(1, gmid, k_mid.at[b]), keep(2, stream, k_two.at[b]), keep(3, packed, k_packed.at[b]),
                keep(4, soft, k_soft.at[b]), keep(5, slope, k_slope.at[b]), keep(6, n1, acts.at[b, N1]), keep(7, mixed, acts.at[b, MIXED]),
                keep(8, n2, acts.at[b, N2])] + [
                    keep(9 + s, hidden.at[pl.ds(0, tokens), pl.ds(s * SIDE, SIDE)], acts.at[b, HIDDEN + s]) for s in range(wide // SIDE)]

    def row_of(b, row):
        return params[b, row : row + 1, :]

    def taps_of(b, j):
        return (lambda t, ls: params[b, pl.ds(CONV + 9 * j + t, 1), ls]), (lambda ls: params[b, pl.ds(CONV_BIAS + j, 1), ls])

    def block_of(k):
        return jnp.where(k < block_pairs, 1, 0)

    def within(k):
        return k - jnp.where(k < block_pairs, 0, block_pairs)

    def parts_of(k):
        return (k, 0) if per == 1 else (lax.div(k, per), lax.rem(k, per))

    def number_of(k, core):
        return 2 * within(k) + core

    def out_at(k):
        return jnp.where(block_of(k) == pipe, number_of(k, pipe), 2 * block_pairs + within(k))

    main = Ring(dp, dims, shapes[0], grad, land, out, out_at, send, recv, local)
    small = Ring(dp, dims, shapes[1], small_pair, small_land, small_out, lambda c: 0, ssend, srecv, slocal)

    def slots_of(k):
        at, part = parts_of(within(k))
        left = jnp.where(at < 4, HIDDEN + at, jnp.where(at < 8, N2, jnp.where(at < 9, MIXED, N1)))
        right = jnp.where(at < 4, COT, jnp.where(at < 8, PRE + at - 4, jnp.where(at < 9, ATT, PACKED + at - 9)))
        return left, right, part

    def fetches(k):
        left, right, part = slots_of(k)
        slot, b = lax.rem(k, 2), block_of(k)
        return (pltpu.make_async_copy(acts.at[b, left], left_buf.at[slot], fetch_sem.at[slot, 0]),
                pltpu.make_async_copy(acts.at[b, right, :, cols(part, 2 * chunk)], right_buf.at[slot], fetch_sem.at[slot, 1]))

    def pair_copy(k):
        return pltpu.make_async_remote_copy(
            src_ref=pair_out.at[lax.rem(k, pair_out.shape[0])], dst_ref=pair_in.at[lax.rem(k, pair_in.shape[0])],
            send_sem=pair_send.at[k], recv_sem=pair_recv.at[k], device_id={"pipe": other}, device_id_type=MESH)

    def make(k):
        for copy in fetches(k):
            copy.wait()

        @pl.when(k >= pair_out.shape[0])
        def _():
            pair_copy(k - pair_out.shape[0]).wait_send()

        @pl.when(k >= main.grads)
        def _():
            main.reduce_ends(k - main.grads)
        slot, place, far = lax.rem(k, 2), lax.rem(k, main.grads), lax.rem(k, pair_out.shape[0])
        both = t_dot(left_buf[slot], right_buf[slot]).astype(BF)

        @pl.when(first)
        def _():
            grad[place, 0:SIDE] = both[:, :chunk]
            pair_out[far] = both[:, chunk:]

        @pl.when(jnp.logical_not(first))
        def _():
            pair_out[far] = both[:, :chunk]
            grad[place, 0:SIDE] = both[:, chunk:]
        pair_copy(k).start()
        if rows > SIDE:
            grad[place, SIDE:rows] = jnp.zeros((rows - SIDE, chunk), BF)

    def join(k):
        pair_copy(k).wait_recv()
        place = lax.rem(k, main.grads)
        grad[place, 0:SIDE] = grad[place, 0:SIDE] + pair_in[lax.rem(k, pair_in.shape[0])]

    def bring(k):
        number = number_of(k, pipe)
        at = within(k)
        return pltpu.make_async_remote_copy(
            src_ref=out.at[out_at(k)], dst_ref=out.at[number], send_sem=bring_send.at[at], recv_sem=bring_recv.at[at],
            device_id={"pipe": other}, device_id_type=MESH)

    def hand_over(k):
        @pl.when(block_of(k) != pipe)
        def _():
            bring(k).start()

    def leave(k):
        main.gather_ends(k)

        @pl.when(block_of(k) != pipe)
        def _():
            bring(k).wait_send()

        @pl.when(block_of(k) == pipe)
        def _():
            arrival = pltpu.make_async_remote_copy(
                src_ref=out.at[number_of(k, other)], dst_ref=out.at[number_of(k, other)], send_sem=bring_send.at[within(k)],
                recv_sem=bring_recv.at[within(k)], device_id={"pipe": other}, device_id_type=MESH)
            arrival.wait_recv()
    small_copy = to_core(7, small_grad.at[other], small_pair.at[1])

    def small_make(k):
        small_copy.start()
        small_pair[0] = small_grad[pipe]

    def small_join(k):
        small_copy.wait_recv()
        small_pair[0] = small_pair[0] + small_pair[1]

    def tick(t, low, high):
        stages = main.stages(make, join, hand_over)
        small_stages = small.stages(small_make, small_join, lambda k: None)
        for s in reversed(range(low, high)):
            k = t - lags[s]

            @pl.when((k >= 0) & (k < pairs))
            def _():
                stages[s](k)

            @pl.when(k == pairs)
            def _():
                small_stages[s](0)

    main.greet()
    for j in range(2):
        for t in range(9):
            params[pipe, CONV + 9 * j + t : CONV + 9 * j + t + 1, :] = conv_w[t, j : j + 1, :]
    for row, ref in ((CONV_BIAS, conv_b), (GAIN, gain), (SHIFT, shift), (B_PROJ, b_proj), (B_FC2, b_fc2)):
        params[pipe, row : row + ref.shape[0], :] = ref[...]
    for j in range(wide // width):
        params[pipe, B_FC1 + j : B_FC1 + j + 1, :] = b_fc1[:, j * width : (j + 1) * width]
    x_copy = pltpu.make_async_copy(halves.at[0], xb.at[0], load.at[5])
    cot_copy = pltpu.make_async_copy(halves.at[1], cot, load.at[5])
    push_params.start()

    @pl.when(first)
    def _():
        push_x.start()
        x_copy.start()

    @pl.when(jnp.logical_not(first))
    def _():
        push_cot.start()
        cot_copy.start()
    for copy in push_weights:
        copy.start()
    fill_swap(swap, images)
    clear_border(pad, images)
    small_grad[...] = jnp.zeros_like(small_grad)
    one[real:tokens, :] = jnp.zeros((tokens - real, width), F32)
    stream[real:tokens, :] = jnp.zeros((tokens - real, width), F32)
    push_params.wait_recv()

    @pl.when(first)
    def _():
        x_copy.wait()

    @pl.when(jnp.logical_not(first))
    def _():
        push_x.wait_recv()

    @pl.loop(0, 2)
    def _(b):
        stores = block_stores(b)

        @pl.when(b > 0)
        def _():
            for copy in stores:
                copy.wait()
        load_weight(b, QKV, True)
        gn[...] = xb[b].astype(F32)
        fill_pad(pad, gn, images)
        kernel, bias = taps_of(b, 0)
        encode(pad, kernel, bias, one, images)
        stores[0].start()
        normalise(one, row_of(b, GAIN), row_of(b, SHIFT), n1)
        stores[6].start()


        gm_s[...] = dot(swap[...], n1[...]).astype(BF)
        wait_weight(QKV)

        @pl.loop(0, 3)
        def _(j):
            scale = jnp.where(j == 0, HEAD ** -0.5, 1.0)
            packed[:, cols(j, width)] = (dot(gm_s[...], v_qkv[:, cols(j, width)]) * scale).astype(BF)
        stores[3].start()
        load_weight(b, PROJ, True)

        @pl.when(b == 0)
        def _():
            spatial_forward(packed, gm_s, soft, images)

        @pl.when(b == 1)
        def _():
            channel_forward(packed, gm_s, soft, images)
        stores[4].start()
        load_weight(b, FC1, True)

        mixed[...] = t_dot(swap[...], gm_s[...]).astype(BF)
        stores[7].start()
        wait_weight(PROJ)

        gmid[...] = one[...] + dot(mixed[...], v_proj[...]) + row_of(b, B_PROJ)
        stores[1].start()
        fill_pad(pad, gmid, images)
        kernel, bias = taps_of(b, 1)
        encode(pad, kernel, bias, stream, images)
        stores[2].start()
        normalise(stream, row_of(b, GAIN + 1), row_of(b, SHIFT + 1), n2)
        stores[8].start()
        wait_weight(FC1)
        load_weight(b, FC2, True)

        @pl.loop(0, wide // width)
        def _(j):
            at = cols(j, width)
            value, rate = gelu_both(dot(n2[...], v_fc1[:, at]) + params[b, pl.ds(B_FC1 + j, 1), :])
            hidden[0:tokens, at] = value.astype(BF)
            slope[:, at] = rate.astype(BF)
        stores[5].start()
        for copy in stores[9:]:
            copy.start()
        wait_weight(FC2)

        gn[...] = stream[...] + dot(hidden[0:tokens, :], v_fc2[...]) + row_of(b, B_FC2)

        @pl.when(b == 0)
        def _():
            xb[1] = gn[...].astype(BF)

    end_copy = pltpu.make_async_copy(gn, ends.at[1], load.at[6])
    last_copy = pltpu.make_async_copy(gmid, ends.at[0], load.at[6])

    @pl.when(first)
    def _():
        push_result.start()
        push_cot.wait_recv()

    @pl.when(jnp.logical_not(first))
    def _():
        end_copy.start()
        cot_copy.wait()
    keep_cot = keep(13, cot, acts.at[1, COT])
    keep_cot.start()
    for copy in block_stores(1):
        copy.wait()
    keep_cot.wait()
    for copy in fetches(0):
        copy.start()

    def put(b):
        def at(row, lane, value):
            small_grad[b, pl.ds(lane * 32 + row, 1), :] = value
        return at

    loads = [pltpu.make_async_copy(k_slope.at[0], slope, load.at[7]), pltpu.make_async_copy(k_packed.at[0], packed, load.at[8]),
             pltpu.make_async_copy(k_soft.at[0], soft, load.at[9]), pltpu.make_async_copy(k_two.at[0], stream, load.at[10]),
             pltpu.make_async_copy(k_mid.at[0], gmid, load.at[11])]

    def later(b, at):
        @pl.when(b == 0)
        def _():
            loads[at].wait()

    def later_weight(b, at):
        @pl.when(b == 0)
        def _():
            wait_weight(at)

    def ahead(b, do):
        pl.when(b == 1)(do)

    def pre_part(part):
        def run(b):
            if part == 0:
                later(b, 0)
                later_weight(b, FC2)
                one[...] = cot[...].astype(F32)
            each = wide // 3
            at = slice(part * each, (part + 1) * each)
            pre = dot_t(cot[...], v_fc2[at, :]) * slope[:, at].astype(F32)
            slope[:, at] = pre.astype(BF)
            total = jnp.sum(pre, axis=0, keepdims=True)
            for piece in range(each // 128):
                lane = part * each // 128 + piece
                put(b)(B_FC1 + lane // (width // 128), lane % (width // 128), total[:, piece * 128 : (piece + 1) * 128])
            if part == 2:
                ahead(b, lambda: load_weight(0, FC2, False))
                copies = [keep(s, slope.at[:, pl.ds(s * SIDE, SIDE)], acts.at[b, PRE + s]) for s in range(wide // SIDE)]
                for copy in copies:
                    copy.start()
                for lane in range(width // 128):
                    put(b)(B_FC2, lane, jnp.sum(one[:, lane * 128 : (lane + 1) * 128], axis=0, keepdims=True))
                for copy in copies:
                    copy.wait()
        return run

    def through_fc1(b):
        @pl.when(b == 1)
        def _():
            @pl.when(first)
            def _():
                push_result.wait_send()

            @pl.when(jnp.logical_not(first))
            def _():
                end_copy.wait()
        later_weight(b, FC1)

        gn[...] = dot_t(slope[...], v_fc1[...])
        ahead(b, lambda: load_weight(0, FC1, False))

    def through_second(b):
        later(b, 3)
        normalise_back(stream, gn, one, row_of(b, GAIN + 1), pad, put(b), GAIN + 1, SHIFT + 1, acc, images)
        pltpu.make_async_copy(k_one.at[b], stream, load.at[12]).start()
        later(b, 4)
        encode_back(pad, gmid, taps_of(b, 1)[0], gmid, put(b), CONV + 9, CONV_BIAS + 1, images)
        gmid[real:tokens, :] = jnp.zeros((tokens - real, width), F32)
        for lane in range(width // 128):
            part = gmid[:, lane * 128 : (lane + 1) * 128]
            put(b)(B_PROJ, lane, jnp.sum(part, axis=0, keepdims=True))
            gatt[:, lane * 128 : (lane + 1) * 128] = part.astype(BF)
        keep(4, gatt, acts.at[b, ATT]).start()

    def through_proj(b):
        later_weight(b, PROJ)

        n2[...] = dot_t(gatt[...], v_proj[...]).astype(BF)
        ahead(b, lambda: load_weight(0, PROJ, False))
        gm_s[...] = dot(swap[...], n2[...]).astype(BF)
        later(b, 1)
        later(b, 2)

    def through_mix(part):
        def run(b):
            each = images // 2

            @pl.when(b == 0)
            def _():
                spatial_backward(packed, hidden, gm_s, soft, part * each, (part + 1) * each)

            @pl.when(b == 1)
            def _():
                channel_backward(packed, hidden, gm_s, soft, part * each, (part + 1) * each)
            if part == 1:
                keep(4, gatt, acts.at[b, ATT]).wait()
        return run

    def unswap(b):
        @pl.loop(0, 3)
        def _(j):
            slope[:, cols(j, width)] = t_dot(swap[...], hidden[:, cols(j, width)]).astype(BF)
        copies = [keep(s, slope.at[:, pl.ds(s * SIDE, SIDE)], acts.at[b, PACKED + s]) for s in range(3)]
        for copy in copies:
            copy.start()
        for copy in copies:
            copy.wait()

    def through_qkv(b):
        later_weight(b, QKV)

        gn[...] = dot_t(slope[:, 0 : 3 * width], v_qkv[...])

        def prepare():
            load_weight(0, QKV, False)
            for at in range(3):
                loads[at].start()
        ahead(b, prepare)

    def through_first(b):
        pltpu.make_async_copy(k_one.at[b], stream, load.at[12]).wait()
        normalise_back(stream, gn, gmid, row_of(b, GAIN), pad, put(b), GAIN, SHIFT, acc, images)
        ahead(b, lambda: loads[3].start())

    def finish(b):
        gn[...] = xb[b].astype(F32)
        encode_back(pad, gn, taps_of(b, 0)[0], gmid, put(b), CONV, CONV_BIAS, images)

        @pl.when(b == 1)
        def _():
            cot[...] = gmid[...].astype(BF)
            copy = keep(5, cot, acts.at[0, COT])
            copy.start()
            loads[4].start()
            copy.wait()

        @pl.when((b == 0) & first)
        def _():
            last_copy.start()

        @pl.when((b == 0) & jnp.logical_not(first))
        def _():
            push_grad.start()
    segments = [pre_part(0), pre_part(1), pre_part(2), through_fc1, through_second, through_proj, through_mix(0), through_mix(1),
                unswap, through_qkv, through_first, finish]

    late = len(lags) * 2 // 3

    @pl.loop(0, pairs + 1 + lags[-1])
    def _(t):
        tick(t, late, len(lags))
        gone = t - lags[-1] - 1

        @pl.when((gone >= 0) & (gone < pairs))
        def _():
            leave(gone)
        at, part = parts_of(within(t))

        @pl.when((t < pairs) & (part == 0))
        def _():
            b = block_of(t)
            for number, segment in enumerate(segments):
                @pl.when(at == number)
                def _():
                    segment(b)
        tick(t, 0, late)

        @pl.when(t + 1 < pairs)
        def _():
            for copy in fetches(t + 1):
                copy.start()

    @pl.loop(pairs - main.grads, pairs)
    def _(k):
        main.reduce_ends(k)

    @pl.loop(pairs - pair_out.shape[0], pairs)
    def _(k):
        pair_copy(k).wait_send()

    small.reduce_ends(0)
    small.gather_ends(0)
    small_copy.wait_send()
    push_params.wait_send()
    for copy in push_weights:
        copy.wait_send()

    @pl.when(first)
    def _():
        push_x.wait_send()
        last_copy.wait()
        push_grad.wait_recv()

    @pl.when(jnp.logical_not(first))
    def _():
        push_cot.wait_send()
        push_grad.wait_send()
        push_result.wait_recv()


def section(halves, small, weights, images, n, collective_id=0):
    w_qkv, w_proj, w_fc1, w_fc2 = weights
    _, tokens, width = halves.shape
    wide = w_fc1.shape[1]
    slots = images * SLOT
    dims = dp_dims(n)
    chunk = 384 if n <= 16 else 128
    total = (wide // SIDE * 2 + 4) * SIDE // chunk
    pairs = total
    rows = -(-SIDE // (16 * n)) * 16 * n
    small_rows = 16 * n
    shapes = (Shape(rows, dims), Shape(small_rows, dims))
    events = shapes[0].events
    hops = sum(0 if s == 1 else 1 if s == 2 else 3 for s in dims[0])
    gaps = [1, 2] + [1] * (2 * hops - 2) + [3]
    lags = [sum(gaps[:s]) for s in range(2 * hops + 2)]
    grads = 8 if lags[hops + 1] < 8 else 16
    lands = 8 if 2 * gaps[1] + 3 <= 8 else 16
    any_space = pl.BlockSpec(memory_space=pl.ANY)
    vmem = pl.BlockSpec(memory_space=pltpu.VMEM)
    soft = (images, width // GROUP, SLOT, 2 * GROUP)
    outs = [((2, tokens, width), F32), ((total + total // 2, rows, chunk), BF), ((1, small_rows, 128), F32),
            ((2, 16, tokens, SIDE), BF), ((2, tokens, width), F32), ((2, tokens, width), F32), ((2, tokens, width), F32),
            ((2, slots, 3 * width), BF), ((2, *soft), BF), ((2, tokens, wide), BF),
            (w_qkv.shape, BF), (w_proj.shape, BF), (w_fc1.shape, BF), (w_fc2.shape, BF)]
    dma = pltpu.SemaphoreType.DMA

    def plain(shape):
        return pltpu.VMEM(shape, F32)

    def low(shape):
        return pltpu.VMEM(shape, BF)
    results = pl.pallas_call(
        functools.partial(section_kernel, images, dims, shapes, rows, lags, chunk),
        out_shape=[jax.ShapeDtypeStruct(*o) for o in outs],
        in_specs=[any_space] + [vmem] * 7 + [any_space] * 4,
        out_specs=[any_space] * len(outs),
        scratch_shapes=[low(w.shape) for w in weights] + [
            plain((2, 32, width)), low((2, tokens, width)), low((tokens, width)), plain((81 * images, width)),
            plain((tokens, width)), plain((tokens, width)), plain((tokens, width)), plain((tokens, width)),
            low((slots, 3 * width)), low(soft), low((tokens, wide)), low((slots, wide)),
            low((slots, tokens)), low((slots, width)), low((tokens, width)), low((tokens, width)), low((tokens, width)), low((tokens, width)),
            plain((2, images, width)), plain((2, small_rows, 128)), plain((2, small_rows, 128)),
            low((grads, rows, chunk)), low((lands, shapes[0].land, chunk)), low((4, SIDE, chunk)), low((8, SIDE, chunk)), plain((1, shapes[1].land, 128)),
            low((2, tokens, SIDE)), low((2, tokens, 2 * chunk)),
            dma((13,)), dma((14,)), dma((8,)), dma((8,)), dma((2, 2)), dma((pairs,)), dma((pairs,)),
            dma((pairs, events)), dma((pairs, events)), dma, dma((1, events)), dma((1, events)), dma, dma((pairs // 2,)), dma((pairs // 2,)),
        ],
        compiler_params=pltpu.CompilerParams(collective_id=collective_id, has_side_effects=True, vmem_limit_bytes=63 * 2**20),
    )(halves, *small, w_qkv, w_proj, w_fc1, w_fc2)
    return results[:3]


def finish_kernel(images, chunk, done, sums, ends, fc2, fc1, proj, qkv, conv_w, conv_b, gain, shift, b_proj, b_fc1, b_fc2, section,
                  low_buf, wide_buf, end_buf, section_buf, read, write, end_sem):
    depth = low_buf.shape[0]
    jobs, start = [], 0
    for dst in (fc2, fc1, proj, qkv):
        across = dst.shape[2] // chunk
        number = dst.shape[1] // SIDE * across
        jobs.append((start, number, across, dst))
        start += number
    end_copy = pltpu.make_async_copy(ends, end_buf, end_sem.at[0])
    end_copy.start()

    def get(c):
        return pltpu.make_async_copy(done.at[c, pl.ds(0, SIDE)], low_buf.at[lax.rem(c, depth)], read.at[lax.rem(c, depth)])

    def give(c, dst, across, at):
        rows = pl.ds(pl.multiple_of(lax.div(at, across) * SIDE, SIDE), SIDE)
        return pltpu.make_async_copy(wide_buf.at[lax.rem(c, depth)], dst.at[0, rows, cols(lax.rem(at, across), chunk)],
                                     write.at[lax.rem(c, depth)])

    @pl.loop(0, depth)
    def _(c):
        get(c).start()
    for begin, number, across, dst in jobs:
        @pl.loop(0, number)
        def _(at):
            c = begin + at
            slot = lax.rem(c, depth)
            get(c).wait()

            @pl.when(c >= depth)
            def _():
                give(c, dst, across, at).wait()
            for r in range(0, SIDE, 128):
                wide_buf[slot, r : r + 128] = low_buf[slot, r : r + 128].astype(F32)
            give(c, dst, across, at).start()

            @pl.when(c + depth < start)
            def _():
                get(c + depth).start()
        if begin == 0:
            end_copy.wait()
            for half in range(2):
                section_buf[:, half * images : (half + 1) * images, :] = end_buf[half, 0:49]
            section_copy = pltpu.make_async_copy(section_buf, section.at[0], end_sem.at[1])
            section_copy.start()
    lanes = fc2.shape[2] // 128
    width = fc2.shape[2]

    def take(first_row, ref, index, rows):
        for lane in range(lanes):
            ref[index + (slice(lane * 128, (lane + 1) * 128),)] = sums[0, lane * 32 + first_row : lane * 32 + first_row + rows, :]
    for j in range(2):
        for t in range(9):
            take(CONV + 9 * j + t, conv_w, (0, t, slice(j, j + 1)), 1)
    take(CONV_BIAS, conv_b, (0, slice(0, 2)), 2)
    take(GAIN, gain, (0, slice(0, 2)), 2)
    take(SHIFT, shift, (0, slice(0, 2)), 2)
    take(B_PROJ, b_proj, (slice(0, 1),), 1)
    take(B_FC2, b_fc2, (slice(0, 1),), 1)
    for lane in range(b_fc1.shape[1] // 128):
        at = lane % lanes * 32 + B_FC1 + lane // lanes
        b_fc1[0:1, lane * 128 : (lane + 1) * 128] = sums[0, at : at + 1, :]
    @pl.loop(start - depth, start)
    def _(c):
        give(c, fc2, 1, 0).wait()
    section_copy.wait()


def finish(done, sums, ends, shapes, images):
    any_space = pl.BlockSpec(memory_space=pl.ANY)
    vmem = pl.BlockSpec(memory_space=pltpu.VMEM)
    chunk, depth = done.shape[2], 6
    return pl.pallas_call(
        functools.partial(finish_kernel, images, chunk),
        out_shape=[jax.ShapeDtypeStruct(s, F32) for s in shapes],
        in_specs=[any_space, vmem, any_space],
        out_specs=[any_space] * 4 + [vmem] * 7 + [any_space],
        scratch_shapes=[pltpu.VMEM((depth, SIDE, chunk), BF), pltpu.VMEM((depth, SIDE, chunk), F32), pltpu.VMEM(ends.shape, F32),
                        pltpu.VMEM(shapes[-1][1:], F32),
                        pltpu.SemaphoreType.DMA((depth,)), pltpu.SemaphoreType.DMA((depth,)), pltpu.SemaphoreType.DMA((2,))],
        compiler_params=pltpu.CompilerParams(vmem_limit_bytes=62 * 2**20),
    )(done, sums, ends)


def on_device(section_inputs, conv_weight, conv_bias, norm_gain, norm_bias, w_qkv, w_proj, b_proj, w_fc1, b_fc1, w_fc2, b_fc2):
    n = lax.axis_size("dp")
    images, positions, width = section_inputs.shape[1:]
    half = images // 2
    spare = -(-positions * half // 16) * 16 // half - positions
    halves = jnp.pad(section_inputs.reshape(2, half, positions, width), ((0, 0), (0, 0), (0, spare), (0, 0)))
    halves = jnp.swapaxes(halves, 1, 2).reshape(2, -1, width)
    small = (jnp.swapaxes(conv_weight[0], 0, 1), conv_bias[0], norm_gain[0], norm_bias[0], b_proj, b_fc1, b_fc2)
    ends, done, sums = section(halves, small, (w_qkv[0], w_proj[0], w_fc1[0], w_fc2[0]), half, n)
    ends = ends.reshape(2, -1, half, width)
    arrays = (w_fc2, w_fc1, w_proj, w_qkv, jnp.swapaxes(conv_weight, 1, 2), conv_bias, norm_gain, norm_bias, b_proj, b_fc1, b_fc2,
              jnp.swapaxes(section_inputs, 1, 2))
    fc2, fc1, proj, qkv, conv_w, conv_b, gain, shift, g_proj, g_fc1, g_fc2, section_ends = finish(done, sums, ends, [a.shape for a in arrays], half)
    return (jnp.swapaxes(section_ends, 1, 2), jnp.swapaxes(conv_w, 1, 2), conv_b, gain, shift, qkv, proj, g_proj, fc1, g_fc1, fc2, g_fc2)


def solution(mesh):
    return jax.shard_map(
        on_device,
        mesh=mesh,
        in_specs=(
            P("pipe", "dp", None, None),
            P("pipe", None, None, None),
            P("pipe", None, None),
            P("pipe", None, None),
            P("pipe", None, None),
            P("pipe", None, None),
            P("pipe", None, None),
            P("pipe", None),
            P("pipe", None, None),
            P("pipe", None),
            P("pipe", None, None),
            P("pipe", None),
        ),
        out_specs=(
            P("pipe", "dp", None, None),
            P("pipe", None, None, None),
            P("pipe", None, None),
            P("pipe", None, None),
            P("pipe", None, None),
            P("pipe", None, None),
            P("pipe", None, None),
            P("pipe", None),
            P("pipe", None, None),
            P("pipe", None),
            P("pipe", None, None),
            P("pipe", None),
        ),
        check_vma=False,
    )
```

```python
import functools

import jax
import jax.numpy as jnp
from jax import lax
from jax.experimental import pallas as pl
from jax.experimental.pallas import tpu as pltpu
from jax.sharding import PartitionSpec as P

MESH = pl.DeviceIdType.MESH
SIDE = 768


HEAD = 32
GROUP = 256
SLOT = 64
BF = jnp.bfloat16
F32 = jnp.float32


def cols(j, width=GROUP):
    return pl.ds(pl.multiple_of(j * width, width), width)


def dot(a, b):
    return lax.dot_general(a, b, (((1,), (0,)), ((), ())), preferred_element_type=F32)


def dot_t(a, b):
    return lax.dot_general(a, b, (((1,), (1,)), ((), ())), preferred_element_type=F32)


def t_dot(a, b):
    return lax.dot_general(a, b, (((0,), (0,)), ((), ())), preferred_element_type=F32)


def fill_swap(ref, images):
    rows, columns = ref.shape
    block = 128

    @pl.loop(0, rows // block)
    def _(b):
        r = lax.broadcasted_iota(jnp.int32, (block, columns), 0) + b * block
        c = lax.broadcasted_iota(jnp.int32, (block, columns), 1)
        image, position = lax.div(r, SLOT), lax.rem(r, SLOT)
        hit = (c == position * images + image) & (position < 49)
        ref[pl.ds(pl.multiple_of(b * block, block), block), :] = jnp.where(hit, 1.0, 0.0).astype(BF)


def clear_border(pad, images):
    zero = jnp.zeros((9 * images, pad.shape[1]), pad.dtype)
    pad[0 : 9 * images, :] = zero
    pad[72 * images : 81 * images, :] = zero
    one = jnp.zeros((images, pad.shape[1]), pad.dtype)

    @pl.loop(1, 8)
    def _(r):
        pad[pl.ds(pl.multiple_of(r * 9 * images, 8), images), :] = one
        pad[pl.ds(pl.multiple_of((r * 9 + 8) * images, 8), images), :] = one


def head_mask(rows_per, count, lanes):
    shape = (count * rows_per, lanes)
    r = lax.broadcasted_iota(jnp.int32, shape, 0)
    c = lax.broadcasted_iota(jnp.int32, shape, 1)
    return lax.div(r, rows_per) == lax.div(c, HEAD)


def spread_heads(x, mask):
    count = mask.shape[0] // x.shape[0]
    return jnp.where(mask, jnp.concatenate([x] * count, axis=0), jnp.zeros((), x.dtype))


def fold_heads(x, mask, rows_per):
    kept = jnp.where(mask, x, 0.0)
    total = kept[0:rows_per]
    for h in range(1, x.shape[0] // rows_per):
        total = total + kept[h * rows_per : (h + 1) * rows_per]
    return total


def soft_down(scores, valid):
    if valid < scores.shape[0]:
        r = lax.broadcasted_iota(jnp.int32, scores.shape, 0)
        scores = jnp.where(r < valid, scores, -jnp.inf)
    e = jnp.exp(scores - jnp.max(scores, axis=0, keepdims=True))
    return e / jnp.sum(e, axis=0, keepdims=True)


def gelu_both(x):
    half = 0.5 + 0.5 * lax.erf(x * 0.7071067811865476)
    return x * half, half + x * (0.3989422804014327 * jnp.exp(-0.5 * x * x))


def dp_dims(n):
    sizes = [1, 1, 1]
    at = 0
    left = n
    while left > 1:
        factor = 2 if left % 2 == 0 else left
        sizes[at % 3] *= factor
        left //= factor
        at += 1
    return tuple(sizes), (sizes[1] * sizes[2], sizes[2], 1)


class Place:
    def __init__(self, dp, size, stride):
        self.size = size
        pos = lax.rem(lax.div(dp, stride), size)
        low = pos < (size + 1) // 2
        self.outer = jnp.where(low, pos, size - 1 - pos)
        self.low = low
        step = jnp.where(low, stride, -stride)
        self.inner_peer = dp + step
        self.outer_peer = dp - step


def pick(flag, a, b):
    out = object.__new__(Place)
    out.size = a.size
    for name in ("low", "outer", "inner_peer", "outer_peer"):
        setattr(out, name, jnp.where(flag, getattr(a, name), getattr(b, name)))
    return out


class Shape:
    def __init__(self, rows, dims):
        s0, s1, s2 = dims[0]
        self.sizes = (s2, s0, s1)
        first = rows // s2
        mid = [first // s0] * s0
        tails = sorted(set(mid), reverse=True) if s0 == 4 else [mid[0]]

        def cut(parts):
            return [sum(parts[:j]) for j in range(len(parts) + 1)]
        self.cuts = ([cut([first] * s2)], [cut(mid)], [cut([tail // s1] * s1) for tail in tails])
        self.starts, total = [], 0
        for n, lists in zip(self.sizes, self.cuts):
            self.starts.append(total)
            at = lists[0]
            total += 0 if n == 1 else at[1] if n == 2 else at[4] + at[1]
        self.land = total
        self.events, self.first_event = 0, []
        for n in self.sizes * 2:
            self.first_event.append(self.events)
            self.events += {1: 0, 2: 1, 4: 4}[n]


class Ring:
    def __init__(self, dp, dims, shape, grad, land, out, out_at, send, recv, local):
        (s0, s1, s2), (t0, t1, t2) = dims
        self.mids = Place(dp, s0, t0)
        self.fast, self.slow = Place(dp, s2, t2), Place(dp, s1, t1)
        self.grad, self.land, self.out, self.out_at = grad, land, out, out_at
        self.grads, self.lands = grad.shape[0], land.shape[0]
        self.send, self.recv, self.local = send, recv, local
        self.shape, self.sizes, self.cuts = shape, shape.sizes, shape.cuts

    def level(self, c, i):
        if i == 1:
            return self.mids
        flag = lax.rem(c + lax.axis_index("pipe"), 2) == 0
        return pick(flag, self.fast, self.slow) if i == 0 else pick(flag, self.slow, self.fast)

    def each(self, i, do):
        if len(self.cuts[i]) == 1:
            do(0)
        else:
            for v in range(2):
                pl.when(self.mids.outer == v)(functools.partial(do, v))

    def own(self, c, i, v):
        place, at = self.level(c, i), self.cuts[i][v]
        near = jnp.where(place.low, at[0], at[-1] - at[1])
        if place.size != 4:
            return near
        return jnp.where(place.outer == 0, near, jnp.where(place.low, at[1], at[-1] - at[2]))

    def base(self, c, i):
        start = 0
        for j in range(i):
            start = start + self.own(c, j, 0)
        return start

    def span(self, c, i, v, a, b):
        at = self.cuts[i][v]
        start = self.base(c, i) + jnp.where(self.level(c, i).low, at[a], at[-1] - at[b])
        return pl.ds(pl.multiple_of(start, 8), at[b] - at[a])

    def mine(self, c, rows):
        return self.grad.at[lax.rem(c, self.grads), rows]

    def landing(self, c, i, at, length):
        return self.land.at[lax.rem(c, self.lands), pl.ds(self.shape.starts[i] + at, length)]

    def copy(self, c, ev, src, dst, peer):
        return pltpu.make_async_remote_copy(
            src_ref=src, dst_ref=dst, send_sem=self.send.at[c, ev], recv_sem=self.recv.at[c, ev],
            device_id={"dp": peer}, device_id_type=MESH)

    def add(self, c, i, v, a, b, at):
        rows = self.span(c, i, v, a, b)
        slot = lax.rem(c, self.grads)
        self.grad[slot, rows] = self.grad[slot, rows] + self.landing(c, i, at, rows.size)[...]

    def give(self, c, i, v, ev, a, b, at, peer):
        rows = self.span(c, i, v, a, b)
        return self.copy(c, ev, self.mine(c, rows), self.landing(c, i, at, rows.size), peer)

    def reduce_stages(self, i):
        n = self.sizes[i]
        ev = self.shape.first_event[i]
        if n == 1:
            return []
        if n == 2:
            def first(c):
                self.each(i, lambda v: self.give(c, i, v, ev, 1, 2, 0, self.level(c, i).inner_peer).start())

            def last(c):
                def do(v):
                    self.give(c, i, v, ev, 0, 1, 0, self.level(c, i).inner_peer).wait_recv()
                    self.add(c, i, v, 0, 1, 0)
                self.each(i, do)
            return [first, last]
        length = self.cuts[i][0][1]

        def zero(c):
            place = self.level(c, i)

            @pl.when(place.outer == 0)
            def _():
                self.give(c, i, 0, ev, 2, 4, 0, place.inner_peer).start()

        def one(c):
            place = self.level(c, i)

            @pl.when(place.outer == 0)
            def _():
                self.give(c, i, 0, ev + 1, 1, 2, 2 * length, place.inner_peer).start()

            @pl.when(place.outer == 1)
            def _():
                self.give(c, i, 0, ev, 2, 4, 0, place.inner_peer).wait_recv()
                self.add(c, i, 0, 2, 4, 0)
                self.give(c, i, 0, ev + 2, 3, 4, 3 * length, place.inner_peer).start()

        def two(c):
            place = self.level(c, i)

            @pl.when(place.outer == 1)
            def _():
                self.give(c, i, 0, ev + 2, 0, 1, 3 * length, place.inner_peer).wait_recv()
                self.add(c, i, 0, 0, 1, 3 * length)
                self.give(c, i, 0, ev, 0, 1, 3 * length, place.outer_peer).start()
                self.give(c, i, 0, ev + 3, 2, 3, 4 * length, place.inner_peer).start()

        def three(c):
            place = self.level(c, i)

            @pl.when(place.outer == 0)
            def _():
                self.give(c, i, 0, ev, 0, 1, 3 * length, place.inner_peer).wait_recv()
                self.add(c, i, 0, 0, 1, 3 * length)

            @pl.when(place.outer == 1)
            def _():
                self.give(c, i, 0, ev + 1, 1, 2, 2 * length, place.inner_peer).wait_recv()
                self.add(c, i, 0, 1, 2, 2 * length)
                self.give(c, i, 0, ev + 3, 1, 2, 4 * length, place.inner_peer).wait_recv()
                self.add(c, i, 0, 1, 2, 4 * length)
        return [zero, one, two, three]

    def reduce_ends(self, c):
        for i in range(3):
            n, place = self.sizes[i], self.level(c, i)
            ev = self.shape.first_event[i]
            if n == 2:
                self.each(i, lambda v: self.give(c, i, v, ev, 1, 2, 0, place.inner_peer).wait_send())
            elif n == 4:
                @pl.when(place.outer == 0)
                def _():
                    self.give(c, i, 0, ev, 2, 4, 0, place.inner_peer).wait_send()
                    self.give(c, i, 0, ev + 1, 1, 2, 0, place.inner_peer).wait_send()

                @pl.when(place.outer == 1)
                def _():
                    self.give(c, i, 0, ev + 2, 3, 4, 0, place.inner_peer).wait_send()
                    self.give(c, i, 0, ev, 0, 1, 0, place.outer_peer).wait_send()
                    self.give(c, i, 0, ev + 3, 2, 3, 0, place.inner_peer).wait_send()

    def spread(self, c, i, v, ev, a, b, peer):
        dst = self.out.at[self.out_at(c), self.span(c, i, v, a, b)]
        return self.copy(c, ev, dst, dst, peer)

    def gather_stages(self, i):
        n = self.sizes[i]
        ev = self.shape.first_event[3 + i]
        if n == 1:
            return []
        if n == 2:
            def first(c):
                self.each(i, lambda v: self.spread(c, i, v, ev, 0, 1, self.level(c, i).inner_peer).start())

            def last(c):
                self.each(i, lambda v: self.spread(c, i, v, ev, 1, 2, self.level(c, i).inner_peer).wait_recv())
            return [first, last]

        def zero(c):
            place = self.level(c, i)

            @pl.when(place.outer == 0)
            def _():
                self.spread(c, i, 0, ev, 0, 1, place.inner_peer).start()

            @pl.when(place.outer == 1)
            def _():
                self.spread(c, i, 0, ev + 2, 1, 2, place.inner_peer).start()
                self.spread(c, i, 0, ev, 1, 2, place.outer_peer).start()

        def one(c):
            place = self.level(c, i)

            @pl.when(place.outer == 1)
            def _():
                self.spread(c, i, 0, ev, 0, 1, place.outer_peer).wait_recv()
                self.spread(c, i, 0, ev + 3, 0, 1, place.inner_peer).start()

        def two(c):
            place = self.level(c, i)

            @pl.when(place.outer == 1)
            def _():
                self.spread(c, i, 0, ev + 2, 2, 3, place.inner_peer).wait_recv()
                self.spread(c, i, 0, ev + 3, 3, 4, place.inner_peer).wait_recv()
                self.spread(c, i, 0, ev + 1, 2, 4, place.outer_peer).start()

        def three(c):
            place = self.level(c, i)

            @pl.when(place.outer == 0)
            def _():
                self.spread(c, i, 0, ev, 1, 2, place.inner_peer).wait_recv()
                self.spread(c, i, 0, ev + 1, 2, 4, place.inner_peer).wait_recv()
        return [zero, one, two, three]

    def gather_ends(self, c):
        for i in range(3):
            n, place = self.sizes[i], self.level(c, i)
            ev = self.shape.first_event[3 + i]
            if n == 2:
                self.each(i, lambda v: self.spread(c, i, v, ev, 0, 1, place.inner_peer).wait_send())
            elif n == 4:
                @pl.when(place.outer == 0)
                def _():
                    self.spread(c, i, 0, ev, 0, 1, place.inner_peer).wait_send()

                @pl.when(place.outer == 1)
                def _():
                    self.spread(c, i, 0, ev + 2, 1, 2, place.inner_peer).wait_send()
                    self.spread(c, i, 0, ev, 1, 2, place.outer_peer).wait_send()
                    self.spread(c, i, 0, ev + 3, 0, 1, place.inner_peer).wait_send()
                    self.spread(c, i, 0, ev + 1, 2, 4, place.outer_peer).wait_send()

    def settle(self, c):
        def do(v):
            at = self.cuts[2][v]
            rows = pl.ds(pl.multiple_of(self.base(c, 2) + self.own(c, 2, v), 8), at[1])
            copy = pltpu.make_async_copy(self.mine(c, rows), self.out.at[self.out_at(c), rows], self.local)
            copy.start()
            copy.wait()
        self.each(2, do)

    def stages(self, first, second, last):
        groups = [self.reduce_stages(0), self.reduce_stages(1), self.reduce_stages(2), [self.settle],
                  self.gather_stages(2), self.gather_stages(1), self.gather_stages(0), [last]]
        joined = [[first], [second]]
        for group in groups:
            if group:
                joined[-1].append(group[0])
                joined += [[stage] for stage in group[1:]]
        return [functools.partial(run_all, stages) for stages in joined]

    def greet(self):
        barrier = pltpu.get_barrier_semaphore()
        pl.semaphore_signal(barrier, inc=1, device_id={"pipe": 1 - lax.axis_index("pipe")}, device_id_type=MESH)
        count = jnp.int32(1)
        for place in (self.fast, self.mids, self.slow):
            if place.size == 1:
                continue
            pl.semaphore_signal(barrier, inc=1, device_id={"dp": place.inner_peer}, device_id_type=MESH)
            count = count + 1
            if place.size == 4:
                @pl.when(place.outer == 1)
                def _():
                    pl.semaphore_signal(barrier, inc=1, device_id={"dp": place.outer_peer}, device_id_type=MESH)
                count = count + jnp.where(place.outer == 1, 1, 0)
        pl.semaphore_wait(barrier, count)


def run_all(stages, c):
    for stage in stages:
        stage(c)


def spatial_forward(packed, mixed, soft, images):
    width = mixed.shape[1]

    @pl.loop(0, images, unroll=8)
    def _(i):
        rows = pl.ds(pl.multiple_of(i * SLOT, SLOT), SLOT)
        mask = head_mask(SLOT, GROUP // HEAD, GROUP)
        for g in range(width // GROUP):
            q, k, v = (packed[rows, part * width + g * GROUP : part * width + (g + 1) * GROUP] for part in range(3))
            weights = soft_down(dot_t(k, spread_heads(q, mask)), 49).astype(BF)
            soft[i, g] = weights
            mixed[rows, g * GROUP : (g + 1) * GROUP] = fold_heads(t_dot(weights, v), mask, SLOT).astype(BF)


def channel_forward(packed, mixed, soft, images):
    width = mixed.shape[1]

    @pl.loop(0, images, unroll=8)
    def _(i):
        rows = pl.ds(pl.multiple_of(i * SLOT, SLOT), SLOT)
        mask = head_mask(HEAD, 128 // HEAD, 128)
        for g in range(width // 128):
            q, k, v = (packed[rows, part * width + g * 128 : part * width + (g + 1) * 128] for part in range(3))
            weights = soft_down(fold_heads(t_dot(k, q), mask, HEAD), HEAD).astype(BF)
            soft[i, g // 2, g % 2 * HEAD : (g % 2 + 1) * HEAD, 0:128] = weights
            mixed[rows, g * 128 : (g + 1) * 128] = dot(v, spread_heads(weights, mask)).astype(BF)


def spatial_backward(packed, made, grad_mixed, soft, start, stop):
    width = grad_mixed.shape[1]

    @pl.loop(start, stop, unroll=stop - start)
    def _(i):
        rows = pl.ds(pl.multiple_of(i * SLOT, SLOT), SLOT)
        mask = head_mask(SLOT, GROUP // HEAD, GROUP)
        for g in range(width // GROUP):
            at = [slice(part * width + g * GROUP, part * width + (g + 1) * GROUP) for part in range(3)]
            q, k, v = (packed[rows, a] for a in at)
            weights = soft[i, g]
            out_spread = spread_heads(grad_mixed[rows, g * GROUP : (g + 1) * GROUP], mask)
            w = weights.astype(F32)
            dw = dot_t(v, out_spread)
            ds = (w * (dw - jnp.sum(dw * w, axis=0, keepdims=True))).astype(BF)
            made[rows, at[2]] = dot(weights, out_spread).astype(BF)
            made[rows, at[1]] = dot(ds, spread_heads(q, mask)).astype(BF)
            made[rows, at[0]] = (fold_heads(t_dot(ds, k), mask, SLOT) * HEAD ** -0.5).astype(BF)


def channel_backward(packed, made, grad_mixed, soft, start, stop):
    width = grad_mixed.shape[1]

    @pl.loop(start, stop, unroll=stop - start)
    def _(i):
        rows = pl.ds(pl.multiple_of(i * SLOT, SLOT), SLOT)
        mask = head_mask(HEAD, 128 // HEAD, 128)
        for g in range(width // 128):
            at = [slice(part * width + g * 128, part * width + (g + 1) * 128) for part in range(3)]
            q, k, v = (packed[rows, a] for a in at)
            weights = soft[i, g // 2, g % 2 * HEAD : (g % 2 + 1) * HEAD, 0:128]
            do = grad_mixed[rows, g * 128 : (g + 1) * 128]
            w = weights.astype(F32)
            dw = fold_heads(t_dot(v, do), mask, HEAD)
            ds = spread_heads((w * (dw - jnp.sum(dw * w, axis=0, keepdims=True))).astype(BF), mask)
            made[rows, at[2]] = dot_t(do, spread_heads(weights, mask)).astype(BF)
            made[rows, at[1]] = dot_t(q, ds).astype(BF)
            made[rows, at[0]] = (dot(k, ds) * HEAD ** -0.5).astype(BF)


def encode(pad, kernel, bias, out, images):
    @pl.loop(0, pad.shape[1] // 128)
    def _(lane):
        ls = cols(lane, 128)
        taps = [jnp.broadcast_to(kernel(t, ls), (images, 128)) for t in range(9)]
        shift = jnp.broadcast_to(bias(ls), (images, 128))

        @pl.loop(0, 7, unroll=7)
        def _(r):
            for c in range(7):
                total = shift
                for t in range(9):
                    at = pl.multiple_of(((r + t // 3) * 9 + c + t % 3) * images, 8)
                    piece = pad[pl.ds(at, images), ls]
                    total = total + piece * taps[t]
                    if t == 4:
                        total = total + piece
                out[pl.ds(pl.multiple_of((r * 7 + c) * images, 8), images), ls] = total


def normalise(stream, gain, bias, out):
    @pl.loop(0, stream.shape[0] // 16, unroll=stream.shape[0] // 16)
    def _(p):
        rows = pl.ds(pl.multiple_of(p * 16, 16), 16)
        s = stream[rows, :]
        centered = s - jnp.mean(s, axis=-1, keepdims=True)
        spread = jnp.mean(centered * centered, axis=-1, keepdims=True)
        out[rows, :] = (centered * lax.rsqrt(spread + 1e-5) * gain + bias).astype(BF)


def encode_back(gpad, given, kernel, out, put, first_row, bias_row, images):
    @pl.loop(0, gpad.shape[1] // 128)
    def _(lane):
        ls = cols(lane, 128)
        taps = [jnp.broadcast_to(kernel(8 - t, ls), (images, 128)) for t in range(9)]

        def row(r, totals):
            totals = list(totals)
            for c in range(7):
                at = pl.ds(pl.multiple_of((r * 7 + c) * images, 8), images)
                source = given[at, ls]
                total = None
                for t in range(9):
                    near = pl.ds(pl.multiple_of(((r + t // 3) * 9 + c + t % 3) * images, 8), images)
                    piece = gpad[near, ls]
                    if t == 4:
                        totals[9] = totals[9] + piece
                        total = total + piece
                    total = piece * taps[t] if total is None else total + piece * taps[t]
                    totals[8 - t] = totals[8 - t] + source * piece
                out[at, ls] = total
            return tuple(totals)
        totals = lax.fori_loop(0, 7, row, (jnp.zeros((images, 128), F32),) * 10, unroll=True)
        for t in range(9):
            put(first_row + t, lane, jnp.sum(totals[t], axis=0, keepdims=True))
        put(bias_row, lane, jnp.sum(totals[9], axis=0, keepdims=True))


def normalise_back(stream, grad, base, gain, gpad, put, gain_row, shift_row, acc, images):
    acc[...] = jnp.zeros_like(acc)

    @pl.loop(0, 49, unroll=7)
    def _(p):
        rows = pl.ds(pl.multiple_of(p * images, 8), images)
        s, dy = stream[rows, :], grad[rows, :]
        centered = s - jnp.mean(s, axis=-1, keepdims=True)
        rate = lax.rsqrt(jnp.mean(centered * centered, axis=-1, keepdims=True) + 1e-5)
        unit = centered * rate
        acc[0] += dy * unit
        acc[1] += dy
        dg = dy * gain
        m1 = jnp.mean(dg, axis=-1, keepdims=True)
        m2 = jnp.mean(dg * unit, axis=-1, keepdims=True)
        at = ((lax.div(p, 7) + 1) * 9 + lax.rem(p, 7) + 1) * images
        gpad[pl.ds(pl.multiple_of(at, 8), images), :] = base[rows, :] + rate * (dg - m1 - unit * m2)
    for row, total in ((gain_row, acc[0]), (shift_row, acc[1])):
        total = jnp.sum(total, axis=0, keepdims=True)
        for lane in range(total.shape[1] // 128):
            put(row, lane, total[:, lane * 128 : (lane + 1) * 128])


def fill_pad(pad, source, images):
    @pl.loop(0, 7)
    def _(r):
        inner = pl.ds(pl.multiple_of(((r + 1) * 9 + 1) * images, 8), 7 * images)
        pad[inner, :] = source[pl.ds(pl.multiple_of(r * 7 * images, 8), 7 * images), :]


CONV, CONV_BIAS, GAIN, SHIFT, B_PROJ, B_FC1, B_FC2 = 0, 18, 20, 22, 24, 25, 29
HIDDEN, COT, N2, PRE, MIXED, ATT, N1, PACKED = 0, 4, 5, 6, 10, 11, 12, 13
SEGMENTS = 12


def section_kernel(images, dims, shapes, rows, lags, chunk,
                   halves, conv_w, conv_b, gain, shift, b_proj, b_fc1, b_fc2, w_qkv, w_proj, w_fc1, w_fc2,
                   ends, out, small_out, acts, k_one, k_mid, k_two, k_packed, k_soft, k_slope, x_qkv, x_proj, x_fc1, x_fc2,
                   v_qkv, v_proj, v_fc1, v_fc2, params, xb, cot, pad, one, stream, gmid, gn, packed, soft, slope, hidden,
                   swap, gm_s, n1, n2, mixed, gatt, acc, small_grad, small_pair,
                   grad, land, pair_out, pair_in, small_land, left_buf, right_buf,
                   load, store, push_send, push_recv, fetch_sem, pair_send, pair_recv, send, recv, local, ssend, srecv, slocal,
                   bring_send, bring_recv):
    pipe, dp = lax.axis_index("pipe"), lax.axis_index("dp")
    other = 1 - pipe
    first = pipe == 0
    tokens, width = gn.shape
    wide = v_fc1.shape[1]
    real = 49 * images
    per = SIDE // (2 * chunk)
    block_pairs = SEGMENTS * per
    pairs = 2 * block_pairs
    weights = ((w_qkv, x_qkv, v_qkv), (w_proj, x_proj, v_proj), (w_fc1, x_fc1, v_fc1), (w_fc2, x_fc2, v_fc2))
    QKV, PROJ, FC1, FC2 = range(4)

    def to_core(at, src, dst):
        return pltpu.make_async_remote_copy(src_ref=src, dst_ref=dst, send_sem=push_send.at[at], recv_sem=push_recv.at[at],
                                            device_id={"pipe": other}, device_id_type=MESH)
    push_params = to_core(0, params.at[pipe], params.at[pipe])
    push_x = to_core(1, halves.at[1], xb.at[0])
    push_cot = to_core(1, halves.at[0], cot)
    push_weights = [to_core(2 + at, own, far) for at, (own, far, _) in enumerate(weights)]
    push_result = to_core(6, gn, ends.at[0])
    push_grad = to_core(6, gmid, ends.at[1])

    def load_weight(b, at, fresh):
        own, far, near = weights[at]

        @pl.when(b == pipe)
        def _():
            pltpu.make_async_copy(own, near, load.at[at]).start()

        @pl.when(b != pipe)
        def _():
            if fresh:
                push_weights[at].wait_recv()
            pltpu.make_async_copy(far, near, load.at[at]).start()

    def wait_weight(at):
        own, _, near = weights[at]
        pltpu.make_async_copy(own, near, load.at[at]).wait()

    def keep(at, src, dst):
        return pltpu.make_async_copy(src, dst, store.at[at])

    def block_stores(b):
        return [keep(0, one, k_one.at[b]), keep(1, gmid, k_mid.at[b]), keep(2, stream, k_two.at[b]), keep(3, packed, k_packed.at[b]),
                keep(4, soft, k_soft.at[b]), keep(5, slope, k_slope.at[b]), keep(6, n1, acts.at[b, N1]), keep(7, mixed, acts.at[b, MIXED]),
                keep(8, n2, acts.at[b, N2])] + [
                    keep(9 + s, hidden.at[pl.ds(0, tokens), pl.ds(s * SIDE, SIDE)], acts.at[b, HIDDEN + s]) for s in range(wide // SIDE)]

    def row_of(b, row):
        return params[b, row : row + 1, :]

    def taps_of(b, j):
        return (lambda t, ls: params[b, pl.ds(CONV + 9 * j + t, 1), ls]), (lambda ls: params[b, pl.ds(CONV_BIAS + j, 1), ls])

    def block_of(k):
        return jnp.where(k < block_pairs, 1, 0)

    def within(k):
        return k - jnp.where(k < block_pairs, 0, block_pairs)

    def parts_of(k):
        return (k, 0) if per == 1 else (lax.div(k, per), lax.rem(k, per))

    def number_of(k, core):
        return 2 * within(k) + core

    def out_at(k):
        return jnp.where(block_of(k) == pipe, number_of(k, pipe), 2 * block_pairs + within(k))

    main = Ring(dp, dims, shapes[0], grad, land, out, out_at, send, recv, local)
    small = Ring(dp, dims, shapes[1], small_pair, small_land, small_out, lambda c: 0, ssend, srecv, slocal)

    def slots_of(k):
        at, part = parts_of(within(k))
        left = jnp.where(at < 4, HIDDEN + at, jnp.where(at < 8, N2, jnp.where(at < 9, MIXED, N1)))
        right = jnp.where(at < 4, COT, jnp.where(at < 8, PRE + at - 4, jnp.where(at < 9, ATT, PACKED + at - 9)))
        return left, right, part

    def fetches(k):
        left, right, part = slots_of(k)
        slot, b = lax.rem(k, 2), block_of(k)
        return (pltpu.make_async_copy(acts.at[b, left], left_buf.at[slot], fetch_sem.at[slot, 0]),
                pltpu.make_async_copy(acts.at[b, right, :, cols(part, 2 * chunk)], right_buf.at[slot], fetch_sem.at[slot, 1]))

    def pair_copy(k):
        return pltpu.make_async_remote_copy(
            src_ref=pair_out.at[lax.rem(k, pair_out.shape[0])], dst_ref=pair_in.at[lax.rem(k, pair_in.shape[0])],
            send_sem=pair_send.at[k], recv_sem=pair_recv.at[k], device_id={"pipe": other}, device_id_type=MESH)

    def make(k):
        for copy in fetches(k):
            copy.wait()

        @pl.when(k >= pair_out.shape[0])
        def _():
            pair_copy(k - pair_out.shape[0]).wait_send()

        @pl.when(k >= main.grads)
        def _():
            main.reduce_ends(k - main.grads)
        slot, place, far = lax.rem(k, 2), lax.rem(k, main.grads), lax.rem(k, pair_out.shape[0])
        both = t_dot(left_buf[slot], right_buf[slot]).astype(BF)

        @pl.when(first)
        def _():
            grad[place, 0:SIDE] = both[:, :chunk]
            pair_out[far] = both[:, chunk:]

        @pl.when(jnp.logical_not(first))
        def _():
            pair_out[far] = both[:, :chunk]
            grad[place, 0:SIDE] = both[:, chunk:]
        pair_copy(k).start()
        if rows > SIDE:
            grad[place, SIDE:rows] = jnp.zeros((rows - SIDE, chunk), BF)

    def join(k):
        pair_copy(k).wait_recv()
        place = lax.rem(k, main.grads)
        grad[place, 0:SIDE] = grad[place, 0:SIDE] + pair_in[lax.rem(k, pair_in.shape[0])]

    def bring(k):
        number = number_of(k, pipe)
        at = within(k)
        return pltpu.make_async_remote_copy(
            src_ref=out.at[out_at(k)], dst_ref=out.at[number], send_sem=bring_send.at[at], recv_sem=bring_recv.at[at],
            device_id={"pipe": other}, device_id_type=MESH)

    def hand_over(k):
        @pl.when(block_of(k) != pipe)
        def _():
            bring(k).start()

    def leave(k):
        main.gather_ends(k)

        @pl.when(block_of(k) != pipe)
        def _():
            bring(k).wait_send()

        @pl.when(block_of(k) == pipe)
        def _():
            arrival = pltpu.make_async_remote_copy(
                src_ref=out.at[number_of(k, other)], dst_ref=out.at[number_of(k, other)], send_sem=bring_send.at[within(k)],
                recv_sem=bring_recv.at[within(k)], device_id={"pipe": other}, device_id_type=MESH)
            arrival.wait_recv()
    small_copy = to_core(7, small_grad.at[other], small_pair.at[1])

    def small_make(k):
        small_copy.start()
        small_pair[0] = small_grad[pipe]

    def small_join(k):
        small_copy.wait_recv()
        small_pair[0] = small_pair[0] + small_pair[1]

    def tick(t, low, high):
        stages = main.stages(make, join, hand_over)
        small_stages = small.stages(small_make, small_join, lambda k: None)
        for s in reversed(range(low, high)):
            k = t - lags[s]

            @pl.when((k >= 0) & (k < pairs))
            def _():
                stages[s](k)

            @pl.when(k == pairs)
            def _():
                small_stages[s](0)

    main.greet()
    for j in range(2):
        for t in range(9):
            params[pipe, CONV + 9 * j + t : CONV + 9 * j + t + 1, :] = conv_w[t, j : j + 1, :]
    for row, ref in ((CONV_BIAS, conv_b), (GAIN, gain), (SHIFT, shift), (B_PROJ, b_proj), (B_FC2, b_fc2)):
        params[pipe, row : row + ref.shape[0], :] = ref[...]
    for j in range(wide // width):
        params[pipe, B_FC1 + j : B_FC1 + j + 1, :] = b_fc1[:, j * width : (j + 1) * width]
    x_copy = pltpu.make_async_copy(halves.at[0], xb.at[0], load.at[5])
    cot_copy = pltpu.make_async_copy(halves.at[1], cot, load.at[5])
    push_params.start()

    @pl.when(first)
    def _():
        push_x.start()
        x_copy.start()

    @pl.when(jnp.logical_not(first))
    def _():
        push_cot.start()
        cot_copy.start()
    for copy in push_weights:
        copy.start()
    fill_swap(swap, images)
    clear_border(pad, images)
    small_grad[...] = jnp.zeros_like(small_grad)
    one[real:tokens, :] = jnp.zeros((tokens - real, width), F32)
    stream[real:tokens, :] = jnp.zeros((tokens - real, width), F32)
    push_params.wait_recv()

    @pl.when(first)
    def _():
        x_copy.wait()

    @pl.when(jnp.logical_not(first))
    def _():
        push_x.wait_recv()

    @pl.loop(0, 2)
    def _(b):
        stores = block_stores(b)

        @pl.when(b > 0)
        def _():
            for copy in stores:
                copy.wait()
        load_weight(b, QKV, True)
        gn[...] = xb[b].astype(F32)
        fill_pad(pad, gn, images)
        kernel, bias = taps_of(b, 0)
        encode(pad, kernel, bias, one, images)
        stores[0].start()
        normalise(one, row_of(b, GAIN), row_of(b, SHIFT), n1)
        stores[6].start()


        gm_s[...] = dot(swap[...], n1[...]).astype(BF)
        wait_weight(QKV)

        @pl.loop(0, 3)
        def _(j):
            scale = jnp.where(j == 0, HEAD ** -0.5, 1.0)
            packed[:, cols(j, width)] = (dot(gm_s[...], v_qkv[:, cols(j, width)]) * scale).astype(BF)
        stores[3].start()
        load_weight(b, PROJ, True)

        @pl.when(b == 0)
        def _():
            spatial_forward(packed, gm_s, soft, images)

        @pl.when(b == 1)
        def _():
            channel_forward(packed, gm_s, soft, images)
        stores[4].start()
        load_weight(b, FC1, True)

        mixed[...] = t_dot(swap[...], gm_s[...]).astype(BF)
        stores[7].start()
        wait_weight(PROJ)

        gmid[...] = one[...] + dot(mixed[...], v_proj[...]) + row_of(b, B_PROJ)
        stores[1].start()
        fill_pad(pad, gmid, images)
        kernel, bias = taps_of(b, 1)
        encode(pad, kernel, bias, stream, images)
        stores[2].start()
        normalise(stream, row_of(b, GAIN + 1), row_of(b, SHIFT + 1), n2)
        stores[8].start()
        wait_weight(FC1)
        load_weight(b, FC2, True)

        @pl.loop(0, wide // width, unroll=2)
        def _(j):
            at = cols(j, width)
            value, rate = gelu_both(dot(n2[...], v_fc1[:, at]) + params[b, pl.ds(B_FC1 + j, 1), :])
            hidden[0:tokens, at] = value.astype(BF)
            slope[:, at] = rate.astype(BF)
        stores[5].start()
        for copy in stores[9:]:
            copy.start()
        wait_weight(FC2)

        gn[...] = stream[...] + dot(hidden[0:tokens, :], v_fc2[...]) + row_of(b, B_FC2)

        @pl.when(b == 0)
        def _():
            xb[1] = gn[...].astype(BF)

    end_copy = pltpu.make_async_copy(gn, ends.at[1], load.at[6])
    last_copy = pltpu.make_async_copy(gmid, ends.at[0], load.at[6])

    @pl.when(first)
    def _():
        push_result.start()
        push_cot.wait_recv()

    @pl.when(jnp.logical_not(first))
    def _():
        end_copy.start()
        cot_copy.wait()
    keep_cot = keep(13, cot, acts.at[1, COT])
    keep_cot.start()
    for copy in block_stores(1):
        copy.wait()
    keep_cot.wait()
    for copy in fetches(0):
        copy.start()

    def put(b):
        def at(row, lane, value):
            small_grad[b, pl.ds(lane * 32 + row, 1), :] = value
        return at

    loads = [pltpu.make_async_copy(k_slope.at[0], slope, load.at[7]), pltpu.make_async_copy(k_packed.at[0], packed, load.at[8]),
             pltpu.make_async_copy(k_soft.at[0], soft, load.at[9]), pltpu.make_async_copy(k_two.at[0], stream, load.at[10]),
             pltpu.make_async_copy(k_mid.at[0], gmid, load.at[11])]

    def later(b, at):
        @pl.when(b == 0)
        def _():
            loads[at].wait()

    def later_weight(b, at):
        @pl.when(b == 0)
        def _():
            wait_weight(at)

    def ahead(b, do):
        pl.when(b == 1)(do)

    def pre_part(part):
        def run(b):
            if part == 0:
                later(b, 0)
                later_weight(b, FC2)
                one[...] = cot[...].astype(F32)
            each = wide // 3
            at = slice(part * each, (part + 1) * each)
            pre = dot_t(cot[...], v_fc2[at, :]) * slope[:, at].astype(F32)
            slope[:, at] = pre.astype(BF)
            total = jnp.sum(pre, axis=0, keepdims=True)
            for piece in range(each // 128):
                lane = part * each // 128 + piece
                put(b)(B_FC1 + lane // (width // 128), lane % (width // 128), total[:, piece * 128 : (piece + 1) * 128])
            if part == 2:
                ahead(b, lambda: load_weight(0, FC2, False))
                copies = [keep(s, slope.at[:, pl.ds(s * SIDE, SIDE)], acts.at[b, PRE + s]) for s in range(wide // SIDE)]
                for copy in copies:
                    copy.start()
                for lane in range(width // 128):
                    put(b)(B_FC2, lane, jnp.sum(one[:, lane * 128 : (lane + 1) * 128], axis=0, keepdims=True))
                for copy in copies:
                    copy.wait()
        return run

    def through_fc1(b):
        @pl.when(b == 1)
        def _():
            @pl.when(first)
            def _():
                push_result.wait_send()

            @pl.when(jnp.logical_not(first))
            def _():
                end_copy.wait()
        later_weight(b, FC1)

        gn[...] = dot_t(slope[...], v_fc1[...])
        ahead(b, lambda: load_weight(0, FC1, False))

    def through_second(b):
        later(b, 3)
        normalise_back(stream, gn, one, row_of(b, GAIN + 1), pad, put(b), GAIN + 1, SHIFT + 1, acc, images)
        pltpu.make_async_copy(k_one.at[b], stream, load.at[12]).start()
        later(b, 4)
        encode_back(pad, gmid, taps_of(b, 1)[0], gmid, put(b), CONV + 9, CONV_BIAS + 1, images)
        gmid[real:tokens, :] = jnp.zeros((tokens - real, width), F32)
        for lane in range(width // 128):
            part = gmid[:, lane * 128 : (lane + 1) * 128]
            put(b)(B_PROJ, lane, jnp.sum(part, axis=0, keepdims=True))
            gatt[:, lane * 128 : (lane + 1) * 128] = part.astype(BF)
        keep(4, gatt, acts.at[b, ATT]).start()

    def through_proj(b):
        later_weight(b, PROJ)

        n2[...] = dot_t(gatt[...], v_proj[...]).astype(BF)
        ahead(b, lambda: load_weight(0, PROJ, False))
        gm_s[...] = dot(swap[...], n2[...]).astype(BF)
        later(b, 1)
        later(b, 2)

    def through_mix(part):
        def run(b):
            each = images // 2

            @pl.when(b == 0)
            def _():
                spatial_backward(packed, hidden, gm_s, soft, part * each, (part + 1) * each)

            @pl.when(b == 1)
            def _():
                channel_backward(packed, hidden, gm_s, soft, part * each, (part + 1) * each)
            if part == 1:
                keep(4, gatt, acts.at[b, ATT]).wait()
        return run

    def unswap(b):
        @pl.loop(0, 3)
        def _(j):
            slope[:, cols(j, width)] = t_dot(swap[...], hidden[:, cols(j, width)]).astype(BF)
        copies = [keep(s, slope.at[:, pl.ds(s * SIDE, SIDE)], acts.at[b, PACKED + s]) for s in range(3)]
        for copy in copies:
            copy.start()
        for copy in copies:
            copy.wait()

    def through_qkv(b):
        later_weight(b, QKV)

        gn[...] = dot_t(slope[:, 0 : 3 * width], v_qkv[...])

        def prepare():
            load_weight(0, QKV, False)
            for at in range(3):
                loads[at].start()
        ahead(b, prepare)

    def through_first(b):
        pltpu.make_async_copy(k_one.at[b], stream, load.at[12]).wait()
        normalise_back(stream, gn, gmid, row_of(b, GAIN), pad, put(b), GAIN, SHIFT, acc, images)
        ahead(b, lambda: loads[3].start())

    def finish(b):
        gn[...] = xb[b].astype(F32)
        encode_back(pad, gn, taps_of(b, 0)[0], gmid, put(b), CONV, CONV_BIAS, images)

        @pl.when(b == 1)
        def _():
            cot[...] = gmid[...].astype(BF)
            copy = keep(5, cot, acts.at[0, COT])
            copy.start()
            loads[4].start()
            copy.wait()

        @pl.when((b == 0) & first)
        def _():
            last_copy.start()

        @pl.when((b == 0) & jnp.logical_not(first))
        def _():
            push_grad.start()
    segments = [pre_part(0), pre_part(1), pre_part(2), through_fc1, through_second, through_proj, through_mix(0), through_mix(1),
                unswap, through_qkv, through_first, finish]

    late = len(lags) * 2 // 3

    @pl.loop(0, pairs + 1 + lags[-1])
    def _(t):
        tick(t, late, len(lags))
        gone = t - lags[-1] - 1

        @pl.when((gone >= 0) & (gone < pairs))
        def _():
            leave(gone)
        at, part = parts_of(within(t))

        @pl.when((t < pairs) & (part == 0))
        def _():
            b = block_of(t)
            for number, segment in enumerate(segments):
                @pl.when(at == number)
                def _():
                    segment(b)
        tick(t, 0, late)

        @pl.when(t + 1 < pairs)
        def _():
            for copy in fetches(t + 1):
                copy.start()

    @pl.loop(pairs - main.grads, pairs)
    def _(k):
        main.reduce_ends(k)

    @pl.loop(pairs - pair_out.shape[0], pairs)
    def _(k):
        pair_copy(k).wait_send()

    small.reduce_ends(0)
    small.gather_ends(0)
    small_copy.wait_send()
    push_params.wait_send()
    for copy in push_weights:
        copy.wait_send()

    @pl.when(first)
    def _():
        push_x.wait_send()
        last_copy.wait()
        push_grad.wait_recv()

    @pl.when(jnp.logical_not(first))
    def _():
        push_cot.wait_send()
        push_grad.wait_send()
        push_result.wait_recv()


def section(halves, small, weights, images, n, collective_id=0):
    w_qkv, w_proj, w_fc1, w_fc2 = weights
    _, tokens, width = halves.shape
    wide = w_fc1.shape[1]
    slots = images * SLOT
    dims = dp_dims(n)
    chunk = 384 if n <= 16 else 128
    total = (wide // SIDE * 2 + 4) * SIDE // chunk
    pairs = total
    rows = -(-SIDE // (16 * n)) * 16 * n
    small_rows = 16 * n
    shapes = (Shape(rows, dims), Shape(small_rows, dims))
    events = shapes[0].events
    hops = sum(0 if s == 1 else 1 if s == 2 else 3 for s in dims[0])
    gaps = [1, 2] + [1] * (2 * hops - 2) + [3]
    lags = [sum(gaps[:s]) for s in range(2 * hops + 2)]
    grads = 8 if lags[hops + 1] < 8 else 16
    lands = 8 if 2 * gaps[1] + 3 <= 8 else 16
    any_space = pl.BlockSpec(memory_space=pl.ANY)
    vmem = pl.BlockSpec(memory_space=pltpu.VMEM)
    soft = (images, width // GROUP, SLOT, 2 * GROUP)
    outs = [((2, tokens, width), F32), ((total + total // 2, rows, chunk), BF), ((1, small_rows, 128), F32),
            ((2, 16, tokens, SIDE), BF), ((2, tokens, width), F32), ((2, tokens, width), F32), ((2, tokens, width), F32),
            ((2, slots, 3 * width), BF), ((2, *soft), BF), ((2, tokens, wide), BF),
            (w_qkv.shape, BF), (w_proj.shape, BF), (w_fc1.shape, BF), (w_fc2.shape, BF)]
    dma = pltpu.SemaphoreType.DMA

    def plain(shape):
        return pltpu.VMEM(shape, F32)

    def low(shape):
        return pltpu.VMEM(shape, BF)
    results = pl.pallas_call(
        functools.partial(section_kernel, images, dims, shapes, rows, lags, chunk),
        out_shape=[jax.ShapeDtypeStruct(*o) for o in outs],
        in_specs=[any_space] + [vmem] * 7 + [any_space] * 4,
        out_specs=[any_space] * len(outs),
        scratch_shapes=[low(w.shape) for w in weights] + [
            plain((2, 32, width)), low((2, tokens, width)), low((tokens, width)), plain((81 * images, width)),
            plain((tokens, width)), plain((tokens, width)), plain((tokens, width)), plain((tokens, width)),
            low((slots, 3 * width)), low(soft), low((tokens, wide)), low((slots, wide)),
            low((slots, tokens)), low((slots, width)), low((tokens, width)), low((tokens, width)), low((tokens, width)), low((tokens, width)),
            plain((2, images, width)), plain((2, small_rows, 128)), plain((2, small_rows, 128)),
            low((grads, rows, chunk)), low((lands, shapes[0].land, chunk)), low((4, SIDE, chunk)), low((8, SIDE, chunk)), plain((1, shapes[1].land, 128)),
            low((2, tokens, SIDE)), low((2, tokens, 2 * chunk)),
            dma((13,)), dma((14,)), dma((8,)), dma((8,)), dma((2, 2)), dma((pairs,)), dma((pairs,)),
            dma((pairs, events)), dma((pairs, events)), dma, dma((1, events)), dma((1, events)), dma, dma((pairs // 2,)), dma((pairs // 2,)),
        ],
        compiler_params=pltpu.CompilerParams(collective_id=collective_id, has_side_effects=True, vmem_limit_bytes=63 * 2**20),
    )(halves, *small, w_qkv, w_proj, w_fc1, w_fc2)
    return results[:3]


def finish_kernel(images, chunk, done, sums, ends, fc2, fc1, proj, qkv, conv_w, conv_b, gain, shift, b_proj, b_fc1, b_fc2, section,
                  low_buf, wide_buf, end_buf, section_buf, read, write, end_sem):
    depth = low_buf.shape[0]
    jobs, start = [], 0
    for dst in (fc2, fc1, proj, qkv):
        across = dst.shape[2] // chunk
        number = dst.shape[1] // SIDE * across
        jobs.append((start, number, across, dst))
        start += number
    end_copy = pltpu.make_async_copy(ends, end_buf, end_sem.at[0])
    end_copy.start()

    def get(c):
        return pltpu.make_async_copy(done.at[c, pl.ds(0, SIDE)], low_buf.at[lax.rem(c, depth)], read.at[lax.rem(c, depth)])

    def give(c, dst, across, at):
        rows = pl.ds(pl.multiple_of(lax.div(at, across) * SIDE, SIDE), SIDE)
        return pltpu.make_async_copy(wide_buf.at[lax.rem(c, depth)], dst.at[0, rows, cols(lax.rem(at, across), chunk)],
                                     write.at[lax.rem(c, depth)])

    @pl.loop(0, depth)
    def _(c):
        get(c).start()
    for begin, number, across, dst in jobs:
        @pl.loop(0, number)
        def _(at):
            c = begin + at
            slot = lax.rem(c, depth)
            get(c).wait()

            @pl.when(c >= depth)
            def _():
                give(c, dst, across, at).wait()
            for r in range(0, SIDE, 128):
                wide_buf[slot, r : r + 128] = low_buf[slot, r : r + 128].astype(F32)
            give(c, dst, across, at).start()

            @pl.when(c + depth < start)
            def _():
                get(c + depth).start()
        if begin == 0:
            end_copy.wait()
            for half in range(2):
                section_buf[:, half * images : (half + 1) * images, :] = end_buf[half, 0:49]
            section_copy = pltpu.make_async_copy(section_buf, section.at[0], end_sem.at[1])
            section_copy.start()
    lanes = fc2.shape[2] // 128
    width = fc2.shape[2]

    def take(first_row, ref, index, rows):
        for lane in range(lanes):
            ref[index + (slice(lane * 128, (lane + 1) * 128),)] = sums[0, lane * 32 + first_row : lane * 32 + first_row + rows, :]
    for j in range(2):
        for t in range(9):
            take(CONV + 9 * j + t, conv_w, (0, t, slice(j, j + 1)), 1)
    take(CONV_BIAS, conv_b, (0, slice(0, 2)), 2)
    take(GAIN, gain, (0, slice(0, 2)), 2)
    take(SHIFT, shift, (0, slice(0, 2)), 2)
    take(B_PROJ, b_proj, (slice(0, 1),), 1)
    take(B_FC2, b_fc2, (slice(0, 1),), 1)
    for lane in range(b_fc1.shape[1] // 128):
        at = lane % lanes * 32 + B_FC1 + lane // lanes
        b_fc1[0:1, lane * 128 : (lane + 1) * 128] = sums[0, at : at + 1, :]
    @pl.loop(start - depth, start)
    def _(c):
        give(c, fc2, 1, 0).wait()
    section_copy.wait()


def finish(done, sums, ends, shapes, images):
    any_space = pl.BlockSpec(memory_space=pl.ANY)
    vmem = pl.BlockSpec(memory_space=pltpu.VMEM)
    chunk, depth = done.shape[2], 6
    return pl.pallas_call(
        functools.partial(finish_kernel, images, chunk),
        out_shape=[jax.ShapeDtypeStruct(s, F32) for s in shapes],
        in_specs=[any_space, vmem, any_space],
        out_specs=[any_space] * 4 + [vmem] * 7 + [any_space],
        scratch_shapes=[pltpu.VMEM((depth, SIDE, chunk), BF), pltpu.VMEM((depth, SIDE, chunk), F32), pltpu.VMEM(ends.shape, F32),
                        pltpu.VMEM(shapes[-1][1:], F32),
                        pltpu.SemaphoreType.DMA((depth,)), pltpu.SemaphoreType.DMA((depth,)), pltpu.SemaphoreType.DMA((2,))],
        compiler_params=pltpu.CompilerParams(vmem_limit_bytes=62 * 2**20),
    )(done, sums, ends)


def on_device(section_inputs, conv_weight, conv_bias, norm_gain, norm_bias, w_qkv, w_proj, b_proj, w_fc1, b_fc1, w_fc2, b_fc2):
    n = lax.axis_size("dp")
    images, positions, width = section_inputs.shape[1:]
    half = images // 2
    spare = -(-positions * half // 16) * 16 // half - positions
    halves = jnp.pad(section_inputs.reshape(2, half, positions, width), ((0, 0), (0, 0), (0, spare), (0, 0)))
    halves = jnp.swapaxes(halves, 1, 2).reshape(2, -1, width)
    small = (jnp.swapaxes(conv_weight[0], 0, 1), conv_bias[0], norm_gain[0], norm_bias[0], b_proj, b_fc1, b_fc2)
    ends, done, sums = section(halves, small, (w_qkv[0], w_proj[0], w_fc1[0], w_fc2[0]), half, n)
    ends = ends.reshape(2, -1, half, width)
    arrays = (w_fc2, w_fc1, w_proj, w_qkv, jnp.swapaxes(conv_weight, 1, 2), conv_bias, norm_gain, norm_bias, b_proj, b_fc1, b_fc2,
              jnp.swapaxes(section_inputs, 1, 2))
    fc2, fc1, proj, qkv, conv_w, conv_b, gain, shift, g_proj, g_fc1, g_fc2, section_ends = finish(done, sums, ends, [a.shape for a in arrays], half)
    return (jnp.swapaxes(section_ends, 1, 2), jnp.swapaxes(conv_w, 1, 2), conv_b, gain, shift, qkv, proj, g_proj, fc1, g_fc1, fc2, g_fc2)


def solution(mesh):
    return jax.shard_map(
        on_device,
        mesh=mesh,
        in_specs=(
            P("pipe", "dp", None, None),
            P("pipe", None, None, None),
            P("pipe", None, None),
            P("pipe", None, None),
            P("pipe", None, None),
            P("pipe", None, None),
            P("pipe", None, None),
            P("pipe", None),
            P("pipe", None, None),
            P("pipe", None),
            P("pipe", None, None),
            P("pipe", None),
        ),
        out_specs=(
            P("pipe", "dp", None, None),
            P("pipe", None, None, None),
            P("pipe", None, None),
            P("pipe", None, None),
            P("pipe", None, None),
            P("pipe", None, None),
            P("pipe", None, None),
            P("pipe", None),
            P("pipe", None, None),
            P("pipe", None),
            P("pipe", None, None),
            P("pipe", None),
        ),
        check_vma=False,
    )
```
